256 devices in a mesh: dp: 8 (over y, core), label: 32 (over z, x).
Axes of the slice: x: 4, y: 4, z: 8, core: 2. Of those that a mesh axis runs over, the one named last changes fastest.
Arguments:
- embed: bfloat16 [16384, 768], P(('dp', 'label')), may hold values from -6 to 6
- cluster_weight: bfloat16 [512, 768], P('label'), may hold values from -0.21875 to 0.21875
- leaf_weight: bfloat16 [512, 32, 768], P('label'), may hold values from -0.21875 to 0.21875
- match_instance: int32 [8, 32, 32, 96], P('dp', 'label'), may hold values from 0 to 63
- match_cluster: int32 [8, 32, 32, 96], P('dp', 'label'), may hold values from 0 to 15
- match_count: int32 [8, 32, 32], P('dp', 'label'), may hold values from 24 to 96, as said below
- prefix: bfloat16 [8, 32, 32, 96], P('dp', 'label'), may hold values from 0.099609375 to 1
- targets: bfloat16 [8, 32, 32, 96, 32], P('dp', 'label'), may hold values from 0 to 1
Outputs:
- grad_embed: float32 [16384, 768], P(('dp', 'label'))
- grad_cluster: float32 [512, 768], P('label')
- grad_leaf: float32 [512, 32, 768], P('label', 'dp')
The draws below stay inside these ranges and needn't reach their ends.
Inputs may be any that keep to these rules, and one draw needn't show every extreme that they name: `match_count`: valid slots from one device to one owner; in each dp group one owner receives 96 valid slots from every device. Slots past the count hold arbitrary in-range indices.
All inputs are finite; a program needn't handle non-finite values.
Results may differ from the reference program's by a relative error of at most 0.0065.
Values may be sent and summed in bfloat16 or wider, within the bound.
No kernel may reach another device: no remote copies, remote signals or barrier semaphores. Data moves between devices by JAX's collectives and lax.ppermute only.
A program may use at most 128 MiB of HBM per device.

```python
import jax
import jax.numpy as jnp
from jax import lax

D = 768
KIDS = 32
INST_DEV = 64
CL_DEV = 16
CAP = 96
INST = 16384
CLUSTERS = 512
N_DP = 8
N_LABEL = 32


def draw_match_count(key, part):
    key = jax.random.fold_in(key, 7)
    first, second = jax.random.split(key)
    base = jax.random.randint(first, (N_DP, N_LABEL, N_LABEL), CAP // 4, 3 * CAP // 4 + 1)
    chosen = jax.random.randint(second, (N_DP, 1, 1), 0, N_LABEL)
    owner = lax.broadcasted_iota(jnp.int32, (N_DP, N_LABEL, N_LABEL), 2)
    return jnp.where(owner == chosen, CAP, base).astype(jnp.int32)


def plant(result, rng, smallest, high):
    longest = result.shape.index(max(result.shape))
    spots = []
    for shift in (0, 1):
        where = [jax.random.randint(jax.random.fold_in(rng, axis), (), 0, length) for axis, length in enumerate(result.shape)]
        where[longest] = (where[longest] + shift) % result.shape[longest]
        spots.append(tuple(where))
    return result.at[spots[0]].set(smallest).at[spots[1]].set(high)


def block_levels(key, dims, shards, smallest, top_value):
    def one(axis_at, shards_of):
        heights = jax.random.uniform(jax.random.fold_in(jax.random.fold_in(key, 6), axis_at), (shards_of,), jnp.float32, smallest / len(shards), top_value / len(shards))
        return jnp.repeat(jnp.exp(heights), dims[axis_at] // shards_of).reshape((-1,) + (1,) * (len(dims) - axis_at - 1))

    gain = one(*shards[0])
    for cut in shards[1:]:
        gain = gain * one(*cut)
    return gain


def bell_draw(stream_key, dims, spread, bound, shards=(), kind=jnp.bfloat16):
    factor_of = block_levels(stream_key, dims, shards, -0.22, 0.18) if shards else 1.0
    result = jax.random.normal(stream_key, dims, jnp.float32) * spread * factor_of
    return jnp.minimum(jnp.maximum(result, -bound), bound).astype(kind)


def setup_inputs(seed: int = 0) -> dict:
    key_list = jax.random.split(jax.random.key(seed), 9)
    embed = bell_draw(key_list[0], (INST, D), 1.0, 6.0, ((0, 256),))
    cluster_weight = bell_draw(key_list[1], (CLUSTERS, D), D ** -0.5, 0.21875, ((0, 32),))
    leaf_weight = bell_draw(key_list[2], (CLUSTERS, KIDS, D), D ** -0.5, 0.21875, ((0, 32),))
    match_instance = plant(jax.random.randint(key_list[3], (N_DP, N_LABEL, N_LABEL, CAP), 0, INST_DEV), jax.random.fold_in(key_list[3], 1), 0, INST_DEV - 1).astype(jnp.int32)
    match_cluster = plant(jax.random.randint(key_list[4], (N_DP, N_LABEL, N_LABEL, CAP), 0, CL_DEV), jax.random.fold_in(key_list[4], 1), 0, CL_DEV - 1).astype(jnp.int32)
    match_count = draw_match_count(jax.random.fold_in(key_list[8], 71), 0)
    prefix = jnp.clip(0.099609375 + 0.9003906 * jax.random.uniform(key_list[6], (N_DP, N_LABEL, N_LABEL, CAP), jnp.float32) ** block_levels(key_list[6], (N_DP, N_LABEL, N_LABEL, CAP), ((0, 8), (1, 32)), -0.2, 0.2), 0.099609375, 1.0).astype(jnp.bfloat16)
    targets = jnp.clip(1.0 * jax.random.uniform(key_list[7], (N_DP, N_LABEL, N_LABEL, CAP, KIDS), jnp.float32) ** block_levels(key_list[7], (N_DP, N_LABEL, N_LABEL, CAP, KIDS), ((0, 8), (1, 32)), -0.2, 0.2), 0.0, 1.0).astype(jnp.bfloat16)
    return dict(embed=embed, cluster_weight=cluster_weight, leaf_weight=leaf_weight, match_instance=match_instance, match_cluster=match_cluster, match_count=match_count, prefix=prefix, targets=targets)


def reference(embed, cluster_weight, leaf_weight, match_instance, match_cluster, match_count, prefix, targets):
    slot = jnp.arange(CAP, dtype=jnp.int32)
    valid = slot[None, None, None, :] < match_count[..., None]
    pre = jnp.where(valid, prefix, jnp.zeros((), prefix.dtype))
    tgt = jnp.where(valid[..., None], targets, jnp.zeros((), targets.dtype))
    group = jnp.arange(N_DP, dtype=jnp.int32)[:, None, None, None]
    source = jnp.arange(N_LABEL, dtype=jnp.int32)[None, :, None, None]
    owner = jnp.arange(N_LABEL, dtype=jnp.int32)[None, None, :, None]
    inst_global = ((group * N_LABEL + source) * INST_DEV + match_instance).astype(jnp.int32)
    clus_global = (owner * CL_DEV + match_cluster).astype(jnp.int32)
    block = CAP * 4
    steps = (N_DP * N_LABEL * N_LABEL * CAP) // block
    inst_blocks = inst_global.reshape(steps, block)
    clus_blocks = clus_global.reshape(steps, block)
    pre_blocks = pre.reshape(steps, block)
    tgt_blocks = tgt.reshape(steps, block, KIDS)

    def advance(carry, item):
        g_emb, g_clu, g_leaf = carry
        ids, cls, alpha, want = item
        rows = jnp.take(embed, ids, axis=0).astype(jnp.float32)
        upper = jnp.take(cluster_weight, cls, axis=0).astype(jnp.float32)
        lower = jnp.take(leaf_weight, cls, axis=0).astype(jnp.float32)
        z1 = jnp.sum(rows * upper, axis=1)
        z2 = jnp.einsum('rd,rkd->rk', rows, lower)
        s1 = jax.nn.sigmoid(z1)
        s2 = jax.nn.sigmoid(z2)
        a = alpha.astype(jnp.float32)
        resid = a[:, None] * s1[:, None] * s2 - want.astype(jnp.float32)
        dz2 = (resid * (a * s1)[:, None] * s2 * (1.0 - s2)).astype(jnp.bfloat16).astype(jnp.float32)
        dz1 = (jnp.sum(resid * a[:, None] * s2, axis=1) * s1 * (1.0 - s1)).astype(jnp.bfloat16).astype(jnp.float32)
        grad_rows = jnp.einsum('rk,rkd->rd', dz2, lower) + dz1[:, None] * upper
        g_emb = g_emb.at[ids].add(grad_rows)
        g_clu = g_clu.at[cls].add(dz1[:, None] * rows)
        g_leaf = g_leaf.at[cls].add(dz2[:, :, None] * rows[:, None, :])
        return (g_emb, g_clu, g_leaf), None

    start = (jnp.zeros((INST, D), jnp.float32), jnp.zeros((CLUSTERS, D), jnp.float32),
             jnp.zeros((CLUSTERS, KIDS, D), jnp.float32))
    (g_emb, g_clu, g_leaf), _ = lax.scan(advance, start, (inst_blocks, clus_blocks, pre_blocks, tgt_blocks))
    return g_emb, g_clu, g_leaf
```

```python
import functools

import jax
import jax.numpy as jnp
from jax import lax
from jax.experimental import pallas as pl
from jax.experimental.pallas import tpu as pltpu
from jax.sharding import Mesh, PartitionSpec as P

BF16 = jnp.bfloat16
F32 = jnp.float32
NY, NC, NZ, NX = 4, 2, 8, 4
HALF = 32
NT = (((1,), (1,)), ((), ()))
NN = (((1,), (0,)), ((), ()))
TN = (((0,), (0,)), ((), ()))


def dot(a, b, dims):
    return lax.dot_general(a, b, dims, preferred_element_type=F32)


def shift(x, axis, by):
    n = {"z": NZ, "x": NX, "y": NY, "core": NC}[axis]
    return lax.ppermute(x, axis, [(i, (i + by) % n) for i in range(n)])


def owner_kernel(*refs):
    (e, x1, x2, x3, a1, a2, a3, a4, a5, a6, a7, ha1, ha3, ha2a, ha2b) = refs[:15]
    (g0, g1, g2, g3, g4a, g4b, g5, g6, g7) = refs[15:24]
    slots = refs[24:32]
    w = refs[32]
    ga, gb, gw, rows, wide = refs[33:]
    own = (None, a1, a2, a3, a4, a5, a6, a7)
    whole = (g0, g1, g2, g3, None, g5, g6, g7)
    for dx, r in enumerate((e, x1, x2, x3)):
        rows[0, dx * HALF : (dx + 1) * HALF] = r[0:HALF]
    for dz in range(1, NZ):
        rows[dz, 0:HALF] = own[dz][...]
        lo = (dz - 1) * HALF
        rows[dz, HALF : 2 * HALF] = ha1[lo : lo + HALF]
        rows[dz, 3 * HALF : 4 * HALF] = ha3[lo : lo + HALF]
        for part in range(2):
            at = lo + part * 16
            src = ha2a[at : at + 16] if at < 112 else ha2b[at - 112 : at - 96]
            rows[dz, 2 * HALF + part * 16 : 2 * HALF + part * 16 + 16] = src
    for dz in range(NZ):
        if dz == 4:
            rows[dz, 128:192] = g4a[...]
            rows[dz, 192:256] = g4b[...]
        else:
            rows[dz, 128:256] = whole[dz][...]

    lane_row = lax.broadcasted_iota(jnp.int32, (256, 128), 0)
    cluster_row = lax.broadcasted_iota(jnp.int32, (16, 128), 0)
    for dz in range(NZ):
        left = []
        for dx in range(NX):
            side = slots[dz][dx].astype(F32)
            alpha = side[32:33]
            inst = side[33:34].astype(jnp.int32)
            clus = side[34:35].astype(jnp.int32)
            here = (inst // HALF) * 128 + dx * HALF + inst % HALF
            left.append(jnp.where(lane_row == here, alpha, 0.0).astype(BF16))
            member = cluster_row == clus
            for k in range(33):
                wide[k * 16 : k * 16 + 16, dx * 128 : dx * 128 + 128] = jnp.where(
                    member, side[k : k + 1], 0.0
                ).astype(BF16)
        ay = dot(wide[...], jnp.concatenate(left, axis=1), NT)
        mine = rows[dz]
        z = dot(w[...], mine, NT)
        s1 = jax.nn.sigmoid(z[512:528])
        a2 = ay[512:528]
        s1a = s1 * a2
        total = jnp.zeros((16, 256), F32)
        parts = []
        for k in range(32):
            s2 = jax.nn.sigmoid(z[k * 16 : k * 16 + 16])
            t = s2 * (s1a * s2 - ay[k * 16 : k * 16 + 16])
            total = total + t
            parts.append((s1 * (1.0 - s2) * t).astype(BF16))
        parts.append((total * s1 * (1.0 - s1)).astype(BF16))
        dz_all = jnp.concatenate(parts, axis=0)
        part = dot(dz_all, mine, NN)
        if dz == 0:
            gw[...] = part
        else:
            gw[...] += part
        ge = dot(dz_all, w[...], TN).astype(BF16)
        gb[dz] = ge[128:256]
        for dx in range(NX):
            ga[dx, dz * HALF : (dz + 1) * HALF] = ge[dx * HALF : (dx + 1) * HALF]


def owner_terms(args):
    return pl.pallas_call(
        owner_kernel,
        out_shape=(
            jax.ShapeDtypeStruct((NX, NZ * HALF, 768), BF16),
            jax.ShapeDtypeStruct((NZ, 128, 768), BF16),
            jax.ShapeDtypeStruct((528, 768), F32),
        ),
        in_specs=[pl.BlockSpec(memory_space=pltpu.VMEM)] * len(args),
        out_specs=[pl.BlockSpec(memory_space=pltpu.VMEM)] * 3,
        scratch_shapes=[pltpu.VMEM((NZ, 256, 768), BF16), pltpu.VMEM((528, 512), BF16)],
        compiler_params=pltpu.CompilerParams(vmem_limit_bytes=40 * 1024 * 1024),
    )(*args)


def add(a, b):
    return (a.astype(F32) + b.astype(F32)).astype(BF16)


def shards(e, cw, lw, inst, clus, counts, prefix, targets):
    iy, ic, iz, ix = (lax.axis_index(n) for n in ("y", "core", "z", "x"))

    with jax.named_scope("gather_rows"):
        x1, x2, x3 = shift(e, "x", 1), shift(e, "x", 2), shift(e, "x", -1)
        a0 = e[:HALF]
        a1, a7 = shift(a0, "z", 1), shift(a0, "z", -1)
        a2, a6 = shift(a1, "z", 1), shift(a7, "z", -1)
        a3, a5 = shift(a2, "z", 1), shift(a6, "z", -1)
        a4 = shift(a3, "z", 1)
        g0 = jnp.concatenate([e[HALF:], x1[HALF:], x2[HALF:], x3[HALF:]], axis=0)
        g1, g7 = shift(g0, "z", 1), shift(g0, "z", -1)
        g2, g6 = shift(g1, "z", 1), shift(g7, "z", -1)
        g3, g5 = shift(g2, "z", 1), shift(g6, "z", -1)
        g4a, g4b = shift(g3[:64], "z", 1), shift(g5[64:], "z", -1)
        ha = jnp.concatenate([a1, a2, a3, a4, a5, a6, a7], axis=0)
        ha1, ha3 = shift(ha, "x", 1), shift(ha, "x", -1)
        ha2a, ha2b = shift(ha1[:112], "x", 1), shift(ha3[112:], "x", -1)

    with jax.named_scope("send_slots"):
        cap = prefix.shape[-1]
        inst, clus = inst.reshape(32, 1, cap), clus.reshape(32, 1, cap)
        valid = jnp.arange(cap, dtype=jnp.int32)[None, None, :] < counts.reshape(32, 1, 1)
        nothing = jnp.zeros((), BF16)
        alpha = jnp.where(valid, prefix.reshape(32, 1, cap), nothing)
        want = jnp.where(valid, jnp.swapaxes(targets.reshape(32, cap, 32), 1, 2), nothing)
        side = jnp.concatenate([want, alpha, inst.astype(BF16), clus.astype(BF16)], axis=1)
        side = jnp.pad(side, ((0, 0), (0, 5), (0, 128 - cap))).reshape(NZ, NX, 40, 128)
        side = jnp.roll(jnp.roll(side, -iz, axis=0), -ix, axis=1)
        u = [side[:, 0]] + [shift(side[:, d], "x", d) for d in range(1, NX)]
        v = jnp.stack(u, axis=1)
        slots = [v[0]] + [shift(v[d], "z", d) for d in range(1, NZ)]

    w = jnp.concatenate([jnp.swapaxes(lw, 0, 1).reshape(512, 768), cw], axis=0)
    ga, gb, gw = owner_terms(
        (e, x1, x2, x3, a1, a2, a3, a4, a5, a6, a7, ha1, ha3, ha2a, ha2b)
        + (g0, g1, g2, g3, g4a, g4b, g5, g6, g7)
        + tuple(slots)
        + (w,)
    )

    with jax.named_scope("return_rows"):
        down = shift(gb[4, :64], "z", -1)
        up = shift(gb[4, 64:], "z", 1)
        down = shift(jnp.concatenate([add(gb[3, :64], down), gb[3, 64:]], axis=0), "z", -1)
        up = shift(jnp.concatenate([gb[5, :64], add(gb[5, 64:], up)], axis=0), "z", 1)
        left = shift(ga[2, :128], "x", -1)
        right = shift(ga[2, 128:], "x", 1)
        down, up = shift(add(gb[2], down), "z", -1), shift(add(gb[6], up), "z", 1)
        left = shift(jnp.concatenate([add(ga[1, :128], left), ga[1, 128:]], axis=0), "x", -1)
        right = shift(jnp.concatenate([ga[3, :128], add(ga[3, 128:], right)], axis=0), "x", 1)
        down, up = shift(add(gb[1], down), "z", -1), shift(add(gb[7], up), "z", 1)
        rb = gb[0].astype(F32) + down.astype(F32) + up.astype(F32)
        ra = ga[0].astype(F32) + left.astype(F32) + right.astype(F32)
        rbh = rb.astype(BF16)
        out_b = rb[:HALF]
        for d in range(1, NX):
            out_b = out_b + shift(rbh[d * HALF : (d + 1) * HALF], "x", -d).astype(F32)
        ra = ra.reshape(NZ, HALF, 768)
        rah = ra.astype(BF16)
        down = shift(rah[4, :16], "z", -1)
        up = shift(rah[4, 16:], "z", 1)
        down = shift(jnp.concatenate([add(rah[3, :16], down), rah[3, 16:]], axis=0), "z", -1)
        up = shift(jnp.concatenate([rah[5, :16], add(rah[5, 16:], up)], axis=0), "z", 1)
        down, up = shift(add(rah[2], down), "z", -1), shift(add(rah[6], up), "z", 1)
        down, up = shift(add(rah[1], down), "z", -1), shift(add(rah[7], up), "z", 1)
        out_a = ra[0] + down.astype(F32) + up.astype(F32)
        grad_embed = jnp.concatenate([out_a, out_b], axis=0)

    with jax.named_scope("sum_weights"):
        leaf = gw[:512].reshape(NY, NC, 64, 768)
        first = ic == 0
        keep = jnp.where(first, leaf[:, 0], leaf[:, 1])
        give = jnp.where(first, leaf[:, 1], leaf[:, 0])
        keep = keep + shift(give, "core", 1)

        def piece(d):
            return lax.dynamic_index_in_dim(keep, (iy + d) % NY, 0, keepdims=False)

        out_leaf = piece(0)
        for d in range(1, NY):
            out_leaf = out_leaf + shift(piece(d), "y", d)
        grad_leaf = jnp.swapaxes(out_leaf.reshape(4, 16, 768), 0, 1)
        up1 = gw[512:]
        up1 = up1 + shift(up1, "core", 1)
        up1 = up1 + lax.ppermute(up1, "y", [(i, i ^ 1) for i in range(NY)])
        grad_cluster = up1 + lax.ppermute(up1, "y", [(i, i ^ 2) for i in range(NY)])
    return grad_embed, grad_cluster, grad_leaf


def solution(mesh):
    fine = Mesh(mesh.devices.reshape(NY, NC, NZ, NX), ("y", "core", "z", "x"))
    dp, label = ("y", "core"), ("z", "x")
    every = dp + label
    in_specs = (
        P(every, None),
        P(label, None),
        P(label, None, None),
        P(dp, label, None, None),
        P(dp, label, None, None),
        P(dp, label, None),
        P(dp, label, None, None),
        P(dp, label, None, None, None),
    )
    out_specs = (P(every, None), P(label, None), P(label, dp, None))
    return jax.shard_map(shards, mesh=fine, in_specs=in_specs, out_specs=out_specs, check_vma=False)
```

```python
import jax
import jax.numpy as jnp
from jax import lax
from jax.experimental import pallas as pl
from jax.experimental.pallas import tpu as pltpu
from jax.sharding import Mesh, PartitionSpec as P

BF16 = jnp.bfloat16
F32 = jnp.float32
NY, NC, NZ, NX = 4, 2, 8, 4
SIZE = {"y": NY, "core": NC, "z": NZ, "x": NX}
INST, D, KIDS, CL = 64, 768, 32, 16
ROWS = INST * NZ
WIDE = (KIDS + 1) * CL
PART = 17 * CL
NT = (((1,), (1,)), ((), ()))
NN = (((1,), (0,)), ((), ()))
TN = (((0,), (0,)), ((), ()))
VMEM = pl.BlockSpec(memory_space=pltpu.VMEM)
PARAMS = pltpu.CompilerParams(vmem_limit_bytes=40 * 1024 * 1024)


def dot(a, b, dims):
    return lax.dot_general(a, b, dims, preferred_element_type=F32)


def shift(x, axis, by):
    n = SIZE[axis]
    return lax.ppermute(x, axis, [(i, (i + by) % n) for i in range(n)])


def slot_kernel(slots, ay, wide):
    lane_row = lax.broadcasted_iota(jnp.int32, (256, 128), 0)
    cluster_row = lax.broadcasted_iota(jnp.int32, (CL, 128), 0)
    left = []
    for q in range(4):
        side = slots[q, 0].astype(F32)
        alpha = side[KIDS : KIDS + 1]
        inst = side[KIDS + 1 : KIDS + 2].astype(jnp.int32)
        clus = side[KIDS + 2 : KIDS + 3].astype(jnp.int32)
        left.append(jnp.where(lane_row == inst + q * INST, alpha, 0.0).astype(BF16))
        member = cluster_row == clus
        for k in range(KIDS + 1):
            wide[k * CL : k * CL + CL, q * 128 : q * 128 + 128] = jnp.where(
                member, side[k : k + 1], 0.0
            ).astype(BF16)
    ay[0] = dot(wide[...], jnp.concatenate(left, axis=1), NT)


def sum_slots(slots):
    return pl.pallas_call(
        slot_kernel,
        grid=(NX, 2),
        out_shape=jax.ShapeDtypeStruct((NX, WIDE, ROWS), F32),
        in_specs=[pl.BlockSpec((4, 1, 40, 128), lambda o, g: (g, o, 0, 0))],
        out_specs=pl.BlockSpec((1, WIDE, 256), lambda o, g: (o, 0, g)),
        scratch_shapes=[pltpu.VMEM((WIDE, 512), BF16)],
        compiler_params=PARAMS,
    )(slots)


def first_kernel(place, e, w, a, b, c, d, ao, bo, co, do, ay, give, top, dzs, wall, z):
    r = pl.program_id(0)
    core = place[1]
    mine = pl.multiple_of(core * 256, 256)
    other = pl.multiple_of((1 - core) * 256, 256)

    @pl.when(r == 0)
    def _():
        wall[0] = w[...]
        for at, near, far in ((1, a, ao), (3, b, bo)):
            wall[at, pl.ds(mine, PART)] = near[...]
            wall[at, pl.ds(other, PART)] = far[...]
        wall[2, pl.ds(mine, 144)] = c[...]
        wall[2, pl.ds(pl.multiple_of(mine + 144, 16), 128)] = d[...]
        wall[2, pl.ds(other, 144)] = co[...]
        wall[2, pl.ds(pl.multiple_of(other + 144, 16), 128)] = do[...]

    z[...] = dot(wall[r], e[...], NT)
    s1 = jax.nn.sigmoid(z[KIDS * CL :])
    s1a = s1 * ay[0, KIDS * CL :]
    total = jnp.zeros((CL, ROWS), F32)
    for k in range(KIDS):
        at = pl.ds(k * CL, CL)
        s2 = jax.nn.sigmoid(z[at])
        t = s2 * (s1a * s2 - ay[0, at])
        total = total + t
        dzs[0, at] = (s1 * (1.0 - s2) * t).astype(BF16)
    dzs[0, KIDS * CL :] = (total * s1 * (1.0 - s1)).astype(BF16)
    out = dot(dzs[0, pl.ds(other, 256)], e[...], NN).astype(BF16)
    for y in range(NY):
        give[y, 0] = out[y * 64 : y * 64 + 64]
    top[0] = dot(dzs[0, KIDS * CL :], e[...], NN)


def first_terms(place, e, w, pieces, ay):
    def owner(r, place):
        return lax.rem(place[0] - r + NX, NX)

    return pl.pallas_call(
        first_kernel,
        grid_spec=pltpu.PrefetchScalarGridSpec(
            num_scalar_prefetch=1,
            grid=(NX,),
            in_specs=[VMEM] * (2 + len(pieces))
            + [pl.BlockSpec((1, WIDE, ROWS), lambda r, p: (owner(r, p), 0, 0))],
            out_specs=[
                pl.BlockSpec((NY, 1, 64, D), lambda r, p: (0, owner(r, p), 0, 0)),
                pl.BlockSpec((1, CL, D), lambda r, p: (owner(r, p), 0, 0)),
                pl.BlockSpec((1, WIDE, ROWS), lambda r, p: (r, 0, 0)),
                VMEM,
            ],
            scratch_shapes=[pltpu.VMEM((WIDE, ROWS), F32)],
        ),
        out_shape=(
            jax.ShapeDtypeStruct((NY, NX, 64, D), BF16),
            jax.ShapeDtypeStruct((NX, CL, D), F32),
            jax.ShapeDtypeStruct((NX, WIDE, ROWS), BF16),
            jax.ShapeDtypeStruct((NX, WIDE, D), BF16),
        ),
        compiler_params=PARAMS,
    )(place, e, w, *pieces, ay)


def second_kernel(place, e, dzs, wall, back, own, keep, ge):
    x, core, zz = place[0], place[1], place[2]
    ge[...] = dot(dzs[0], wall[0], TN)
    for r in range(1, NX):
        ge[...] += dot(dzs[r], wall[r], TN)
    for d in range(NZ):
        at = lax.rem(zz + d, NZ) * INST
        block = ge[pl.ds(pl.multiple_of(at, INST), INST)]
        if d == 0:
            own[...] = block
        else:
            back[d - 1] = block.astype(BF16)
    mine = pl.multiple_of(core * 256, 256)
    for r in range(NX):
        out = dot(dzs[r, pl.ds(mine, 256)], e[...], NN)
        to = lax.rem(x - r + NX, NX)
        for y in range(NY):
            keep[y, to] = out[y * 64 : y * 64 + 64]


def second_terms(place, e, dzs, wall):
    return pl.pallas_call(
        second_kernel,
        out_shape=(
            jax.ShapeDtypeStruct((NZ - 1, INST, D), BF16),
            jax.ShapeDtypeStruct((INST, D), F32),
            jax.ShapeDtypeStruct((NY, NX, 64, D), F32),
        ),
        in_specs=[pl.BlockSpec(memory_space=pltpu.SMEM)] + [VMEM] * 3,
        out_specs=[VMEM] * 3,
        scratch_shapes=[pltpu.VMEM((ROWS, D), F32)],
        compiler_params=PARAMS,
    )(place, e, dzs, wall)


def shards(e, cw, lw, inst, clus, counts, prefix, targets):
    iz, ix, ic = lax.axis_index("z"), lax.axis_index("x"), lax.axis_index("core")
    place = jnp.stack([ix, ic, iz]).astype(jnp.int32)

    with jax.named_scope("rows"):
        rows = lax.all_gather(e, "z", axis=0, tiled=True)

    with jax.named_scope("weights"):
        leaf = lw.reshape(CL, NY, NC, 4, D).transpose(2, 1, 3, 0, 4).reshape(KIDS * CL, D)
        w = jnp.concatenate([leaf, cw], axis=0)
        part = lax.dynamic_slice_in_dim(w, ic * 256, PART, 0)
        a, b = shift(part, "x", 1), shift(part, "x", -1)
        c, d = shift(a[:144], "x", 1), shift(b[144:], "x", -1)
        pieces = [a, b, c, d]
        pieces += [shift(p, "core", 1) for p in pieces]

    with jax.named_scope("slots"):
        cap = prefix.shape[-1]
        owners = NZ * NX
        inst, clus = inst.reshape(owners, 1, cap), clus.reshape(owners, 1, cap)
        valid = jnp.arange(cap, dtype=jnp.int32)[None, None, :] < counts.reshape(owners, 1, 1)
        nothing = jnp.zeros((), BF16)
        alpha = jnp.where(valid, prefix.reshape(owners, 1, cap), nothing)
        want = targets.reshape(owners, cap, NY, NC, 4).transpose(0, 3, 2, 4, 1)
        want = jnp.where(valid, want.reshape(owners, KIDS, cap), nothing)
        side = jnp.concatenate([want, alpha, inst.astype(BF16), clus.astype(BF16)], axis=1)
        side = jnp.pad(side, ((0, 0), (0, 5), (0, 128 - cap))).reshape(NZ, NX, 40, 128)
        slots = lax.all_to_all(side, "z", 0, 0, tiled=True)
    ay = sum_slots(slots)

    give, top, dzs, wall = first_terms(place, rows, w, pieces, ay)
    with jax.named_scope("weights_core"):
        got = shift(give, "core", 1)
        top = top + shift(top, "core", 1)
    back, own, keep = second_terms(place, rows, dzs, wall)

    with jax.named_scope("weights_back"):
        summed = (keep + got.astype(F32)).astype(BF16)
        tops = jnp.broadcast_to(top.astype(BF16)[None], (NY, NX, CL, D))
        out = jnp.concatenate([summed, tops], axis=2).reshape(NY * NX, 64 + CL, D)
        out = lax.all_to_all(out, ("y", "x"), 0, 0, tiled=True)
        out = jnp.sum(out.astype(F32), axis=0)
        grad_leaf = jnp.swapaxes(out[:64].reshape(4, CL, D), 0, 1)
        grad_cluster = out[64:]

    with jax.named_scope("rows_back"):
        grad_embed = own
        for d in (1, 7, 2, 6, 3, 5, 4):
            grad_embed = grad_embed + shift(back[d - 1], "z", d).astype(F32)
    return grad_embed, grad_cluster, grad_leaf


def solution(mesh):
    fine = Mesh(mesh.devices.reshape(NY, NC, NZ, NX), ("y", "core", "z", "x"))
    dp, label = ("y", "core"), ("z", "x")
    every = dp + label
    in_specs = (
        P(every, None),
        P(label, None),
        P(label, None, None),
        P(dp, label, None, None),
        P(dp, label, None, None),
        P(dp, label, None),
        P(dp, label, None, None),
        P(dp, label, None, None, None),
    )
    out_specs = (P(every, None), P(label, None), P(label, dp, None))
    return jax.shard_map(shards, mesh=fine, in_specs=in_specs, out_specs=out_specs, check_vma=False)
```

```python
import functools

import jax
import jax.numpy as jnp
from jax import lax
from jax.experimental import pallas as pl
from jax.experimental.pallas import tpu as pltpu
from jax.sharding import Mesh, PartitionSpec as P

BF16 = jnp.bfloat16
F32 = jnp.float32
NY, NC, NZ, NX = 4, 2, 8, 4
SIZE = {"y": NY, "core": NC, "z": NZ, "x": NX}
INST, D, KIDS, CL = 64, 768, 32, 16
ROWS = INST * NZ
WIDE = (KIDS + 1) * CL
PART = 17 * CL
NT = (((1,), (1,)), ((), ()))
NN = (((1,), (0,)), ((), ()))
TN = (((0,), (0,)), ((), ()))
VMEM = pl.BlockSpec(memory_space=pltpu.VMEM)
SMEM = pl.BlockSpec(memory_space=pltpu.SMEM)
PARAMS = pltpu.CompilerParams(vmem_limit_bytes=40 * 1024 * 1024)


def dot(a, b, dims):
    return lax.dot_general(a, b, dims, preferred_element_type=F32)


def shift(x, axis, by):
    n = SIZE[axis]
    return lax.ppermute(x, axis, [(i, (i + by) % n) for i in range(n)])


def cost(flops):
    return pl.CostEstimate(flops=flops, bytes_accessed=1 << 20, transcendentals=0)


def slot_kernel(place, slots, ay, wide):
    x, z = place[0], place[2]
    lane_row = lax.broadcasted_iota(jnp.int32, (256, 128), 0)
    cluster_row = lax.broadcasted_iota(jnp.int32, (CL, 128), 0)

    def step(i, _):
        r, g = i // 2, lax.rem(i, 2)
        owner = lax.rem(x - r + NX, NX)
        left = []
        for q in range(4):
            side = slots[lax.rem(z - (g * 4 + q) + NZ, NZ), owner].astype(F32)
            alpha = side[KIDS : KIDS + 1]
            inst = side[KIDS + 1 : KIDS + 2].astype(jnp.int32)
            clus = side[KIDS + 2 : KIDS + 3].astype(jnp.int32)
            left.append(jnp.where(lane_row == inst + q * INST, alpha, 0.0).astype(BF16))
            member = cluster_row == clus
            for k in range(KIDS + 1):
                wide[k * CL : k * CL + CL, q * 128 : q * 128 + 128] = jnp.where(
                    member, side[k : k + 1], 0.0
                ).astype(BF16)
        ay[r, :, pl.ds(pl.multiple_of(g * 256, 256), 256)] = dot(
            wide[...], jnp.concatenate(left, axis=1), NT
        )
        return 0

    lax.fori_loop(0, 2 * NX, step, 0)


def sum_slots(place, slots):
    return pl.pallas_call(
        slot_kernel,
        out_shape=jax.ShapeDtypeStruct((NX, WIDE, ROWS), F32),
        in_specs=[SMEM, VMEM],
        out_specs=VMEM,
        scratch_shapes=[pltpu.VMEM((WIDE, 512), BF16)],
        compiler_params=PARAMS,
        cost_estimate=cost(2 * 10**9),
    )(place, slots)


def owner_kernel(r, n_e, n_w, place, *refs):
    core = place[1]
    blocks, refs = refs[:n_e], refs[n_e:]
    pieces, refs = refs[:n_w], refs[n_w:]
    ay, refs = refs[0], refs[1:]
    keep, give, dzs, refs = refs[0], refs[1], refs[2], refs[3:]
    z = refs[-1]
    mine = pl.multiple_of(core * 256, 256)
    other = pl.multiple_of((1 - core) * 256, 256)
    if n_e > 1:
        e = refs[0]
        for i in range(n_e):
            e[i * INST : i * INST + INST] = blocks[i][...]
    else:
        e = blocks[0]
    if n_w == 1:
        w = pieces[0]
    else:
        w = refs[-2]
        half = n_w // 2
        for base, part in ((mine, pieces[:half]), (other, pieces[half:])):
            at = 0
            for p in part:
                w[pl.ds(pl.multiple_of(base + at, 16), p.shape[0])] = p[...]
                at += p.shape[0]
    z[...] = dot(w[...], e[...], NT)
    s1 = jax.nn.sigmoid(z[KIDS * CL :])
    s1a = s1 * ay[r, KIDS * CL :]
    total = jnp.zeros((CL, ROWS), F32)
    for k in range(KIDS):
        at = pl.ds(k * CL, CL)
        s2 = jax.nn.sigmoid(z[at])
        t = s2 * (s1a * s2 - ay[r, at])
        total = total + t
        dzs[at] = (s1 * (1.0 - s2) * t).astype(BF16)
    dzs[KIDS * CL :] = (total * s1 * (1.0 - s1)).astype(BF16)
    top = dot(dzs[KIDS * CL :], e[...], NN).astype(BF16)
    give[:256] = dot(dzs[pl.ds(other, 256)], e[...], NN).astype(BF16)
    give[256:] = top
    keep[:256] = dot(dzs[pl.ds(mine, 256)], e[...], NN)
    keep[256:] = top.astype(F32)


def owner_terms(r, place, blocks, pieces, ay):
    n_e, n_w = len(blocks), len(pieces)
    out = [
        jax.ShapeDtypeStruct((PART, D), F32),
        jax.ShapeDtypeStruct((PART, D), BF16),
        jax.ShapeDtypeStruct((WIDE, ROWS), BF16),
    ]
    if n_e > 1:
        out.append(jax.ShapeDtypeStruct((ROWS, D), BF16))
    if n_w > 1:
        out.append(jax.ShapeDtypeStruct((WIDE, D), BF16))
    return pl.pallas_call(
        functools.partial(owner_kernel, r, n_e, n_w),
        out_shape=tuple(out),
        in_specs=[SMEM] + [VMEM] * (n_e + n_w + 1),
        out_specs=[VMEM] * len(out),
        scratch_shapes=[pltpu.VMEM((WIDE, ROWS), F32)],
        compiler_params=PARAMS,
        cost_estimate=cost(2 * 10**9),
    )(place, *blocks, *pieces, ay)


def rows_kernel(*refs):
    dzs, ws, back, own, ge = refs[:NX], refs[NX : 2 * NX], refs[-3], refs[-2], refs[-1]
    ge[...] = dot(dzs[0][...], ws[0][...], TN)
    for r in range(1, NX):
        ge[...] += dot(dzs[r][...], ws[r][...], TN)
    own[...] = ge[:INST]
    for d in range(1, NZ):
        back[d - 1] = ge[d * INST : d * INST + INST].astype(BF16)


def row_terms(dzs, ws):
    return pl.pallas_call(
        rows_kernel,
        out_shape=(
            jax.ShapeDtypeStruct((NZ - 1, INST, D), BF16),
            jax.ShapeDtypeStruct((INST, D), F32),
        ),
        in_specs=[VMEM] * (2 * NX),
        out_specs=[VMEM] * 2,
        scratch_shapes=[pltpu.VMEM((ROWS, D), F32)],
        compiler_params=PARAMS,
        cost_estimate=cost(2 * 10**9),
    )(*dzs, *ws)


def shards(e, cw, lw, inst, clus, counts, prefix, targets):
    ix, iy, iz = lax.axis_index("x"), lax.axis_index("y"), lax.axis_index("z")
    ic = lax.axis_index("core")
    place = jnp.stack([ix, ic, iz]).astype(jnp.int32)

    with jax.named_scope("rows"):
        e1, e7 = shift(e, "z", 1), shift(e, "z", -1)
        e2, e6 = shift(e1, "z", 1), shift(e7, "z", -1)
        e3, e5 = shift(e2, "z", 1), shift(e6, "z", -1)
        e4a, e4b = shift(e3[:32], "z", 1), shift(e5[32:], "z", -1)
        blocks = [e, e1, e2, e3, jnp.concatenate([e4a, e4b], axis=0), e5, e6, e7]

    with jax.named_scope("weights"):
        leaf = lw.reshape(CL, NY, NC, 4, D).transpose(2, 1, 3, 0, 4).reshape(KIDS * CL, D)
        w = jnp.concatenate([leaf, cw], axis=0)
        part = lax.dynamic_slice_in_dim(w, ic * 256, PART, 0)
        a, b = shift(part, "x", 1), shift(part, "x", -1)
        c, d = shift(a[:144], "x", 1), shift(b[144:], "x", -1)
        ao, bo, co, do = (shift(p, "core", 1) for p in (a, b, c, d))

    with jax.named_scope("slots"):
        cap = prefix.shape[-1]
        owners = NZ * NX
        inst, clus = inst.reshape(owners, 1, cap), clus.reshape(owners, 1, cap)
        valid = jnp.arange(cap, dtype=jnp.int32)[None, None, :] < counts.reshape(owners, 1, 1)
        nothing = jnp.zeros((), BF16)
        alpha = jnp.where(valid, prefix.reshape(owners, 1, cap), nothing)
        want = targets.reshape(owners, cap, NY, NC, 4).transpose(0, 3, 2, 4, 1)
        want = jnp.where(valid, want.reshape(owners, KIDS, cap), nothing)
        side = jnp.concatenate([want, alpha, inst.astype(BF16), clus.astype(BF16)], axis=1)
        side = jnp.pad(side, ((0, 0), (0, 5), (0, 128 - cap))).reshape(NZ, NX, 40, 128)
        slots = lax.all_to_all(side, "z", 0, 0, tiled=True)
    ay = sum_slots(place, slots)

    def settle(keep, give):
        return keep + shift(give, "core", 1).astype(F32)

    keep2, give2, dz2, rows, w2 = owner_terms(2, place, blocks, (c, d, co, do), ay)
    with jax.named_scope("weights_x"):
        t2 = settle(keep2, give2).astype(BF16)
        low, high = shift(t2[:144], "x", -1), shift(t2[144:], "x", 1)
    keep1, give1, dz1, w1 = owner_terms(1, place, (rows,), (a, ao), ay)
    keep3, give3, dz3, w3 = owner_terms(3, place, (rows,), (b, bo), ay)
    with jax.named_scope("weights_x"):
        t1 = settle(keep1, give1) + jnp.pad(low.astype(F32), ((0, 128), (0, 0)))
        t3 = settle(keep3, give3) + jnp.pad(high.astype(F32), ((144, 0), (0, 0)))
        t1, t3 = shift(t1.astype(BF16), "x", -1), shift(t3.astype(BF16), "x", 1)
    keep0, give0, dz0 = owner_terms(0, place, (rows,), (w,), ay)
    back, own = row_terms((dz0, dz1, dz2, dz3), (w, w1, w2, w3))

    with jax.named_scope("weights_y"):
        t0 = settle(keep0, give0) + t1.astype(F32) + t3.astype(F32)
        top = t0[256:].astype(BF16)

        def piece(d):
            return lax.dynamic_slice_in_dim(t0, lax.rem(iy + d, NY) * 64, 64, 0)

        got = [
            shift(jnp.concatenate([piece(d).astype(BF16), top], axis=0), "y", d).astype(F32)
            for d in (1, 3, 2)
        ]
        out = piece(0) + got[0][:64] + got[1][:64] + got[2][:64]
        grad_leaf = jnp.swapaxes(out.reshape(4, CL, D), 0, 1)
        even = lax.rem(iy, 2) == 0
        one, three, two = (g[64:] for g in got)
        near = jnp.where(even, three, one)
        far = jnp.where(even, one, three)
        grad_cluster = (top.astype(F32) + near) + (two + far)

    with jax.named_scope("rows_back"):
        grad_embed = own
        for d in (1, 7, 2, 6, 3, 5, 4):
            grad_embed = grad_embed + shift(back[d - 1], "z", -d).astype(F32)
    return grad_embed, grad_cluster, grad_leaf


def solution(mesh):
    fine = Mesh(mesh.devices.reshape(NY, NC, NZ, NX), ("y", "core", "z", "x"))
    dp, label = ("y", "core"), ("z", "x")
    every = dp + label
    in_specs = (
        P(every, None),
        P(label, None),
        P(label, None, None),
        P(dp, label, None, None),
        P(dp, label, None, None),
        P(dp, label, None),
        P(dp, label, None, None),
        P(dp, label, None, None, None),
    )
    out_specs = (P(every, None), P(label, None), P(label, dp, None))
    return jax.shard_map(shards, mesh=fine, in_specs=in_specs, out_specs=out_specs, check_vma=False)
```

```python
import functools

import jax
import jax.numpy as jnp
from jax import lax
from jax.experimental import pallas as pl
from jax.experimental.pallas import tpu as pltpu
from jax.sharding import Mesh, PartitionSpec as P

BF16 = jnp.bfloat16
F32 = jnp.float32
NY, NC, NZ, NX = 4, 2, 8, 4
SIZE = {"y": NY, "core": NC, "z": NZ, "x": NX}
INST, D, KIDS, CL = 64, 768, 32, 16
ROWS = INST * NZ
WIDE = (KIDS + 1) * CL
TOP = 256
PART = 272
NT = (((1,), (1,)), ((), ()))
NN = (((1,), (0,)), ((), ()))
TN = (((0,), (0,)), ((), ()))
VMEM = pl.BlockSpec(memory_space=pltpu.VMEM)
SMEM = pl.BlockSpec(memory_space=pltpu.SMEM)


def dot(a, b, dims):
    return lax.dot_general(a, b, dims, preferred_element_type=F32)


def call(kernel, out, args, scratch=(), flops=10**8, **static):
    return pl.pallas_call(
        functools.partial(kernel, **static),
        out_shape=tuple(jax.ShapeDtypeStruct(s, t) for s, t in out),
        in_specs=[SMEM] + [VMEM] * (len(args) - 1),
        out_specs=(VMEM,) * len(out),
        scratch_shapes=[pltpu.VMEM(s, t) for s, t in scratch],
        compiler_params=pltpu.CompilerParams(vmem_limit_bytes=16 * 1024 * 1024),
        cost_estimate=pl.CostEstimate(flops=flops, bytes_accessed=1 << 20, transcendentals=0),
    )(*args)


def shift(x, axis, by):
    n = SIZE[axis]
    return lax.ppermute(x, axis, [(i, (i + by) % n) for i in range(n)])


def swap(x):
    return shift(x, "core", 1)


def turn(x, axis, by):
    n = SIZE[axis]
    pairs = [(i, (i + by) % n) for i in range(n)] + [(n + i, n + (i - by) % n) for i in range(n)]
    return lax.ppermute(x, ("core", axis), pairs)


def slot_kernel(place, slots, ay, wide):
    x, z, sign = place[0], place[2], 1 - 2 * place[1]
    lane_row = lax.broadcasted_iota(jnp.int32, (256, 128), 0)
    cluster_row = lax.broadcasted_iota(jnp.int32, (CL, 128), 0)

    def step(i, _):
        r, g = i // 2, lax.rem(i, 2)
        owner = lax.rem(x - sign * r + NX, NX)
        left = []
        for q in range(4):
            source = lax.rem(z - sign * (g * 4 + q) + NZ, NZ)
            side = slots[source, owner].astype(F32)
            alpha = side[KIDS : KIDS + 1]
            inst = side[KIDS + 1 : KIDS + 2].astype(jnp.int32)
            clus = side[KIDS + 2 : KIDS + 3].astype(jnp.int32)
            left.append(jnp.where(lane_row == inst + q * INST, alpha, 0.0).astype(BF16))
            member = cluster_row == clus
            for k in range(KIDS + 1):
                at = TOP if k == KIDS else k * CL + (CL if k * CL >= TOP else 0)
                wide[at : at + CL, q * 128 : q * 128 + 128] = jnp.where(
                    member, side[k : k + 1], 0.0
                ).astype(BF16)
        ay[r, :, pl.ds(pl.multiple_of(g * 256, 256), 256)] = dot(
            wide[...], jnp.concatenate(left, axis=1), NT
        )
        return 0

    lax.fori_loop(0, 2 * NX, step, 0)


def owner_kernel(place, *refs, r):
    core = place[1]
    if r == 2:
        blocks, (near, far, ay, a, b, dzs, e, w, z) = refs[:8], refs[8:]
        for d, (ref, lo) in enumerate(zip(blocks, (0,) * NZ)):
            e[d * INST : d * INST + INST] = ref[lo : lo + INST]
        w[pl.ds(pl.multiple_of(core * TOP, 16), PART)] = near[...]
        w[pl.ds(pl.multiple_of((1 - core) * TOP, 16), PART)] = far[...]
    elif r == 0:
        e, w, ay, a, b, dzs, z = refs
    else:
        e, w, ay, a, dzs, z = refs
    z[...] = dot(w[...], e[...], NT)
    top = pl.ds(TOP, CL)
    s1 = jax.nn.sigmoid(z[top])
    s1a = s1 * ay[r, top]
    total = jnp.zeros((CL, ROWS), F32)
    for k in range(KIDS + 1):
        if k * CL == TOP:
            continue
        at = pl.ds(k * CL, CL)
        s2 = jax.nn.sigmoid(z[at])
        t = s2 * (s1a * s2 - ay[r, at])
        total = total + t
        dzs[at] = (s1 * (1.0 - s2) * t).astype(BF16)
    dzs[top] = (total * s1 * (1.0 - s1)).astype(BF16)
    if r in (1, 3):
        a[...] = dot(dzs[...], e[...], NN).astype(a.dtype)
        return
    mine = pl.ds(pl.multiple_of(core * TOP, 16), PART)
    other = pl.ds(pl.multiple_of((1 - core) * TOP, 16), PART)
    b[...] = dot(dzs[other], e[...], NN).astype(BF16)
    a[...] = dot(dzs[mine], e[...], NN).astype(a.dtype)
    if r == 2:

        @pl.when(core == 0)
        def _():
            b[:CL] = jnp.zeros((CL, D), BF16)

        @pl.when(core == 1)
        def _():
            a[:CL] = jnp.zeros((CL, D), F32)


def rows_kernel(place, *refs):
    dzs, ws, (near, far, own, ge) = refs[:NX], refs[NX : 2 * NX], refs[2 * NX :]
    ge[...] = dot(dzs[0][...], ws[0][...], TN)
    for r in range(1, NX):
        ge[...] += dot(dzs[r][...], ws[r][...], TN)
    own[...] = ge[:INST]
    near[...] = ge[INST : 5 * INST].astype(BF16)
    for i, d in enumerate((7, 6, 5)):
        far[i * INST : i * INST + INST] = ge[d * INST : d * INST + INST].astype(BF16)


def pass_kernel(place, near, far, got, out, *, d):
    at = pl.ds((d - 1) * INST, INST)
    out[:INST] = (near[at].astype(F32) + got[:INST].astype(F32)).astype(BF16)
    if d == 3:
        out[INST:] = far[at]
    else:
        out[INST:] = (far[at].astype(F32) + got[INST:].astype(F32)).astype(BF16)


def merge_kernel(place, a, b, got, out, total):
    total[...] = a[...] + b[...].astype(F32)
    at = pl.ds(pl.multiple_of(place[1] * TOP, 16), PART)
    total[at] = total[at] + got[...].astype(F32)
    out[...] = total[...].astype(BF16)


def split_kernel(place, keep, give, mine, other, own, top, p1, p2, p3, total):
    core, y = place[1], place[3]
    at = pl.ds(pl.multiple_of(core * TOP, 16), PART)
    total[...] = (keep[...].astype(F32) + give[...].astype(F32)) + (
        mine[at].astype(F32) + other[...].astype(F32)
    )

    def piece(d):
        return total[pl.ds(pl.multiple_of(core * CL + lax.rem(y + d, NY) * 64, 16), 64)]

    own[...] = piece(0)
    cluster = total[pl.ds(pl.multiple_of((1 - core) * TOP, 16), CL)].astype(BF16)
    top[...] = cluster
    for d, p in ((1, p1), (2, p2), (3, p3)):
        p[:64] = piece(d).astype(BF16)
        p[64:] = cluster


def finish_kernel(place, own, top, g1, g2, g3, leaf, cluster):
    out = own[...] + g1[:64].astype(F32) + g2[:64].astype(F32) + g3[:64].astype(F32)
    for k in range(4):
        leaf[:, k, :] = out[k * CL : k * CL + CL]
    even = lax.rem(place[3], 2) == 0
    one, two, three = (g[64:].astype(F32) for g in (g1, g2, g3))
    near = jnp.where(even, three, one)
    far = jnp.where(even, one, three)
    cluster[...] = (top[...].astype(F32) + near) + (two + far)


def shards(e, cw, lw, inst, clus, counts, prefix, targets):
    iy, ic, iz, ix = (lax.axis_index(n) for n in ("y", "core", "z", "x"))
    place = jnp.stack([ix, ic, iz, iy]).astype(jnp.int32)

    with jax.named_scope("rows"):
        p1 = turn(jnp.concatenate([e, swap(e)], axis=0), "z", 1)
        p2 = turn(p1, "z", 1)
        p3 = turn(p2, "z", 1)
        p4 = turn(p3[:INST], "z", 1)
        q1, q2, q3 = (swap(p[INST:]) for p in (p1, p2, p3))
        blocks = (e, p1, p2, p3, p4, q3, q2, q1)

    with jax.named_scope("weights"):
        leaf = lw.reshape(CL, NY, NC, 4, D).transpose(2, 1, 3, 0, 4).reshape(2, TOP, D)
        w = jnp.concatenate([leaf[0], cw, leaf[1]], axis=0)
        v1 = turn(w, "x", 1)
        v2 = turn(lax.dynamic_slice_in_dim(v1, ic * TOP, PART, 0), "x", 1)
        u1, u2 = swap(v1), swap(v2)

    with jax.named_scope("slots"):
        counts, _ = lax.optimization_barrier((counts, p1))
        cap = prefix.shape[-1]
        owners = NZ * NX
        inst, clus = inst.reshape(owners, 1, cap), clus.reshape(owners, 1, cap)
        valid = jnp.arange(cap, dtype=jnp.int32)[None, None, :] < counts.reshape(owners, 1, 1)
        nothing = jnp.zeros((), BF16)
        alpha = jnp.where(valid, prefix.reshape(owners, 1, cap), nothing)
        want = targets.reshape(owners, cap, NY, NC, 4).transpose(0, 3, 2, 4, 1)
        want = jnp.where(valid, want.reshape(owners, KIDS, cap), nothing)
        side = jnp.concatenate([want, alpha, inst.astype(BF16), clus.astype(BF16)], axis=1)
        side = jnp.pad(side, ((0, 0), (0, 5), (0, 128 - cap))).reshape(NZ, NX, 40, 128)
        slots = lax.all_to_all(side, "z", 0, 0, tiled=True)
    (ay,) = call(
        slot_kernel, [((NX, WIDE, ROWS), F32)], (place, slots), [((WIDE, 512), BF16)], 2 * 10**9
    )

    wide, dzs = ((WIDE, D), BF16), ((WIDE, ROWS), BF16)
    half, half32 = ((PART, D), BF16), ((PART, D), F32)
    z = [((WIDE, ROWS), F32)]
    work = 2 * 10**9

    a2, b2, dz2, rows, w2 = call(
        owner_kernel,
        [half32, half, dzs, ((ROWS, D), BF16), wide],
        (place,) + blocks + (v2, u2, ay),
        z,
        work,
        r=2,
    )
    with jax.named_scope("weights_x"):
        t2 = turn((a2 + swap(b2).astype(F32)).astype(BF16), "x", -1)
    b3, dz3 = call(owner_kernel, [wide, dzs], (place, rows, u1, ay), z, work, r=3)
    with jax.named_scope("weights_x"):
        b3 = swap(b3)
    a1, dz1 = call(
        owner_kernel, [((WIDE, D), F32), dzs], (place, rows, v1, ay), z, work, r=1
    )
    with jax.named_scope("weights_x"):
        (t1,) = call(merge_kernel, [wide], (place, a1, b3, t2), [((WIDE, D), F32)])
        t1 = turn(t1, "x", -1)
    a0, b0, dz0 = call(owner_kernel, [half, half, dzs], (place, rows, w, ay), z, work, r=0)
    near, far, own = call(
        rows_kernel,
        [((4 * INST, D), BF16), ((3 * INST, D), BF16), ((INST, D), F32)],
        (place, dz0, dz1, dz2, dz3, w, v1, w2, u1),
        [((ROWS, D), F32)],
        work,
    )

    with jax.named_scope("rows_back"):
        far = swap(far)
        run = turn(near[3 * INST :], "z", -1)
        for d in (3, 2, 1):
            (run,) = call(pass_kernel, [((2 * INST, D), BF16)], (place, near, far, run), d=d)
            run = turn(run, "z", -1)
        grad_embed = own + run[:INST].astype(F32) + swap(run[INST:]).astype(F32)

    with jax.named_scope("weights_y"):
        b0 = swap(b0)
        other = swap(lax.dynamic_slice_in_dim(t1, (1 - ic) * TOP, PART, 0))
        send = ((80, D), BF16)
        mine, top, s1, s2, s3 = call(
            split_kernel,
            [((64, D), F32), ((CL, D), BF16), send, send, send],
            (place, a0, b0, t1, other),
            [((PART, D), F32)],
        )
        g1, g3, g2 = shift(s1, "y", 1), shift(s3, "y", 3), shift(s2, "y", 2)
        grad_leaf, grad_cluster = call(
            finish_kernel, [((CL, 4, D), F32), ((CL, D), F32)], (place, mine, top, g1, g2, g3)
        )
    return grad_embed, grad_cluster, grad_leaf


def solution(mesh):
    fine = Mesh(mesh.devices.reshape(NY, NC, NZ, NX), ("y", "core", "z", "x"))
    dp, label = ("y", "core"), ("z", "x")
    every = dp + label
    in_specs = (
        P(every, None),
        P(label, None),
        P(label, None, None),
        P(dp, label, None, None),
        P(dp, label, None, None),
        P(dp, label, None),
        P(dp, label, None, None),
        P(dp, label, None, None, None),
    )
    out_specs = (P(every, None), P(label, None), P(label, dp, None))
    return jax.shard_map(shards, mesh=fine, in_specs=in_specs, out_specs=out_specs, check_vma=False)
```

```python
import functools

import jax
import jax.numpy as jnp
from jax import lax
from jax.experimental import pallas as pl
from jax.experimental.pallas import tpu as pltpu
from jax.sharding import Mesh, PartitionSpec as P

BF16 = jnp.bfloat16
F32 = jnp.float32
NY, NC, NZ, NX = 4, 2, 8, 4
SIZE = {"y": NY, "core": NC, "z": NZ, "x": NX}
INST, D, KIDS, CL = 64, 768, 32, 16
ROWS = INST * NZ
WIDE = (KIDS + 1) * CL
TOP = 256
PART = 272
CUT = 144
NT = (((1,), (1,)), ((), ()))
NN = (((1,), (0,)), ((), ()))
TN = (((0,), (0,)), ((), ()))
VMEM = pl.BlockSpec(memory_space=pltpu.VMEM)
SMEM = pl.BlockSpec(memory_space=pltpu.SMEM)


def dot(a, b, dims):
    return lax.dot_general(a, b, dims, preferred_element_type=F32)


def call(kernel, out, args, scratch=(), **static):
    return pl.pallas_call(
        functools.partial(kernel, **static),
        out_shape=tuple(jax.ShapeDtypeStruct(s, t) for s, t in out),
        in_specs=[SMEM] + [VMEM] * (len(args) - 1),
        out_specs=(VMEM,) * len(out),
        scratch_shapes=[pltpu.VMEM(s, t) for s, t in scratch],
        compiler_params=pltpu.CompilerParams(vmem_limit_bytes=16 * 1024 * 1024),
        cost_estimate=pl.CostEstimate(flops=2 * 10**9, bytes_accessed=1 << 20, transcendentals=0),
    )(*args)


def shift(x, axis, by):
    n = SIZE[axis]
    return lax.ppermute(x, axis, [(i, (i + by) % n) for i in range(n)])


def swap(x):
    return shift(x, "core", 1)


def turn(x, axis, by):
    n = SIZE[axis]
    pairs = [(i, (i + by) % n) for i in range(n)] + [(n + i, n + (i - by) % n) for i in range(n)]
    return lax.ppermute(x, ("core", axis), pairs)


def slot_kernel(place, slots, ay, wide):
    x, z, sign = place[0], place[2], 1 - 2 * place[1]
    lane_row = lax.broadcasted_iota(jnp.int32, (256, 128), 0)
    cluster_row = lax.broadcasted_iota(jnp.int32, (CL, 128), 0)

    def step(i, _):
        r, g = i // 2, lax.rem(i, 2)
        owner = lax.rem(x - r + NX, NX)
        left = []
        for q in range(4):
            source = lax.rem(z - sign * (g * 4 + q) + NZ, NZ)
            side = slots[source, owner].astype(F32)
            alpha = side[KIDS : KIDS + 1]
            inst = side[KIDS + 1 : KIDS + 2].astype(jnp.int32)
            clus = side[KIDS + 2 : KIDS + 3].astype(jnp.int32)
            left.append(jnp.where(lane_row == inst + q * INST, alpha, 0.0).astype(BF16))
            member = cluster_row == clus
            for k in range(KIDS + 1):
                at = TOP if k == KIDS else k * CL + (CL if k * CL >= TOP else 0)
                wide[at : at + CL, q * 128 : q * 128 + 128] = jnp.where(
                    member, side[k : k + 1], 0.0
                ).astype(BF16)
        ay[r, :, pl.ds(pl.multiple_of(g * 256, 256), 256)] = dot(
            wide[...], jnp.concatenate(left, axis=1), NT
        )
        return 0

    lax.fori_loop(0, 2 * NX, step, 0)


def owner_kernel(place, *refs, r):
    core = place[1]
    mine = pl.ds(pl.multiple_of(core * TOP, 16), PART)
    other = pl.ds(pl.multiple_of((1 - core) * TOP, 16), PART)
    if r == 2:
        blocks, (n1, n2, f1, f2, ay, a, b, dzs, e, w, z) = refs[:NZ], refs[NZ:]
        for d in range(NZ):
            e[d * INST : d * INST + INST] = blocks[d][:INST]
        for at, p1, p2 in ((core, n1, n2), (1 - core, f1, f2)):
            w[pl.ds(pl.multiple_of(at * TOP, 16), CUT)] = p1[...]
            w[pl.ds(pl.multiple_of(at * TOP + CUT, 16), PART - CUT)] = p2[...]
    elif r == 0:
        e, w, ay, a, b, dzs, z = refs
    else:
        e, near, far, ay, a, b, dzs, w, z = refs
        w[mine] = near[...]
        w[other] = far[...]
    z[...] = dot(w[...], e[...], NT)
    top = pl.ds(TOP, CL)
    s1 = jax.nn.sigmoid(z[top])
    s1a = s1 * ay[r, top]
    total = jnp.zeros((CL, ROWS), F32)
    for k in range(KIDS + 1):
        if k * CL == TOP:
            continue
        at = pl.ds(k * CL, CL)
        s2 = jax.nn.sigmoid(z[at])
        t = s2 * (s1a * s2 - ay[r, at])
        total = total + t
        dzs[at] = (s1 * (1.0 - s2) * t).astype(BF16)
    dzs[top] = (total * s1 * (1.0 - s1)).astype(BF16)
    b[...] = dot(dzs[other], e[...], NN).astype(BF16)
    a[...] = dot(dzs[mine], e[...], NN).astype(a.dtype)


def rows_kernel(place, *refs):
    dzs, ws, (near, last, far, own, ge) = refs[:NX], refs[NX : 2 * NX], refs[2 * NX :]
    ge[...] = dot(dzs[0][...], ws[0][...], TN)
    for r in range(1, NX):
        ge[...] += dot(dzs[r][...], ws[r][...], TN)
    own[...] = ge[:INST]
    near[...] = ge[INST : 4 * INST].astype(BF16)
    last[...] = ge[4 * INST : 5 * INST].astype(BF16)
    for i, d in enumerate((7, 6, 5)):
        far[i * INST : i * INST + INST] = ge[d * INST : d * INST + INST].astype(BF16)


def pack_kernel(place, near, far, h1, h3):
    for h, at in ((h1, 0), (h3, 2 * INST)):
        h[:INST] = near[at : at + INST]
        h[INST:] = far[at : at + INST]


def pass_kernel(place, near, far, got3, got4, out):
    at = pl.ds(INST, INST)
    out[:INST] = (near[at].astype(F32) + got3[:INST].astype(F32) + got4[...].astype(F32)).astype(BF16)
    out[INST:] = (far[at].astype(F32) + got3[INST:].astype(F32)).astype(BF16)


def cut_kernel(place, a, b, low, high):
    low[...] = (a[:CUT] + b[:CUT].astype(F32)).astype(BF16)
    high[...] = (a[CUT:] + b[CUT:].astype(F32)).astype(BF16)


def merge_kernel(place, a1, b1, a3, b3, low, high, t1, t3):
    t1[:CUT] = (a1[:CUT] + b1[:CUT].astype(F32) + low[...].astype(F32)).astype(BF16)
    t1[CUT:] = (a1[CUT:] + b1[CUT:].astype(F32)).astype(BF16)
    t3[:CUT] = (a3[:CUT] + b3[:CUT].astype(F32)).astype(BF16)
    t3[CUT:] = (a3[CUT:] + b3[CUT:].astype(F32) + high[...].astype(F32)).astype(BF16)


def split_kernel(place, a, b, t1, t3, own, top, p1, p2, p3, total):
    core, y = place[1], place[3]
    total[...] = (a[...].astype(F32) + b[...].astype(F32)) + (
        t1[...].astype(F32) + t3[...].astype(F32)
    )

    def piece(d):
        return total[pl.ds(pl.multiple_of(core * CL + lax.rem(y + d, NY) * 64, 16), 64)]

    own[...] = piece(0)
    cluster = total[pl.ds(pl.multiple_of((1 - core) * TOP, 16), CL)].astype(BF16)
    top[...] = cluster
    for d, p in ((1, p1), (2, p2), (3, p3)):
        p[:64] = piece(d).astype(BF16)
        p[64:] = cluster


def finish_kernel(place, own, top, g1, g2, g3, leaf, cluster):
    out = own[...] + g1[:64].astype(F32) + g2[:64].astype(F32) + g3[:64].astype(F32)
    for k in range(4):
        leaf[:, k, :] = out[k * CL : k * CL + CL]
    even = lax.rem(place[3], 2) == 0
    one, two, three = (g[64:].astype(F32) for g in (g1, g2, g3))
    near = jnp.where(even, three, one)
    far = jnp.where(even, one, three)
    cluster[...] = (top[...].astype(F32) + near) + (two + far)


def shards(e, cw, lw, inst, clus, counts, prefix, targets):
    iy, ic, iz, ix = (lax.axis_index(n) for n in ("y", "core", "z", "x"))
    place = jnp.stack([ix, ic, iz, iy]).astype(jnp.int32)

    with jax.named_scope("rows"):
        p0 = jnp.concatenate([e, swap(e)], axis=0)
        p1, p2 = turn(p0, "z", 1), turn(p0, "z", 2)
        p3, p4 = turn(p2, "z", 1), turn(p2[:INST], "z", 2)
        q1, q2, q3 = (swap(p[INST:]) for p in (p1, p2, p3))
        blocks = (e, p1, p2, p3, p4, q3, q2, q1)

    with jax.named_scope("weights"):
        leaf = lw.reshape(CL, NY, NC, 4, D).transpose(2, 1, 3, 0, 4).reshape(2, TOP, D)
        w = jnp.concatenate([leaf[0], cw, leaf[1]], axis=0)
        part = lax.dynamic_slice_in_dim(w, ic * TOP, PART, 0)
        low, high = shift(part, "x", 1), shift(part, "x", -1)
        low2, high2 = shift(low[:CUT], "x", 1), shift(high[CUT:], "x", -1)
        low_o, high_o, low2_o, high2_o = (swap(p) for p in (low, high, low2, high2))

    with jax.named_scope("slots"):
        counts, _ = lax.optimization_barrier((counts, p1))
        cap = prefix.shape[-1]
        owners = NZ * NX
        inst, clus = inst.reshape(owners, 1, cap), clus.reshape(owners, 1, cap)
        valid = jnp.arange(cap, dtype=jnp.int32)[None, None, :] < counts.reshape(owners, 1, 1)
        nothing = jnp.zeros((), BF16)
        alpha = jnp.where(valid, prefix.reshape(owners, 1, cap), nothing)
        want = targets.reshape(owners, cap, NY, NC, 4).transpose(0, 3, 2, 4, 1)
        want = jnp.where(valid, want.reshape(owners, KIDS, cap), nothing)
        side = jnp.concatenate([want, alpha, inst.astype(BF16), clus.astype(BF16)], axis=1)
        side = jnp.pad(side, ((0, 0), (0, 5), (0, 128 - cap))).reshape(NZ, NX, 40, 128)
        slots = lax.all_to_all(side, "z", 0, 0, tiled=True)
    (ay,) = call(
        slot_kernel, [((NX, WIDE, ROWS), F32)], (place, slots), [((WIDE, 512), BF16)]
    )

    wide, dzs = ((WIDE, D), BF16), ((WIDE, ROWS), BF16)
    half, half32 = ((PART, D), BF16), ((PART, D), F32)
    z = [((WIDE, ROWS), F32)]

    a2, b2, dz2, rows, w2 = call(
        owner_kernel,
        [half32, half, dzs, ((ROWS, D), BF16), wide],
        (place,) + blocks + (low2, high2, low2_o, high2_o, ay),
        z,
        r=2,
    )
    with jax.named_scope("weights_x"):
        down, up = call(
            cut_kernel, [((CUT, D), BF16), ((PART - CUT, D), BF16)], (place, a2, swap(b2))
        )
    outs = [half32, half, dzs, wide]
    a1, b1, dz1, w1 = call(owner_kernel, outs, (place, rows, low, low_o, ay), z, r=1)
    b1 = swap(b1)
    rows, down, up = lax.optimization_barrier((rows, down, up))
    down, up = shift(down, "x", -1), shift(up, "x", 1)
    a3, b3, dz3, w3 = call(owner_kernel, outs, (place, rows, high, high_o, ay), z, r=3)
    b3 = swap(b3)
    a0, b0, dz0 = call(owner_kernel, [half, half, dzs], (place, rows, w, ay), z, r=0)
    b0 = swap(b0)
    near, last, far, own = call(
        rows_kernel,
        [((3 * INST, D), BF16), ((INST, D), BF16), ((3 * INST, D), BF16), ((INST, D), F32)],
        (place, dz0, dz1, dz2, dz3, w, w1, w2, w3),
        [((ROWS, D), F32)],
    )

    with jax.named_scope("rows_back"):
        last = turn(last, "z", -2)
        far = swap(far)
        pair = ((2 * INST, D), BF16)
        h1, h3 = call(pack_kernel, [pair, pair], (place, near, far))
        h3, h1 = turn(h3, "z", -1), turn(h1, "z", -1)

    with jax.named_scope("weights_x"):
        down, a0 = lax.optimization_barrier((down, a0))
        t1, t3 = call(merge_kernel, [half, half], (place, a1, b1, a3, b3, down, up))
        t1, t3 = shift(t1, "x", -1), shift(t3, "x", 1)

    with jax.named_scope("rows_back"):
        (h2,) = call(pass_kernel, [pair], (place, near, far, h3, last))
        h2 = turn(h2, "z", -2)

    with jax.named_scope("weights_y"):
        send = ((80, D), BF16)
        mine, top, s1, s2, s3 = call(
            split_kernel,
            [((64, D), F32), ((CL, D), BF16), send, send, send],
            (place, a0, b0, t1, t3),
            [((PART, D), F32)],
        )
        g2, g1, g3 = shift(s2, "y", 2), shift(s1, "y", 1), shift(s3, "y", 3)

    with jax.named_scope("rows_back"):
        h2, g2 = lax.optimization_barrier((h2, g2))
        both = h1.astype(F32) + h2.astype(F32)
        grad_embed = (own + both[:INST]) + swap(both[INST:])

    with jax.named_scope("weights_y"):
        grad_leaf, grad_cluster = call(
            finish_kernel, [((CL, 4, D), F32), ((CL, D), F32)], (place, mine, top, g1, g2, g3)
        )
    return grad_embed, grad_cluster, grad_leaf


def solution(mesh):
    fine = Mesh(mesh.devices.reshape(NY, NC, NZ, NX), ("y", "core", "z", "x"))
    dp, label = ("y", "core"), ("z", "x")
    every = dp + label
    in_specs = (
        P(every, None),
        P(label, None),
        P(label, None, None),
        P(dp, label, None, None),
        P(dp, label, None, None),
        P(dp, label, None),
        P(dp, label, None, None),
        P(dp, label, None, None, None),
    )
    out_specs = (P(every, None), P(label, None), P(label, dp, None))
    return jax.shard_map(shards, mesh=fine, in_specs=in_specs, out_specs=out_specs, check_vma=False)
```

```python
import functools

import jax
import jax.numpy as jnp
from jax import lax
from jax.experimental import pallas as pl
from jax.experimental.pallas import tpu as pltpu
from jax.sharding import Mesh, PartitionSpec as P

BF16 = jnp.bfloat16
F32 = jnp.float32
NY, NC, NZ, NX = 4, 2, 8, 4
SIZE = {"y": NY, "core": NC, "z": NZ, "x": NX}
INST, D, KIDS, CL = 64, 768, 32, 16
ROWS = INST * NZ
WIDE = (KIDS + 1) * CL
TOP = 256
PART = 272
CUT = 144
ORDER = (0, 1, 7, 2, 6, 3, 4, 5)
ROW_AT = (0, 0, 0, 32, 0, 0, 32, 32)
SLOT_AT = (0, 64, 64, 256, 64, 64, 0, 0)
NT = (((1,), (1,)), ((), ()))
NN = (((1,), (0,)), ((), ()))
TN = (((0,), (0,)), ((), ()))
VMEM = pl.BlockSpec(memory_space=pltpu.VMEM)
SMEM = pl.BlockSpec(memory_space=pltpu.SMEM)


def dot(a, b, dims):
    return lax.dot_general(a, b, dims, preferred_element_type=F32)


def call(kernel, out, args, scratch=(), **static):
    return pl.pallas_call(
        functools.partial(kernel, **static),
        out_shape=tuple(jax.ShapeDtypeStruct(s, t) for s, t in out),
        in_specs=[SMEM] + [VMEM] * (len(args) - 1),
        out_specs=(VMEM,) * len(out),
        scratch_shapes=[pltpu.VMEM(s, t) for s, t in scratch],
        compiler_params=pltpu.CompilerParams(vmem_limit_bytes=16 * 1024 * 1024),
        cost_estimate=pl.CostEstimate(flops=2 * 10**9, bytes_accessed=1 << 20, transcendentals=0),
    )(*args)


def shift(x, axis, by):
    n = SIZE[axis]
    return lax.ppermute(x, axis, [(i, (i + by) % n) for i in range(n)])


def swap(x):
    return shift(x, "core", 1)


def turn(x, axis, by):
    n = SIZE[axis]
    pairs = [(i, (i + by) % n) for i in range(n)] + [(n + i, n + (i - by) % n) for i in range(n)]
    return lax.ppermute(x, ("core", axis), pairs)


def load_kernel(place, e, eo, want, want_o, side, side_o, m1, m2, s0):
    z, sign = place[2], 1 - 2 * place[1]

    def put(ref, lo, d, wants, sides):
        to = lax.rem(z + sign * d + NZ, NZ)
        for x in range(NX):
            ref[lo : lo + 32, x * 128 : x * 128 + 128] = wants[to, x]
        ref[lo : lo + 32, 512:640] = sides[to]
        ref[lo : lo + 32, 640:768] = jnp.zeros((32, 128), BF16)

    put(s0, 0, 0, want, side)
    m1[0:64], m1[96:160] = e[...], eo[...]
    put(m1, 64, 1, want, side)
    put(m1, 160, 1, want_o, side_o)
    m2[32:96], m2[160:224] = e[...], eo[...]
    put(m2, 0, 4, want, side)
    put(m2, 96, 3, want, side)
    put(m2, 128, 3, want_o, side_o)
    put(m2, 224, 2, want_o, side_o)
    put(m2, 256, 2, want, side)


def kid_row(k):
    core, y = k // 4 % NC, k // 8
    return core * (TOP + CL) + (y * 4 + k % 4) * CL


def slot_kernel(place, b0, b1, b2, b3, ay, wide, sides, *, offsets):
    x = place[0]
    lane_row = lax.broadcasted_iota(jnp.int32, (256, 128), 0)
    cluster_row = lax.broadcasted_iota(jnp.int32, (CL, 128), 0)
    blocks = (b0, b1, b2, b3)
    for q, (b, lo) in enumerate(zip(blocks, offsets)):
        sides[q] = b[lo : lo + 32, 512:640].astype(F32)

    def step(r, _):
        owner = lax.rem(x - r + NX, NX)
        left = []
        for q, (b, lo) in enumerate(zip(blocks, offsets)):
            want = b[lo : lo + 32, pl.ds(pl.multiple_of(owner * 128, 128), 128)].astype(F32)
            side = sides[q, pl.ds(pl.multiple_of(owner * 8, 8), 8)]
            alpha, inst, clus = side[0:1], side[1:2].astype(jnp.int32), side[2:3].astype(jnp.int32)
            left.append(jnp.where(lane_row == inst + q * INST, alpha, 0.0).astype(BF16))
            member = cluster_row == clus
            for k in range(KIDS + 1):
                at = TOP if k == KIDS else kid_row(k)
                row = alpha if k == KIDS else want[k : k + 1]
                wide[at : at + CL, q * 128 : q * 128 + 128] = jnp.where(member, row, 0.0).astype(BF16)
        ay[r] = dot(wide[...], jnp.concatenate(left, axis=1), NT)
        return 0

    lax.fori_loop(0, NX, step, 0)


def owner_kernel(place, *refs, r):
    core = place[1]
    mine = pl.ds(pl.multiple_of(core * TOP, 16), PART)
    other = pl.ds(pl.multiple_of((1 - core) * TOP, 16), PART)
    if r == 2:
        blocks, (n1, n2, f1, f2, ay1, ay2, a, b, dzs, e, w, z) = refs[:NZ], refs[NZ:]
        for d in range(NZ):
            lo = ROW_AT[d]
            e[d * INST : d * INST + INST] = blocks[d][lo : lo + INST]
        for at, p1, p2 in ((core, n1, n2), (1 - core, f1, f2)):
            w[pl.ds(pl.multiple_of(at * TOP, 16), CUT)] = p1[...]
            w[pl.ds(pl.multiple_of(at * TOP + CUT, 16), PART - CUT)] = p2[...]
    elif r == 0:
        e, w, ay1, ay2, a, b, dzs, z = refs
    else:
        e, near, far, ay1, ay2, a, b, dzs, w, z = refs
        w[mine] = near[...]
        w[other] = far[...]
    z[...] = dot(w[...], e[...], NT)
    top = pl.ds(TOP, CL)
    for ay, lanes in ((ay1, pl.ds(0, 256)), (ay2, pl.ds(256, 256))):
        s1 = jax.nn.sigmoid(z[top, lanes])
        s1a = s1 * ay[r, top]
        total = jnp.zeros((CL, 256), F32)
        for k in range(KIDS + 1):
            if k * CL == TOP:
                continue
            at = pl.ds(k * CL, CL)
            s2 = jax.nn.sigmoid(z[at, lanes])
            t = s2 * (s1a * s2 - ay[r, at])
            total = total + t
            dzs[at, lanes] = (s1 * (1.0 - s2) * t).astype(BF16)
        dzs[top, lanes] = (total * s1 * (1.0 - s1)).astype(BF16)
    b[...] = dot(dzs[other], e[...], NN).astype(BF16)
    a[...] = dot(dzs[mine], e[...], NN).astype(a.dtype)


def rows_kernel(place, *refs):
    dzs, ws, (near, last, far, own, ge) = refs[:NX], refs[NX : 2 * NX], refs[2 * NX :]
    ge[...] = dot(dzs[0][...], ws[0][...], TN)
    for r in range(1, NX):
        ge[...] += dot(dzs[r][...], ws[r][...], TN)
    def block(d):
        return ge[ORDER.index(d) * INST : ORDER.index(d) * INST + INST]

    own[...] = block(0)
    last[...] = block(4).astype(BF16)
    for i, d in enumerate((1, 2, 3)):
        near[i * INST : i * INST + INST] = block(d).astype(BF16)
        far[i * INST : i * INST + INST] = block(NZ - d).astype(BF16)


def pack_kernel(place, near, far, h1, h3):
    for h, at in ((h1, 0), (h3, 2 * INST)):
        h[:INST] = near[at : at + INST]
        h[INST:] = far[at : at + INST]


def pass_kernel(place, near, far, got3, got4, out):
    at = pl.ds(INST, INST)
    out[:INST] = (near[at].astype(F32) + got3[:INST].astype(F32) + got4[...].astype(F32)).astype(BF16)
    out[INST:] = (far[at].astype(F32) + got3[INST:].astype(F32)).astype(BF16)


def cut_kernel(place, a, b, low, high):
    low[...] = (a[:CUT] + b[:CUT].astype(F32)).astype(BF16)
    high[...] = (a[CUT:] + b[CUT:].astype(F32)).astype(BF16)


def merge_kernel(place, a1, b1, a3, b3, low, high, t1, t3):
    t1[:CUT] = (a1[:CUT] + b1[:CUT].astype(F32) + low[...].astype(F32)).astype(BF16)
    t1[CUT:] = (a1[CUT:] + b1[CUT:].astype(F32)).astype(BF16)
    t3[:CUT] = (a3[:CUT] + b3[:CUT].astype(F32)).astype(BF16)
    t3[CUT:] = (a3[CUT:] + b3[CUT:].astype(F32) + high[...].astype(F32)).astype(BF16)


def split_kernel(place, a, b, t1, t3, own, top, p1, p2, p3, total):
    core, y = place[1], place[3]
    total[...] = (a[...].astype(F32) + b[...].astype(F32)) + (
        t1[...].astype(F32) + t3[...].astype(F32)
    )

    def piece(d):
        return total[pl.ds(pl.multiple_of(core * CL + lax.rem(y + d, NY) * 64, 16), 64)]

    own[...] = piece(0)
    cluster = total[pl.ds(pl.multiple_of((1 - core) * TOP, 16), CL)].astype(BF16)
    top[...] = cluster
    for d, p in ((1, p1), (2, p2), (3, p3)):
        p[:64] = piece(d).astype(BF16)
        p[64:] = cluster


def finish_kernel(place, own, top, g1, g2, g3, leaf, cluster):
    out = own[...] + g1[:64].astype(F32) + g2[:64].astype(F32) + g3[:64].astype(F32)
    for k in range(4):
        leaf[:, k, :] = out[k * CL : k * CL + CL]
    even = lax.rem(place[3], 2) == 0
    one, two, three = (g[64:].astype(F32) for g in (g1, g2, g3))
    near = jnp.where(even, three, one)
    far = jnp.where(even, one, three)
    cluster[...] = (top[...].astype(F32) + near) + (two + far)


def shards(e, cw, lw, inst, clus, counts, prefix, targets):
    iy, ic, iz, ix = (lax.axis_index(n) for n in ("y", "core", "z", "x"))
    place = jnp.stack([ix, ic, iz, iy]).astype(jnp.int32)

    with jax.named_scope("weights"):
        leaf = lw.reshape(CL, NY, NC, 4, D).transpose(2, 1, 3, 0, 4).reshape(2, TOP, D)
        w = jnp.concatenate([leaf[0], cw, leaf[1]], axis=0)
        part = lax.dynamic_slice_in_dim(w, ic * TOP, PART, 0)
        low, high = shift(part, "x", 1), shift(part, "x", -1)
        low2, high2 = shift(low[:CUT], "x", 1), shift(high[CUT:], "x", -1)

    with jax.named_scope("slots"):
        cap = prefix.shape[-1]
        owners = NZ * NX
        inst, clus = inst.reshape(owners, 1, cap), clus.reshape(owners, 1, cap)
        valid = jnp.arange(cap, dtype=jnp.int32)[None, None, :] < counts.reshape(owners, 1, 1)
        nothing = jnp.zeros((), BF16)
        alpha = jnp.where(valid, prefix.reshape(owners, 1, cap), nothing)
        want = jnp.where(valid, jnp.swapaxes(targets.reshape(owners, cap, KIDS), 1, 2), nothing)
        want = jnp.pad(want, ((0, 0), (0, 0), (0, 128 - cap))).reshape(NZ, NX, KIDS, 128)
        side = jnp.concatenate([alpha, inst.astype(BF16), clus.astype(BF16)], axis=1)
        side = jnp.pad(side, ((0, 0), (0, 5), (0, 128 - cap))).reshape(NZ, NX * 8, 128)

    with jax.named_scope("rows"):
        m1, m2, s0 = call(
            load_kernel,
            [((192, D), BF16), ((288, D), BF16), ((32, D), BF16)],
            (place, e, swap(e), want, swap(want), side, swap(side)),
        )
        m2, m1 = turn(m2, "z", 2), turn(m1, "z", 1)
        m3, m4 = turn(m2[32:224], "z", 1), turn(m2[:96], "z", 2)
        q2, q1, q3 = swap(m2[160:256]), swap(m1[96:]), swap(m3[96:])
        low2, high2, m4 = lax.optimization_barrier((low2, high2, m4))
    with jax.named_scope("weights"):
        low_o, high_o, low2_o, high2_o = (swap(p) for p in (low, high, low2, high2))
    halves = []
    for blocks, at in (((s0, m1, q1, m2), SLOT_AT[:4]), ((q2, m3, m4, q3), SLOT_AT[4:])):
        halves += call(
            slot_kernel,
            [((NX, WIDE, 256), F32)],
            (place,) + blocks,
            [((WIDE, 512), BF16), ((4, 32, 128), F32)],
            offsets=at,
        )
    blocks, ay = (e, m1, q1, m2, q2, m3, m4, q3), tuple(halves)

    wide, dzs = ((WIDE, D), BF16), ((WIDE, ROWS), BF16)
    half, half32 = ((PART, D), BF16), ((PART, D), F32)
    z = [((WIDE, ROWS), F32)]

    a2, b2, dz2, rows, w2 = call(
        owner_kernel,
        [half32, half, dzs, ((ROWS, D), BF16), wide],
        (place,) + blocks + (low2, high2, low2_o, high2_o) + ay,
        z,
        r=2,
    )
    with jax.named_scope("weights_x"):
        down, up = call(
            cut_kernel, [((CUT, D), BF16), ((PART - CUT, D), BF16)], (place, a2, swap(b2))
        )
    outs = [half32, half, dzs, wide]
    a1, b1, dz1, w1 = call(owner_kernel, outs, (place, rows, low, low_o) + ay, z, r=1)
    b1 = swap(b1)
    rows, down, up = lax.optimization_barrier((rows, down, up))
    down, up = shift(down, "x", -1), shift(up, "x", 1)
    a3, b3, dz3, w3 = call(owner_kernel, outs, (place, rows, high, high_o) + ay, z, r=3)
    b3 = swap(b3)
    a0, b0, dz0 = call(owner_kernel, [half, half, dzs], (place, rows, w) + ay, z, r=0)
    b0 = swap(b0)
    near, last, far, own = call(
        rows_kernel,
        [((3 * INST, D), BF16), ((INST, D), BF16), ((3 * INST, D), BF16), ((INST, D), F32)],
        (place, dz0, dz1, dz2, dz3, w, w1, w2, w3),
        [((ROWS, D), F32)],
    )

    with jax.named_scope("rows_back"):
        last = turn(last, "z", -2)
        far = swap(far)
        pair = ((2 * INST, D), BF16)
        h1, h3 = call(pack_kernel, [pair, pair], (place, near, far))
        h3, h1 = turn(h3, "z", -1), turn(h1, "z", -1)

    with jax.named_scope("weights_x"):
        down, a0 = lax.optimization_barrier((down, a0))
        t1, t3 = call(merge_kernel, [half, half], (place, a1, b1, a3, b3, down, up))
        t1, t3 = shift(t1, "x", -1), shift(t3, "x", 1)

    with jax.named_scope("rows_back"):
        (h2,) = call(pass_kernel, [pair], (place, near, far, h3, last))
        h2 = turn(h2, "z", -2)

    with jax.named_scope("weights_y"):
        send = ((80, D), BF16)
        mine, top, s1, s2, s3 = call(
            split_kernel,
            [((64, D), F32), ((CL, D), BF16), send, send, send],
            (place, a0, b0, t1, t3),
            [((PART, D), F32)],
        )
        g2, g1, g3 = shift(s2, "y", 2), shift(s1, "y", 1), shift(s3, "y", 3)

    with jax.named_scope("rows_back"):
        h2, g2 = lax.optimization_barrier((h2, g2))
        both = h1.astype(F32) + h2.astype(F32)
        grad_embed = (own + both[:INST]) + swap(both[INST:])

    with jax.named_scope("weights_y"):
        grad_leaf, grad_cluster = call(
            finish_kernel, [((CL, 4, D), F32), ((CL, D), F32)], (place, mine, top, g1, g2, g3)
        )
    return grad_embed, grad_cluster, grad_leaf


def solution(mesh):
    fine = Mesh(mesh.devices.reshape(NY, NC, NZ, NX), ("y", "core", "z", "x"))
    dp, label = ("y", "core"), ("z", "x")
    every = dp + label
    in_specs = (
        P(every, None),
        P(label, None),
        P(label, None, None),
        P(dp, label, None, None),
        P(dp, label, None, None),
        P(dp, label, None),
        P(dp, label, None, None),
        P(dp, label, None, None, None),
    )
    out_specs = (P(every, None), P(label, None), P(label, dp, None))
    return jax.shard_map(shards, mesh=fine, in_specs=in_specs, out_specs=out_specs, check_vma=False)
```

```python
import functools

import jax
import jax.numpy as jnp
from jax import lax
from jax.experimental import pallas as pl
from jax.experimental.pallas import tpu as pltpu
from jax.sharding import Mesh, PartitionSpec as P

BF16 = jnp.bfloat16
F32 = jnp.float32
NY, NC, NZ, NX = 4, 2, 8, 4
SIZE = {"y": NY, "core": NC, "z": NZ, "x": NX}
INST, D, KIDS, CL = 64, 768, 32, 16
ROWS = INST * NZ
WIDE = (KIDS + 1) * CL
TOP = 256
PART = 272
CUT = 144
ORDER = (0, 1, 7, 4, 2, 6, 3, 5)
ROW_AT = (0, 0, 0, 32, 32, 0, 0, 32)
SLOT_AT = (0, 64, 64, 0, 256, 64, 64, 0)
NT = (((1,), (1,)), ((), ()))
NN = (((1,), (0,)), ((), ()))
TN = (((0,), (0,)), ((), ()))
VMEM = pl.BlockSpec(memory_space=pltpu.VMEM)
SMEM = pl.BlockSpec(memory_space=pltpu.SMEM)


def dot(a, b, dims):
    return lax.dot_general(a, b, dims, preferred_element_type=F32)


def call(kernel, out, args, scratch=(), **static):
    return pl.pallas_call(
        functools.partial(kernel, **static),
        out_shape=tuple(jax.ShapeDtypeStruct(s, t) for s, t in out),
        in_specs=[SMEM] + [VMEM] * (len(args) - 1),
        out_specs=(VMEM,) * len(out),
        scratch_shapes=[pltpu.VMEM(s, t) for s, t in scratch],
        compiler_params=pltpu.CompilerParams(vmem_limit_bytes=16 * 1024 * 1024),
        cost_estimate=pl.CostEstimate(flops=2 * 10**9, bytes_accessed=1 << 20, transcendentals=0),
    )(*args)


def shift(x, axis, by):
    n = SIZE[axis]
    return lax.ppermute(x, axis, [(i, (i + by) % n) for i in range(n)])


def swap(x):
    return shift(x, "core", 1)


def turn(x, axis, by):
    n = SIZE[axis]
    pairs = [(i, (i + by) % n) for i in range(n)] + [(n + i, n + (i - by) % n) for i in range(n)]
    return lax.ppermute(x, ("core", axis), pairs)


def side_kernel(counts, inst, clus, prefix, side, rows):
    rows[...] = jnp.zeros(rows.shape, F32)
    lane = lax.broadcasted_iota(jnp.int32, (1, inst.shape[1]), 1)
    for o in range(NZ * NX):
        alpha = jnp.where(lane < counts[o], prefix[o : o + 1].astype(F32), 0.0)
        rows[o * 8 : o * 8 + 1, : inst.shape[1]] = alpha
        rows[o * 8 + 1 : o * 8 + 2, : inst.shape[1]] = inst[o : o + 1].astype(F32)
        rows[o * 8 + 2 : o * 8 + 3, : inst.shape[1]] = clus[o : o + 1].astype(F32)
    for z in range(NZ):
        side[z] = rows[z * 32 : z * 32 + 32].astype(BF16)


def load_kernel(place, e, eo, want, want_o, side, side_o, m1, m2, s0):
    z, sign = place[2], 1 - 2 * place[1]

    def put(ref, lo, d, wants, sides):
        to = lax.rem(z + sign * d + NZ, NZ)
        ref[lo : lo + 32] = jnp.zeros((32, D), BF16)
        for x in range(NX):
            ref[lo : lo + 32, x * 128 : x * 128 + wants.shape[2]] = wants[to * NX + x]
        ref[lo : lo + 32, 512:640] = sides[to]

    put(s0, 0, 0, want, side)
    m1[0:64], m1[96:160] = e[...], eo[...]
    put(m1, 64, 1, want, side)
    put(m1, 160, 1, want_o, side_o)
    m2[32:96], m2[160:224] = e[...], eo[...]
    put(m2, 0, 4, want, side)
    put(m2, 96, 3, want, side)
    put(m2, 128, 3, want_o, side_o)
    put(m2, 224, 2, want_o, side_o)
    put(m2, 256, 2, want, side)


def kid_row(k):
    core, y = k // 4 % NC, k // 8
    return core * (TOP + CL) + (y * 4 + k % 4) * CL


def slot_kernel(place, b0, b1, b2, b3, ay, wide, sides, *, offsets):
    x = place[0]
    lane_row = lax.broadcasted_iota(jnp.int32, (256, 128), 0)
    cluster_row = lax.broadcasted_iota(jnp.int32, (CL, 128), 0)
    blocks = (b0, b1, b2, b3)
    for q, (b, lo) in enumerate(zip(blocks, offsets)):
        sides[q] = b[lo : lo + 32, 512:640].astype(F32)

    def step(r, _):
        owner = lax.rem(x - r + NX, NX)
        left = []
        for q, (b, lo) in enumerate(zip(blocks, offsets)):
            want = b[lo : lo + 32, pl.ds(pl.multiple_of(owner * 128, 128), 128)].astype(F32)
            side = sides[q, pl.ds(pl.multiple_of(owner * 8, 8), 8)]
            alpha, inst, clus = side[0:1], side[1:2].astype(jnp.int32), side[2:3].astype(jnp.int32)
            left.append(jnp.where(lane_row == inst + q * INST, alpha, 0.0).astype(BF16))
            member = cluster_row == clus
            for k in range(KIDS + 1):
                at = TOP if k == KIDS else kid_row(k)
                row = alpha if k == KIDS else want[k : k + 1]
                wide[at : at + CL, q * 128 : q * 128 + 128] = jnp.where(member, row, 0.0).astype(BF16)
        ay[r] = dot(wide[...], jnp.concatenate(left, axis=1), NT)
        return 0

    lax.fori_loop(0, NX, step, 0)


def owner_kernel(place, *refs, r):
    core = place[1]
    mine = pl.ds(pl.multiple_of(core * TOP, 16), PART)
    other = pl.ds(pl.multiple_of((1 - core) * TOP, 16), PART)
    if r == 2:
        blocks, (n1, n2, f1, f2, ay1, ay2, a, b, dzs, e, w, z) = refs[:NZ], refs[NZ:]
        for d in range(NZ):
            lo = ROW_AT[d]
            e[d * INST : d * INST + INST] = blocks[d][lo : lo + INST]
        for at, p1, p2 in ((core, n1, n2), (1 - core, f1, f2)):
            w[pl.ds(pl.multiple_of(at * TOP, 16), CUT)] = p1[...]
            w[pl.ds(pl.multiple_of(at * TOP + CUT, 16), PART - CUT)] = p2[...]
    elif r == 0:
        e, w, ay1, ay2, a, b, dzs, z = refs
    else:
        e, near, far, ay1, ay2, a, b, dzs, w, z = refs
        w[mine] = near[...]
        w[other] = far[...]
    z[...] = dot(w[...], e[...], NT)
    top = pl.ds(TOP, CL)
    for ay, lanes in ((ay1, pl.ds(0, 256)), (ay2, pl.ds(256, 256))):
        s1 = jax.nn.sigmoid(z[top, lanes])
        s1a = s1 * ay[r, top]
        total = jnp.zeros((CL, 256), F32)
        for k in range(KIDS + 1):
            if k * CL == TOP:
                continue
            at = pl.ds(k * CL, CL)
            s2 = jax.nn.sigmoid(z[at, lanes])
            t = s2 * (s1a * s2 - ay[r, at])
            total = total + t
            dzs[at, lanes] = (s1 * (1.0 - s2) * t).astype(BF16)
        dzs[top, lanes] = (total * s1 * (1.0 - s1)).astype(BF16)
    b[...] = dot(dzs[other], e[...], NN).astype(BF16)
    a[...] = dot(dzs[mine], e[...], NN).astype(a.dtype)


def rows_kernel(place, *refs):
    dzs, ws, (near, last, far, own, ge) = refs[:NX], refs[NX : 2 * NX], refs[2 * NX :]
    ge[...] = sum(dot(dzs[r][...], ws[r][...], TN) for r in range(NX))
    def block(d):
        return ge[ORDER.index(d) * INST : ORDER.index(d) * INST + INST]

    own[...] = block(0)
    last[...] = block(4).astype(BF16)
    for i, d in enumerate((1, 2, 3)):
        near[i * INST : i * INST + INST] = block(d).astype(BF16)
        far[i * INST : i * INST + INST] = block(NZ - d).astype(BF16)


def pack_kernel(place, near, last, far, h1, h2, h3):
    for h, at in ((h1, 0), (h2, INST), (h3, 2 * INST)):
        h[:INST] = near[at : at + INST]
        h[INST : 2 * INST] = far[at : at + INST]
    h3[2 * INST :] = last[...]


def cut_kernel(place, a, b, low, high):
    low[...] = (a[:CUT] + b[:CUT].astype(F32)).astype(BF16)
    high[...] = (a[CUT:] + b[CUT:].astype(F32)).astype(BF16)


def merge_kernel(place, a1, b1, a3, b3, low, high, t1, t3):
    t1[:CUT] = (a1[:CUT] + b1[:CUT].astype(F32) + low[...].astype(F32)).astype(BF16)
    t1[CUT:] = (a1[CUT:] + b1[CUT:].astype(F32)).astype(BF16)
    t3[:CUT] = (a3[:CUT] + b3[:CUT].astype(F32)).astype(BF16)
    t3[CUT:] = (a3[CUT:] + b3[CUT:].astype(F32) + high[...].astype(F32)).astype(BF16)


def split_kernel(place, a, b, t1, t3, own, top, p1, p2, p3, total):
    core, y = place[1], place[3]
    total[...] = (a[...].astype(F32) + b[...].astype(F32)) + (
        t1[...].astype(F32) + t3[...].astype(F32)
    )

    def piece(d):
        return total[pl.ds(pl.multiple_of(core * CL + lax.rem(y + d, NY) * 64, 16), 64)]

    own[...] = piece(0)
    cluster = total[pl.ds(pl.multiple_of((1 - core) * TOP, 16), CL)].astype(BF16)
    top[...] = cluster
    for d, p in ((1, p1), (2, p2), (3, p3)):
        p[:64] = piece(d).astype(BF16)
        p[64:] = cluster


def finish_kernel(place, own, top, g1, g2, g3, leaf, cluster):
    out = own[...] + g1[:64].astype(F32) + g2[:64].astype(F32) + g3[:64].astype(F32)
    for k in range(4):
        leaf[:, k, :] = out[k * CL : k * CL + CL]
    even = lax.rem(place[3], 2) == 0
    one, two, three = (g[64:].astype(F32) for g in (g1, g2, g3))
    near = jnp.where(even, three, one)
    far = jnp.where(even, one, three)
    cluster[...] = (top[...].astype(F32) + near) + (two + far)


def shards(e, cw, lw, inst, clus, counts, prefix, targets):
    iy, ic, iz, ix = (lax.axis_index(n) for n in ("y", "core", "z", "x"))
    place = jnp.stack([ix, ic, iz, iy]).astype(jnp.int32)

    with jax.named_scope("weights"):
        leaf = lw.reshape(CL, NY, NC, 4, D).transpose(2, 1, 3, 0, 4).reshape(2, TOP, D)
        w = jnp.concatenate([leaf[0], cw, leaf[1]], axis=0)
        part = lax.dynamic_slice_in_dim(w, ic * TOP, PART, 0)
        low, high = shift(part, "x", 1), shift(part, "x", -1)

    with jax.named_scope("slots"):
        cap = prefix.shape[-1]
        owners = NZ * NX
        want = jnp.swapaxes(targets.reshape(owners, cap, KIDS), 1, 2)
        (side,) = call(
            side_kernel,
            [((NZ, NX * 8, 128), BF16)],
            (counts.reshape(owners),)
            + tuple(v.reshape(owners, cap) for v in (inst, clus, prefix)),
            [((owners * 8, 128), F32)],
        )

    with jax.named_scope("rows"):
        m1, m2, s0 = call(
            load_kernel,
            [((192, D), BF16), ((288, D), BF16), ((32, D), BF16)],
            (place, e, swap(e), want, swap(want), side, swap(side)),
        )
        m2, m1 = turn(m2, "z", 2), turn(m1, "z", 1)
        m3, m4 = turn(m2[32:224], "z", 1), turn(m2[:96], "z", 2)
        q2, q1, q3 = swap(m2[160:256]), swap(m1[96:]), swap(m3[96:])

    def sum_slots(blocks, at):
        return call(
            slot_kernel,
            [((NX, WIDE, 256), F32)],
            (place,) + blocks,
            [((WIDE, 512), BF16), ((4, 32, 128), F32)],
            offsets=at,
        )[0]

    ay1 = sum_slots((s0, m1, q1, m4), SLOT_AT[:4])
    with jax.named_scope("weights"):
        near_low, near_high, _ = lax.optimization_barrier((low, high, m2))
        low2, high2 = shift(near_low[:CUT], "x", 1), shift(near_high[CUT:], "x", -1)
        low2, high2, ay1 = lax.optimization_barrier((low2, high2, ay1))
        low_o, high_o, low2_o, high2_o = (swap(p) for p in (low, high, low2, high2))
    ay2 = sum_slots((m2, q2, m3, q3), SLOT_AT[4:])
    blocks, ay = (e, m1, q1, m4, m2, q2, m3, q3), (ay1, ay2)

    wide, dzs = ((WIDE, D), BF16), ((WIDE, ROWS), BF16)
    half, half32 = ((PART, D), BF16), ((PART, D), F32)
    z = [((WIDE, ROWS), F32)]

    a2, b2, dz2, rows, w2 = call(
        owner_kernel,
        [half32, half, dzs, ((ROWS, D), BF16), wide],
        (place,) + blocks + (low2, high2, low2_o, high2_o) + ay,
        z,
        r=2,
    )
    with jax.named_scope("weights_x"):
        down, up = call(
            cut_kernel, [((CUT, D), BF16), ((PART - CUT, D), BF16)], (place, a2, swap(b2))
        )
    outs = [half32, half, dzs, wide]
    a1, b1, dz1, w1 = call(owner_kernel, outs, (place, rows, low, low_o) + ay, z, r=1)
    b1 = swap(b1)
    rows, down, up = lax.optimization_barrier((rows, down, up))
    down, up = shift(down, "x", -1), shift(up, "x", 1)
    a3, b3, dz3, w3 = call(owner_kernel, outs, (place, rows, high, high_o) + ay, z, r=3)
    b3 = swap(b3)
    a0, b0, dz0 = call(owner_kernel, [half, half, dzs], (place, rows, w) + ay, z, r=0)
    b0 = swap(b0)
    near, last, far, own = call(
        rows_kernel,
        [((3 * INST, D), BF16), ((INST, D), BF16), ((3 * INST, D), BF16), ((INST, D), F32)],
        (place, dz0, dz1, dz2, dz3, w, w1, w2, w3),
        [((ROWS, D), F32)],
    )

    with jax.named_scope("rows_back"):
        far = swap(far)

    with jax.named_scope("weights_x"):
        down, a0 = lax.optimization_barrier((down, a0))
        t1, t3 = call(merge_kernel, [half, half], (place, a1, b1, a3, b3, down, up))
        near, _ = lax.optimization_barrier((near, t1))
        t1, t3 = shift(t1, "x", -1), shift(t3, "x", 1)

    with jax.named_scope("rows_back"):
        pair = ((2 * INST, D), BF16)
        h1, h2, h3 = call(
            pack_kernel, [pair, pair, ((3 * INST, D), BF16)], (place, near, last, far)
        )
        h3, h2, h1 = turn(h3, "z", -3), turn(h2, "z", -2), turn(h1, "z", -1)

    with jax.named_scope("weights_y"):
        send = ((80, D), BF16)
        mine, top, s1, s2, s3 = call(
            split_kernel,
            [((64, D), F32), ((CL, D), BF16), send, send, send],
            (place, a0, b0, t1, t3),
            [((PART, D), F32)],
        )
        g2, g1, g3 = shift(s2, "y", 2), shift(s1, "y", 1), shift(s3, "y", 3)

    with jax.named_scope("rows_back"):
        h2, g2 = lax.optimization_barrier((h2, g2))
        last = turn(h3[2 * INST :], "z", -1)
        both = h1.astype(F32) + h2.astype(F32) + h3[: 2 * INST].astype(F32)
        grad_embed = (own + both[:INST] + last.astype(F32)) + swap(both[INST:])

    with jax.named_scope("weights_y"):
        grad_leaf, grad_cluster = call(
            finish_kernel, [((CL, 4, D), F32), ((CL, D), F32)], (place, mine, top, g1, g2, g3)
        )
    return grad_embed, grad_cluster, grad_leaf


def solution(mesh):
    fine = Mesh(mesh.devices.reshape(NY, NC, NZ, NX), ("y", "core", "z", "x"))
    dp, label = ("y", "core"), ("z", "x")
    every = dp + label
    in_specs = (
        P(every, None),
        P(label, None),
        P(label, None, None),
        P(dp, label, None, None),
        P(dp, label, None, None),
        P(dp, label, None),
        P(dp, label, None, None),
        P(dp, label, None, None, None),
    )
    out_specs = (P(every, None), P(label, None), P(label, dp, None))
    return jax.shard_map(shards, mesh=fine, in_specs=in_specs, out_specs=out_specs, check_vma=False)
```

```python
import functools

import jax
import jax.numpy as jnp
from jax import lax
from jax.experimental import pallas as pl
from jax.experimental.pallas import tpu as pltpu
from jax.sharding import Mesh, PartitionSpec as P

BF16 = jnp.bfloat16
F32 = jnp.float32
NY, NC, NZ, NX = 4, 2, 8, 4
SIZE = {"y": NY, "core": NC, "z": NZ, "x": NX}
INST, D, KIDS, CL = 64, 768, 32, 16
ROWS = INST * NZ
WIDE = (KIDS + 1) * CL
TOP = 256
PART = 272
CUT = 144
ORDER = (0, 1, 7, 2, 6, 3, 5, 4)
ROW_AT = (
    ((0, 0, 64),),
    ((1, 0, 64),),
    ((2, 0, 64),),
    ((3, 16, 64),),
    ((4, 48, 32), (4, 16, 32)),
    ((5, 0, 64),),
    ((6, 32, 32), (6, 0, 32)),
    ((7, 16, 32), (8, 16, 32)),
)
SLOT_AT = (
    (((0, 0, 32),), ((1, 64, 32),), ((2, 64, 32),), ((3, 112, 32),)),
    (((0, 112, 32),), ((1, 64, 32),), ((2, 64, 32),), ((3, 0, 16), (4, 0, 16))),
)
NT = (((1,), (1,)), ((), ()))
NN = (((1,), (0,)), ((), ()))
TN = (((0,), (0,)), ((), ()))
VMEM = pl.BlockSpec(memory_space=pltpu.VMEM)
SMEM = pl.BlockSpec(memory_space=pltpu.SMEM)


def dot(a, b, dims):
    return lax.dot_general(a, b, dims, preferred_element_type=F32)


def call(kernel, out, args, scratch=(), own=0, **static):
    specs = [SMEM] + [VMEM] * (len(args) - 1 - own)
    specs += [pl.BlockSpec(memory_space=pltpu.HBM)] * own
    return pl.pallas_call(
        functools.partial(kernel, **static),
        out_shape=tuple(jax.ShapeDtypeStruct(s, t) for s, t in out),
        in_specs=specs,
        out_specs=(VMEM,) * len(out),
        scratch_shapes=[s if t is None else pltpu.VMEM(s, t) for s, t in scratch],
        compiler_params=pltpu.CompilerParams(vmem_limit_bytes=16 * 1024 * 1024),
        cost_estimate=pl.CostEstimate(flops=2 * 10**9, bytes_accessed=1 << 20, transcendentals=0),
    )(*args)


def shift(x, axis, by):
    n = SIZE[axis]
    return lax.ppermute(x, axis, [(i, (i + by) % n) for i in range(n)])


def swap(x):
    return shift(x, "core", 1)


def turn(x, axis, by):
    n = SIZE[axis]
    pairs = [(i, (i + by) % n) for i in range(n)] + [(n + i, n + (i - by) % n) for i in range(n)]
    return lax.ppermute(x, ("core", axis), pairs)


def prepare_kernel(place, lw, cw, w, part, raw, top, kids, sems):
    copies = [
        pltpu.make_async_copy(lw, raw, sems.at[0]),
        pltpu.make_async_copy(cw, top, sems.at[1]),
    ]
    for c in copies:
        c.start()
    for c in copies:
        c.wait()
    for c in range(CL):
        for j in range(D // 128):
            kids[j, pl.ds(c, KIDS, stride=CL)] = raw[c, :, j * 128 : j * 128 + 128].astype(F32)
    for y in range(NY):
        for core in range(NC):
            to, at = core * PART + y * 64, (y * NC + core) * 64
            for j in range(D // 128):
                w[to : to + 64, j * 128 : j * 128 + 128] = kids[j, at : at + 64].astype(BF16)
    w[TOP : TOP + CL] = top[...]
    part[...] = w[pl.ds(pl.multiple_of(place[1] * TOP, 16), PART)]


def load_kernel(place, counts, inst, clus, prefix, e, want, *refs):
    (up1, dn1, up2, dn2, s0), (n, i, c, a, ev, wv, rows, side, sems) = refs[:5], refs[5:]
    pairs = ((counts, n), (inst, i), (clus, c), (prefix, a), (e, ev), (want, wv))
    copies = [pltpu.make_async_copy(x, v, sems.at[k]) for k, (x, v) in enumerate(pairs)]
    for copy in copies:
        copy.start()
    for copy in copies:
        copy.wait()
    cap = inst.shape[1]
    rows[...] = jnp.zeros(rows.shape, F32)
    lane = lax.broadcasted_iota(jnp.int32, (1, cap), 1)
    for o in range(NZ * NX):
        alpha = jnp.where(lane < n[o], a[o : o + 1].astype(F32), 0.0)
        rows[o * 8 : o * 8 + 1, :cap] = alpha
        rows[o * 8 + 1 : o * 8 + 2, :cap] = i[o : o + 1].astype(F32)
        rows[o * 8 + 2 : o * 8 + 3, :cap] = c[o : o + 1].astype(F32)
    for z in range(NZ):
        side[z] = rows[z * 32 : z * 32 + 32].astype(BF16)

    def put(ref, lo, d, first=0, count=32):
        to = lax.rem(place[2] + d + NZ, NZ)
        ref[lo : lo + count] = jnp.zeros((count, D), BF16)
        for x in range(NX):
            ref[lo : lo + count, x * 128 : x * 128 + cap] = wv[to * NX + x, first : first + count]
        ref[lo : lo + count, 512:640] = side[to, first : first + count]

    put(s0, 0, 0)
    for ref1, ref2, by, half in ((up1, up2, 1, 0), (dn1, dn2, -1, 1)):
        ref1[0:64] = ev[...]
        put(ref1, 64, by)
        put(ref2, 0, 4, 16 * half, 16)
        ref2[16:48] = ev[half * 32 : half * 32 + 32]
        ref2[48:80] = ev[32 - half * 32 : 64 - half * 32]
        put(ref2, 80, 3 * by)
        put(ref2, 112, 2 * by)


def kid_row(k):
    core, y = k // 4 % NC, k // 8
    return core * (TOP + CL) + (y * 4 + k % 4) * CL


def slot_kernel(place, *refs, spots):
    blocks, (ay, wide, wants, sides) = refs[:-4], refs[-4:]
    x = place[0]
    lane_row = lax.broadcasted_iota(jnp.int32, (256, 128), 0)
    cluster_row = lax.broadcasted_iota(jnp.int32, (CL, 128), 0)
    for q in range(4):
        to = 0
        for ref, lo, n in spots[q]:
            sides[q, to : to + n] = blocks[ref][lo : lo + n, 512:640].astype(F32)
            wants[q, to : to + n] = blocks[ref][lo : lo + n, :512].astype(F32)
            to += n

    def step(r, _):
        owner = lax.rem(x - r + NX, NX)
        left = []
        for q in range(4):
            want = wants[q, :, pl.ds(pl.multiple_of(owner * 128, 128), 128)]
            side = sides[q, pl.ds(pl.multiple_of(owner * 8, 8), 8)]
            alpha, inst, clus = side[0:1], side[1:2].astype(jnp.int32), side[2:3].astype(jnp.int32)
            left.append(jnp.where(lane_row == inst + q * INST, alpha, 0.0).astype(BF16))
            member = cluster_row == clus
            for k in range(KIDS + 1):
                at = TOP if k == KIDS else kid_row(k)
                row = alpha if k == KIDS else want[k : k + 1]
                wide[at : at + CL, q * 128 : q * 128 + 128] = jnp.where(member, row, 0.0).astype(BF16)
        ay[r] = dot(wide[...], jnp.concatenate(left, axis=1), NT)
        return 0

    lax.fori_loop(0, NX, step, 0)


def owner_kernel(place, *refs, r):
    core = place[1]
    mine = pl.ds(pl.multiple_of(core * TOP, 16), PART)
    other = pl.ds(pl.multiple_of((1 - core) * TOP, 16), PART)
    if r == 2:
        blocks, (n1, n2, f1, f2, ay1, ay2, a, b, dzs, e, w, z) = refs[:9], refs[9:]
        for d in range(NZ):
            to = d * INST
            for ref, lo, n in ROW_AT[d]:
                e[to : to + n] = blocks[ref][lo : lo + n]
                to += n
        for at, p1, p2 in ((core, n1, n2), (1 - core, f1, f2)):
            w[pl.ds(pl.multiple_of(at * TOP, 16), CUT)] = p1[...]
            w[pl.ds(pl.multiple_of(at * TOP + CUT, 16), PART - CUT)] = p2[...]
    elif r == 0:
        e, w, ay1, ay2, a, b, dzs, z = refs
    else:
        e, near, far, ay1, ay2, a, b, dzs, w, z = refs
        w[mine] = near[...]
        w[other] = far[...]
    z[...] = dot(w[...], e[...], NT)
    top = pl.ds(TOP, CL)
    for ay, lanes in ((ay1, pl.ds(0, 256)), (ay2, pl.ds(256, 256))):
        s1 = jax.nn.sigmoid(z[top, lanes])
        s1a = s1 * ay[r, top]
        total = jnp.zeros((CL, 256), F32)
        for k in range(KIDS + 1):
            if k * CL == TOP:
                continue
            at = pl.ds(k * CL, CL)
            s2 = jax.nn.sigmoid(z[at, lanes])
            t = s2 * (s1a * s2 - ay[r, at])
            total = total + t
            dzs[at, lanes] = (s1 * (1.0 - s2) * t).astype(BF16)
        dzs[top, lanes] = (total * s1 * (1.0 - s1)).astype(BF16)
    b[...] = dot(dzs[other], e[...], NN).astype(BF16)
    a[...] = dot(dzs[mine], e[...], NN).astype(a.dtype)


def rows_kernel(place, *refs):
    dzs, ws, (near, last, far, own, ge) = refs[:NX], refs[NX : 2 * NX], refs[2 * NX :]
    ge[...] = sum(dot(dzs[r][...], ws[r][...], TN) for r in range(NX))

    def block(d):
        at = jnp.where(place[1] == 0, ORDER.index(d), ORDER.index(-d % NZ))
        return ge[pl.ds(pl.multiple_of(at * INST, INST), INST)]

    own[...] = block(0)
    last[...] = block(4).astype(BF16)
    for i, d in enumerate((1, 2, 3)):
        near[i * INST : i * INST + INST] = block(d).astype(BF16)
        far[i * INST : i * INST + INST] = block(NZ - d).astype(BF16)


def pack_kernel(place, near, far, h1, h3):
    for h, at in ((h1, 0), (h3, 2 * INST)):
        h[:INST] = near[at : at + INST]
        h[INST:] = far[at : at + INST]


def pass_kernel(place, near, far, got3, got4, out):
    at = pl.ds(INST, INST)
    out[:INST] = (near[at].astype(F32) + got3[:INST].astype(F32) + got4[...].astype(F32)).astype(BF16)
    out[INST:] = (far[at].astype(F32) + got3[INST:].astype(F32)).astype(BF16)


def cut_kernel(place, a, b, low, high):
    low[...] = (a[:CUT] + b[:CUT].astype(F32)).astype(BF16)
    high[...] = (a[CUT:] + b[CUT:].astype(F32)).astype(BF16)


def merge_kernel(place, a1, b1, a3, b3, low, high, t1, t3):
    t1[:CUT] = (a1[:CUT] + b1[:CUT].astype(F32) + low[...].astype(F32)).astype(BF16)
    t1[CUT:] = (a1[CUT:] + b1[CUT:].astype(F32)).astype(BF16)
    t3[:CUT] = (a3[:CUT] + b3[:CUT].astype(F32)).astype(BF16)
    t3[CUT:] = (a3[CUT:] + b3[CUT:].astype(F32) + high[...].astype(F32)).astype(BF16)


def split_kernel(place, a, b, t1, t3, own, top, p1, p2, p3, total):
    core, y = place[1], place[3]
    total[...] = (a[...].astype(F32) + b[...].astype(F32)) + (
        t1[...].astype(F32) + t3[...].astype(F32)
    )

    def piece(d):
        return total[pl.ds(pl.multiple_of(core * CL + lax.rem(y + d, NY) * 64, 16), 64)]

    own[...] = piece(0)
    cluster = total[pl.ds(pl.multiple_of((1 - core) * TOP, 16), CL)].astype(BF16)
    top[...] = cluster
    for d, p in ((1, p1), (2, p2), (3, p3)):
        p[:64] = piece(d).astype(BF16)
        p[64:] = cluster


def finish_kernel(place, own, top, g1, g2, g3, leaf, cluster):
    out = own[...] + g1[:64].astype(F32) + g2[:64].astype(F32) + g3[:64].astype(F32)
    for k in range(4):
        leaf[:, k, :] = out[k * CL : k * CL + CL]
    even = lax.rem(place[3], 2) == 0
    one, two, three = (g[64:].astype(F32) for g in (g1, g2, g3))
    near = jnp.where(even, three, one)
    far = jnp.where(even, one, three)
    cluster[...] = (top[...].astype(F32) + near) + (two + far)


def shards(e, cw, lw, inst, clus, counts, prefix, targets):
    iy, ic, iz, ix = (lax.axis_index(n) for n in ("y", "core", "z", "x"))
    place = jnp.stack([ix, ic, iz, iy]).astype(jnp.int32)

    with jax.named_scope("weights"):
        w, part = call(
            prepare_kernel,
            [((WIDE, D), BF16), ((PART, D), BF16)],
            (place, lw, cw),
            [
                ((CL, KIDS, D), BF16),
                ((CL, D), BF16),
                ((D // 128, KIDS * CL, 128), F32),
                (pltpu.SemaphoreType.DMA((2,)), None),
            ],
            own=2,
        )
        low, high = shift(part, "x", 1), shift(part, "x", -1)

    with jax.named_scope("rows"):
        cap = prefix.shape[-1]
        owners = NZ * NX
        want = jnp.swapaxes(targets.reshape(owners, cap, KIDS), 1, 2)
        flat = tuple(v.reshape(owners, cap) for v in (inst, clus, prefix))
        up1, dn1, up2, dn2, s0 = call(
            load_kernel,
            [((n, D), BF16) for n in (96, 96, 144, 144, 32)],
            (place, counts.reshape(owners)) + flat + (e, want),
            [
                (pltpu.SMEM((owners,), jnp.int32), None),
                ((owners, cap), jnp.int32),
                ((owners, cap), jnp.int32),
                ((owners, cap), BF16),
                ((INST, D), BF16),
                ((owners, KIDS, cap), BF16),
                ((owners * 8, 128), F32),
                ((NZ, 32, 128), BF16),
                (pltpu.SemaphoreType.DMA((6,)), None),
            ],
            own=6,
        )
        up2, dn2 = shift(up2, "z", 2), shift(dn2, "z", -2)
        up1, dn1 = shift(up1, "z", 1), shift(dn1, "z", -1)
        up3, dn3 = shift(up2[16:112], "z", 1), shift(dn2[16:112], "z", -1)
        up4, dn4 = shift(up2[:48], "z", 2), shift(dn2[:48], "z", -2)

    def sum_slots(blocks, spots):
        return call(
            slot_kernel,
            [((NX, WIDE, 256), F32)],
            (place,) + blocks,
            [((WIDE, 512), BF16), ((4, 32, 512), F32), ((4, 32, 128), F32)],
            spots=spots,
        )[0]

    ay1 = sum_slots((s0, up1, dn1, up2), SLOT_AT[0])
    with jax.named_scope("weights"):
        low2, high2 = shift(low[:CUT], "x", 1), shift(high[CUT:], "x", -1)
        low2, high2, up4, dn4, ay1 = lax.optimization_barrier((low2, high2, up4, dn4, ay1))
        low_o, high_o, low2_o, high2_o = (swap(p) for p in (low, high, low2, high2))
    ay2 = sum_slots((dn2, up3, dn3, up4, dn4), SLOT_AT[1])
    blocks, ay = (e, up1, dn1, up2, dn2, up3, dn3, up4, dn4), (ay1, ay2)

    wide, dzs = ((WIDE, D), BF16), ((WIDE, ROWS), BF16)
    half, half32 = ((PART, D), BF16), ((PART, D), F32)
    z = [((WIDE, ROWS), F32)]

    a2, b2, dz2, rows, w2 = call(
        owner_kernel,
        [half32, half, dzs, ((ROWS, D), BF16), wide],
        (place,) + blocks + (low2, high2, low2_o, high2_o) + ay,
        z,
        r=2,
    )
    with jax.named_scope("weights_x"):
        down, up = call(
            cut_kernel, [((CUT, D), BF16), ((PART - CUT, D), BF16)], (place, a2, swap(b2))
        )
    outs = [half32, half, dzs, wide]
    a1, b1, dz1, w1 = call(owner_kernel, outs, (place, rows, low, low_o) + ay, z, r=1)
    b1 = swap(b1)
    rows, down, up = lax.optimization_barrier((rows, down, up))
    down, up = shift(down, "x", -1), shift(up, "x", 1)
    a3, b3, dz3, w3 = call(owner_kernel, outs, (place, rows, high, high_o) + ay, z, r=3)
    b3 = swap(b3)
    a0, b0, dz0 = call(owner_kernel, [half, half, dzs], (place, rows, w) + ay, z, r=0)
    b0 = swap(b0)
    near, last, far, own = call(
        rows_kernel,
        [((3 * INST, D), BF16), ((INST, D), BF16), ((3 * INST, D), BF16), ((INST, D), F32)],
        (place, dz0, dz1, dz2, dz3, w, w1, w2, w3),
        [((ROWS, D), F32)],
    )

    with jax.named_scope("rows_back"):
        last = turn(last, "z", -2)
        far = swap(far)
        pair = ((2 * INST, D), BF16)
        h1, h3 = call(pack_kernel, [pair, pair], (place, near, far))
        h3, h1 = turn(h3, "z", -1), turn(h1, "z", -1)

    with jax.named_scope("weights_x"):
        down, a0 = lax.optimization_barrier((down, a0))
        t1, t3 = call(merge_kernel, [half, half], (place, a1, b1, a3, b3, down, up))
        t1, t3 = shift(t1, "x", -1), shift(t3, "x", 1)

    with jax.named_scope("rows_back"):
        (h2,) = call(pass_kernel, [pair], (place, near, far, h3, last))
        h2 = turn(h2, "z", -2)

    with jax.named_scope("weights_y"):
        send = ((80, D), BF16)
        mine, top, s1, s2, s3 = call(
            split_kernel,
            [((64, D), F32), ((CL, D), BF16), send, send, send],
            (place, a0, b0, t1, t3),
            [((PART, D), F32)],
        )
        g2, g1, g3 = shift(s2, "y", 2), shift(s1, "y", 1), shift(s3, "y", 3)

    with jax.named_scope("rows_back"):
        h2, g2 = lax.optimization_barrier((h2, g2))
        both = h1.astype(F32) + h2.astype(F32)
        grad_embed = (own + both[:INST]) + swap(both[INST:])

    with jax.named_scope("weights_y"):
        grad_leaf, grad_cluster = call(
            finish_kernel, [((CL, 4, D), F32), ((CL, D), F32)], (place, mine, top, g1, g2, g3)
        )
    return grad_embed, grad_cluster, grad_leaf


def solution(mesh):
    fine = Mesh(mesh.devices.reshape(NY, NC, NZ, NX), ("y", "core", "z", "x"))
    dp, label = ("y", "core"), ("z", "x")
    every = dp + label
    in_specs = (
        P(every, None),
        P(label, None),
        P(label, None, None),
        P(dp, label, None, None),
        P(dp, label, None, None),
        P(dp, label, None),
        P(dp, label, None, None),
        P(dp, label, None, None, None),
    )
    out_specs = (P(every, None), P(label, None), P(label, dp, None))
    return jax.shard_map(shards, mesh=fine, in_specs=in_specs, out_specs=out_specs, check_vma=False)
```

```python
import functools

import jax
import jax.numpy as jnp
from jax import lax
from jax.experimental import pallas as pl
from jax.experimental.pallas import tpu as pltpu
from jax.sharding import Mesh, PartitionSpec as P

BF16 = jnp.bfloat16
F32 = jnp.float32
NY, NC, NZ, NX = 4, 2, 8, 4
SIZE = {"y": NY, "core": NC, "z": NZ, "x": NX}
INST, D, KIDS, CL = 64, 768, 32, 16
ROWS = INST * NZ
WIDE = (KIDS + 1) * CL
TOP = 256
PART = 272
CUT = 144
ORDER = (0, 1, 7, 2, 6, 3, 5, 4)
ROW_AT = (
    ((0, 0, 64),),
    ((1, 0, 64),),
    ((2, 0, 64),),
    ((3, 16, 64),),
    ((4, 48, 32), (4, 16, 32)),
    ((5, 0, 64),),
    ((6, 32, 32), (6, 0, 32)),
    ((7, 16, 32), (8, 16, 32)),
)
SLOT_AT = (
    (((0, 0, 32),), ((1, 64, 32),), ((2, 64, 32),), ((3, 112, 32),)),
    (((0, 112, 32),), ((1, 64, 32),), ((2, 64, 32),), ((3, 0, 16), (4, 0, 16))),
)
NT = (((1,), (1,)), ((), ()))
NN = (((1,), (0,)), ((), ()))
TN = (((0,), (0,)), ((), ()))
VMEM = pl.BlockSpec(memory_space=pltpu.VMEM)
SMEM = pl.BlockSpec(memory_space=pltpu.SMEM)


def dot(a, b, dims):
    return lax.dot_general(a, b, dims, preferred_element_type=F32)


def call(kernel, out, args, scratch=(), own=0, **static):
    specs = [SMEM] + [VMEM] * (len(args) - 1 - own)
    specs += [pl.BlockSpec(memory_space=pltpu.HBM)] * own
    return pl.pallas_call(
        functools.partial(kernel, **static),
        out_shape=tuple(jax.ShapeDtypeStruct(s, t) for s, t in out),
        in_specs=specs,
        out_specs=(VMEM,) * len(out),
        scratch_shapes=[s if t is None else pltpu.VMEM(s, t) for s, t in scratch],
        compiler_params=pltpu.CompilerParams(vmem_limit_bytes=16 * 1024 * 1024),
        cost_estimate=pl.CostEstimate(flops=2 * 10**9, bytes_accessed=1 << 20, transcendentals=0),
    )(*args)


def shift(x, axis, by):
    n = SIZE[axis]
    return lax.ppermute(x, axis, [(i, (i + by) % n) for i in range(n)])


def swap(x):
    return shift(x, "core", 1)


def turn(x, axis, by):
    n = SIZE[axis]
    pairs = [(i, (i + by) % n) for i in range(n)] + [(n + i, n + (i - by) % n) for i in range(n)]
    return lax.ppermute(x, ("core", axis), pairs)


def prepare_kernel(place, lw, cw, w, part, raw, top, kids, sems):
    copies = [
        pltpu.make_async_copy(lw, raw, sems.at[0]),
        pltpu.make_async_copy(cw, top, sems.at[1]),
    ]
    for c in copies:
        c.start()
    for c in copies:
        c.wait()
    for c in range(CL):
        for j in range(D // 128):
            kids[j, pl.ds(c, KIDS, stride=CL)] = raw[c, :, j * 128 : j * 128 + 128].astype(F32)
    for y in range(NY):
        for core in range(NC):
            to, at = core * PART + y * 64, (y * NC + core) * 64
            for j in range(D // 128):
                w[to : to + 64, j * 128 : j * 128 + 128] = kids[j, at : at + 64].astype(BF16)
    w[TOP : TOP + CL] = top[...]
    part[...] = w[pl.ds(pl.multiple_of(place[1] * TOP, 16), PART)]


def load_kernel(place, counts, inst, clus, prefix, e, want, *refs):
    (up1, dn1, up2, dn2, s0), (n, i, c, a, ev, wv, rows, side, sems) = refs[:5], refs[5:]
    pairs = ((counts, n), (inst, i), (clus, c), (prefix, a), (e, ev), (want, wv))
    copies = [pltpu.make_async_copy(x, v, sems.at[k]) for k, (x, v) in enumerate(pairs)]
    for copy in copies:
        copy.start()
    for copy in copies:
        copy.wait()
    cap = inst.shape[1]
    rows[...] = jnp.zeros(rows.shape, F32)
    lane = lax.broadcasted_iota(jnp.int32, (1, cap), 1)
    for o in range(NZ * NX):
        alpha = jnp.where(lane < n[o], a[o : o + 1].astype(F32), 0.0)
        rows[o * 8 : o * 8 + 1, :cap] = alpha
        rows[o * 8 + 1 : o * 8 + 2, :cap] = i[o : o + 1].astype(F32)
        rows[o * 8 + 2 : o * 8 + 3, :cap] = c[o : o + 1].astype(F32)
    for z in range(NZ):
        side[z] = rows[z * 32 : z * 32 + 32].astype(BF16)

    def put(ref, lo, d, first=0, count=32):
        to = lax.rem(place[2] + d + NZ, NZ)
        ref[lo : lo + count] = jnp.zeros((count, D), BF16)
        for x in range(NX):
            ref[lo : lo + count, x * 128 : x * 128 + cap] = wv[to * NX + x, first : first + count]
        ref[lo : lo + count, 512:640] = side[to, first : first + count]

    put(s0, 0, 0)
    for ref1, ref2, by, half in ((up1, up2, 1, 0), (dn1, dn2, -1, 1)):
        ref1[0:64] = ev[...]
        put(ref1, 64, by)
        put(ref2, 0, 4, 16 * half, 16)
        ref2[16:48] = ev[half * 32 : half * 32 + 32]
        ref2[48:80] = ev[32 - half * 32 : 64 - half * 32]
        put(ref2, 80, 3 * by)
        put(ref2, 112, 2 * by)


def kid_row(k):
    core, y = k // 4 % NC, k // 8
    return core * (TOP + CL) + (y * 4 + k % 4) * CL


def slot_kernel(place, *refs, spots):
    blocks, (ay, wide, wants, sides) = refs[:-4], refs[-4:]
    x = place[0]
    lane_row = lax.broadcasted_iota(jnp.int32, (256, 128), 0)
    cluster_row = lax.broadcasted_iota(jnp.int32, (CL, 128), 0)
    for q in range(4):
        to = 0
        for ref, lo, n in spots[q]:
            sides[q, to : to + n] = blocks[ref][lo : lo + n, 512:640].astype(F32)
            wants[q, to : to + n] = blocks[ref][lo : lo + n, :512].astype(F32)
            to += n

    def step(r, _):
        owner = lax.rem(x - r + NX, NX)
        left = []
        for q in range(4):
            want = wants[q, :, pl.ds(pl.multiple_of(owner * 128, 128), 128)]
            side = sides[q, pl.ds(pl.multiple_of(owner * 8, 8), 8)]
            alpha, inst, clus = side[0:1], side[1:2].astype(jnp.int32), side[2:3].astype(jnp.int32)
            left.append(jnp.where(lane_row == inst + q * INST, alpha, 0.0).astype(BF16))
            member = cluster_row == clus
            for k in range(KIDS + 1):
                at = TOP if k == KIDS else kid_row(k)
                row = alpha if k == KIDS else want[k : k + 1]
                wide[at : at + CL, q * 128 : q * 128 + 128] = jnp.where(member, row, 0.0).astype(BF16)
        ay[r] = dot(wide[...], jnp.concatenate(left, axis=1), NT)
        return 0

    lax.fori_loop(0, NX, step, 0)


def owner_kernel(place, *refs, r):
    core = place[1]
    mine = pl.ds(pl.multiple_of(core * TOP, 16), PART)
    other = pl.ds(pl.multiple_of((1 - core) * TOP, 16), PART)
    if r == 2:
        blocks, (n1, n2, f1, f2, ay1, ay2, a, b, dzs, e, w, z) = refs[:9], refs[9:]
        for d in range(NZ):
            to = d * INST
            for ref, lo, n in ROW_AT[d]:
                e[to : to + n] = blocks[ref][lo : lo + n]
                to += n
        for at, p1, p2 in ((core, n1, n2), (1 - core, f1, f2)):
            w[pl.ds(pl.multiple_of(at * TOP, 16), CUT)] = p1[...]
            w[pl.ds(pl.multiple_of(at * TOP + CUT, 16), PART - CUT)] = p2[...]
    elif r == 0:
        e, w, ay1, ay2, a, b, dzs, z = refs
    else:
        e, near, far, ay1, ay2, a, b, dzs, w, z = refs
        w[mine] = near[...]
        w[other] = far[...]
    z[...] = dot(w[...], e[...], NT)
    top = pl.ds(TOP, CL)
    for ay, lanes in ((ay1, pl.ds(0, 256)), (ay2, pl.ds(256, 256))):
        s1 = jax.nn.sigmoid(z[top, lanes])
        s1a = s1 * ay[r, top]
        total = jnp.zeros((CL, 256), F32)
        for k in range(KIDS + 1):
            if k * CL == TOP:
                continue
            at = pl.ds(k * CL, CL)
            s2 = jax.nn.sigmoid(z[at, lanes])
            t = s2 * (s1a * s2 - ay[r, at])
            total = total + t
            dzs[at, lanes] = (s1 * (1.0 - s2) * t).astype(BF16)
        dzs[top, lanes] = (total * s1 * (1.0 - s1)).astype(BF16)
    b[...] = dot(dzs[other], e[...], NN).astype(BF16)
    a[...] = dot(dzs[mine], e[...], NN).astype(a.dtype)


def rows_kernel(place, *refs):
    dzs, ws, (near, last, far, own, ge) = refs[:NX], refs[NX : 2 * NX], refs[2 * NX :]
    ge[...] = sum(dot(dzs[r][...], ws[r][...], TN) for r in range(NX))

    def block(d):
        at = jnp.where(place[1] == 0, ORDER.index(d), ORDER.index(-d % NZ))
        return ge[pl.ds(pl.multiple_of(at * INST, INST), INST)]

    own[...] = block(0)
    last[...] = block(4).astype(BF16)
    for i, d in enumerate((1, 2, 3)):
        near[i * INST : i * INST + INST] = block(d).astype(BF16)
        far[i * INST : i * INST + INST] = block(NZ - d).astype(BF16)


def pack_kernel(place, near, far, h1, h3):
    for h, at in ((h1, 0), (h3, 2 * INST)):
        h[:INST] = near[at : at + INST]
        h[INST:] = far[at : at + INST]


def pass_kernel(place, near, far, got3, got4, out):
    at = pl.ds(INST, INST)
    out[:INST] = (near[at].astype(F32) + got3[:INST].astype(F32) + got4[...].astype(F32)).astype(BF16)
    out[INST:] = (far[at].astype(F32) + got3[INST:].astype(F32)).astype(BF16)


def cut_kernel(place, a, b, low, high):
    low[...] = (a[:CUT] + b[:CUT].astype(F32)).astype(BF16)
    high[...] = (a[CUT:] + b[CUT:].astype(F32)).astype(BF16)


def merge_kernel(place, a1, b1, a3, b3, low, high, t1, t3):
    t1[:CUT] = (a1[:CUT] + b1[:CUT].astype(F32) + low[...].astype(F32)).astype(BF16)
    t1[CUT:] = (a1[CUT:] + b1[CUT:].astype(F32)).astype(BF16)
    t3[:CUT] = (a3[:CUT] + b3[:CUT].astype(F32)).astype(BF16)
    t3[CUT:] = (a3[CUT:] + b3[CUT:].astype(F32) + high[...].astype(F32)).astype(BF16)


def split_kernel(place, a, b, t1, t3, own, top, p1, p2, p3, total):
    core, y = place[1], place[3]
    total[...] = (a[...].astype(F32) + b[...].astype(F32)) + (
        t1[...].astype(F32) + t3[...].astype(F32)
    )

    def piece(d):
        return total[pl.ds(pl.multiple_of(core * CL + lax.rem(y + d, NY) * 64, 16), 64)]

    own[...] = piece(0)
    cluster = total[pl.ds(pl.multiple_of((1 - core) * TOP, 16), CL)].astype(BF16)
    top[...] = cluster
    for d, p in ((1, p1), (2, p2), (3, p3)):
        p[:64] = piece(d).astype(BF16)
        p[64:] = cluster


def finish_kernel(place, own, top, g1, g2, g3, leaf, cluster):
    out = own[...] + g1[:64].astype(F32) + g2[:64].astype(F32) + g3[:64].astype(F32)
    for k in range(4):
        leaf[:, k, :] = out[k * CL : k * CL + CL]
    even = lax.rem(place[3], 2) == 0
    one, two, three = (g[64:].astype(F32) for g in (g1, g2, g3))
    near = jnp.where(even, three, one)
    far = jnp.where(even, one, three)
    cluster[...] = (top[...].astype(F32) + near) + (two + far)


def shards(e, cw, lw, inst, clus, counts, prefix, targets):
    iy, ic, iz, ix = (lax.axis_index(n) for n in ("y", "core", "z", "x"))
    place = jnp.stack([ix, ic, iz, iy]).astype(jnp.int32)

    with jax.named_scope("weights"):
        w, part = call(
            prepare_kernel,
            [((WIDE, D), BF16), ((PART, D), BF16)],
            (place, lw, cw),
            [
                ((CL, KIDS, D), BF16),
                ((CL, D), BF16),
                ((D // 128, KIDS * CL, 128), F32),
                (pltpu.SemaphoreType.DMA((2,)), None),
            ],
            own=2,
        )
        low, high = shift(part, "x", 1), shift(part, "x", -1)
        low2, high2 = shift(low[:CUT], "x", 1), shift(high[CUT:], "x", -1)

    with jax.named_scope("rows"):
        cap = prefix.shape[-1]
        owners = NZ * NX
        want = jnp.swapaxes(targets.reshape(owners, cap, KIDS), 1, 2)
        flat = tuple(v.reshape(owners, cap) for v in (inst, clus, prefix))
        up1, dn1, up2, dn2, s0 = call(
            load_kernel,
            [((n, D), BF16) for n in (96, 96, 144, 144, 32)],
            (place, counts.reshape(owners)) + flat + (e, want),
            [
                (pltpu.SMEM((owners,), jnp.int32), None),
                ((owners, cap), jnp.int32),
                ((owners, cap), jnp.int32),
                ((owners, cap), BF16),
                ((INST, D), BF16),
                ((owners, KIDS, cap), BF16),
                ((owners * 8, 128), F32),
                ((NZ, 32, 128), BF16),
                (pltpu.SemaphoreType.DMA((6,)), None),
            ],
            own=6,
        )
        up2, dn2 = shift(up2, "z", 2), shift(dn2, "z", -2)
        up1, dn1 = shift(up1, "z", 1), shift(dn1, "z", -1)
        low2, high2, up2, dn2 = lax.optimization_barrier((low2, high2, up2, dn2))
        up3, dn3 = shift(up2[16:112], "z", 1), shift(dn2[16:112], "z", -1)
        up4, dn4 = shift(up2[:48], "z", 2), shift(dn2[:48], "z", -2)

    def sum_slots(blocks, spots):
        return call(
            slot_kernel,
            [((NX, WIDE, 256), F32)],
            (place,) + blocks,
            [((WIDE, 512), BF16), ((4, 32, 512), F32), ((4, 32, 128), F32)],
            spots=spots,
        )[0]

    ay1 = sum_slots((s0, up1, dn1, up2), SLOT_AT[0])
    with jax.named_scope("weights"):
        low2, high2, up4, dn4, ay1 = lax.optimization_barrier((low2, high2, up4, dn4, ay1))
        low_o, high_o, low2_o, high2_o = (swap(p) for p in (low, high, low2, high2))
    ay2 = sum_slots((dn2, up3, dn3, up4, dn4), SLOT_AT[1])
    blocks, ay = (e, up1, dn1, up2, dn2, up3, dn3, up4, dn4), (ay1, ay2)

    wide, dzs = ((WIDE, D), BF16), ((WIDE, ROWS), BF16)
    half, half32 = ((PART, D), BF16), ((PART, D), F32)
    z = [((WIDE, ROWS), F32)]

    a2, b2, dz2, rows, w2 = call(
        owner_kernel,
        [half32, half, dzs, ((ROWS, D), BF16), wide],
        (place,) + blocks + (low2, high2, low2_o, high2_o) + ay,
        z,
        r=2,
    )
    with jax.named_scope("weights_x"):
        down, up = call(
            cut_kernel, [((CUT, D), BF16), ((PART - CUT, D), BF16)], (place, a2, swap(b2))
        )
    outs = [half32, half, dzs, wide]
    a1, b1, dz1, w1 = call(owner_kernel, outs, (place, rows, low, low_o) + ay, z, r=1)
    b1 = swap(b1)
    rows, down, up = lax.optimization_barrier((rows, down, up))
    down, up = shift(down, "x", -1), shift(up, "x", 1)
    a3, b3, dz3, w3 = call(owner_kernel, outs, (place, rows, high, high_o) + ay, z, r=3)
    b3 = swap(b3)
    a0, b0, dz0 = call(owner_kernel, [half, half, dzs], (place, rows, w) + ay, z, r=0)
    b0 = swap(b0)
    near, last, far, own = call(
        rows_kernel,
        [((3 * INST, D), BF16), ((INST, D), BF16), ((3 * INST, D), BF16), ((INST, D), F32)],
        (place, dz0, dz1, dz2, dz3, w, w1, w2, w3),
        [((ROWS, D), F32)],
    )

    with jax.named_scope("rows_back"):
        last = turn(last, "z", -2)
        far = swap(far)
        pair = ((2 * INST, D), BF16)
        h1, h3 = call(pack_kernel, [pair, pair], (place, near, far))
        h3, h1 = turn(h3, "z", -1), turn(h1, "z", -1)

    with jax.named_scope("weights_x"):
        down, a0 = lax.optimization_barrier((down, a0))
        t1, t3 = call(merge_kernel, [half, half], (place, a1, b1, a3, b3, down, up))
        t1, t3 = shift(t1, "x", -1), shift(t3, "x", 1)

    with jax.named_scope("rows_back"):
        (h2,) = call(pass_kernel, [pair], (place, near, far, h3, last))
        h2 = turn(h2, "z", -2)

    with jax.named_scope("weights_y"):
        send = ((80, D), BF16)
        mine, top, s1, s2, s3 = call(
            split_kernel,
            [((64, D), F32), ((CL, D), BF16), send, send, send],
            (place, a0, b0, t1, t3),
            [((PART, D), F32)],
        )
        g2, g1, g3 = shift(s2, "y", 2), shift(s1, "y", 1), shift(s3, "y", 3)

    with jax.named_scope("rows_back"):
        h2, g2 = lax.optimization_barrier((h2, g2))
        both = h1.astype(F32) + h2.astype(F32)
        grad_embed = (own + both[:INST]) + swap(both[INST:])

    with jax.named_scope("weights_y"):
        grad_leaf, grad_cluster = call(
            finish_kernel, [((CL, 4, D), F32), ((CL, D), F32)], (place, mine, top, g1, g2, g3)
        )
    return grad_embed, grad_cluster, grad_leaf


def solution(mesh):
    fine = Mesh(mesh.devices.reshape(NY, NC, NZ, NX), ("y", "core", "z", "x"))
    dp, label = ("y", "core"), ("z", "x")
    every = dp + label
    in_specs = (
        P(every, None),
        P(label, None),
        P(label, None, None),
        P(dp, label, None, None),
        P(dp, label, None, None),
        P(dp, label, None),
        P(dp, label, None, None),
        P(dp, label, None, None, None),
    )
    out_specs = (P(every, None), P(label, None), P(label, dp, None))
    return jax.shard_map(shards, mesh=fine, in_specs=in_specs, out_specs=out_specs, check_vma=False)
```

```python
import functools

import jax
import jax.numpy as jnp
from jax import lax
from jax.experimental import pallas as pl
from jax.experimental.pallas import tpu as pltpu
from jax.sharding import Mesh, PartitionSpec as P

BF16 = jnp.bfloat16
F32 = jnp.float32
NY, NC, NZ, NX = 4, 2, 8, 4
SIZE = {"y": NY, "core": NC, "z": NZ, "x": NX}
INST, D, KIDS, CL = 64, 768, 32, 16
ROWS = INST * NZ
WIDE = (KIDS + 1) * CL
TOP = 256
PART = 272
CUT = 144
ORDER = (0, 1, 7, 2, 6, 3, 5, 4)
ROW_AT = (
    ((0, 0, 64),),
    ((1, 0, 64),),
    ((2, 0, 64),),
    ((3, 16, 64),),
    ((4, 48, 32), (4, 16, 32)),
    ((5, 0, 64),),
    ((6, 32, 32), (6, 0, 32)),
    ((7, 16, 32), (8, 16, 32)),
)
SLOT_AT = (
    (((0, 0, 32),), ((1, 64, 32),), ((2, 64, 32),), ((3, 112, 32),)),
    (((0, 112, 32),), ((1, 64, 32),), ((2, 64, 32),), ((3, 0, 16), (4, 0, 16))),
)
NT = (((1,), (1,)), ((), ()))
NN = (((1,), (0,)), ((), ()))
TN = (((0,), (0,)), ((), ()))
VMEM = pl.BlockSpec(memory_space=pltpu.VMEM)
SMEM = pl.BlockSpec(memory_space=pltpu.SMEM)


def dot(a, b, dims):
    return lax.dot_general(a, b, dims, preferred_element_type=F32)


def call(kernel, out, args, scratch=(), own=0, **static):
    specs = [SMEM] + [VMEM] * (len(args) - 1 - own)
    specs += [pl.BlockSpec(memory_space=pltpu.HBM)] * own
    return pl.pallas_call(
        functools.partial(kernel, **static),
        out_shape=tuple(jax.ShapeDtypeStruct(s, t) for s, t in out),
        in_specs=specs,
        out_specs=(VMEM,) * len(out),
        scratch_shapes=[s if t is None else pltpu.VMEM(s, t) for s, t in scratch],
        compiler_params=pltpu.CompilerParams(vmem_limit_bytes=18 * 1024 * 1024),
        cost_estimate=pl.CostEstimate(flops=2 * 10**9, bytes_accessed=1 << 20, transcendentals=0),
    )(*args)


def shift(x, axis, by):
    n = SIZE[axis]
    return lax.ppermute(x, axis, [(i, (i + by) % n) for i in range(n)])


def swap(x):
    return shift(x, "core", 1)


def turn(x, axis, by):
    n = SIZE[axis]
    pairs = [(i, (i + by) % n) for i in range(n)] + [(n + i, n + (i - by) % n) for i in range(n)]
    return lax.ppermute(x, ("core", axis), pairs)


def prepare_kernel(place, counts, inst, clus, prefix, e, want, lw, cw, *refs):
    (w, part, up1, dn1, up2, dn2, s0), refs = refs[:7], refs[7:]
    n, i, c, a, ev, wv, raw, top, kids, rows, side, sems = refs
    pairs = ((counts, n), (inst, i), (clus, c), (prefix, a), (e, ev), (want, wv), (lw, raw), (cw, top))
    copies = [pltpu.make_async_copy(x, v, sems.at[k]) for k, (x, v) in enumerate(pairs)]
    for copy in copies:
        copy.start()
    for copy in copies:
        copy.wait()
    for k in range(CL):
        for j in range(D // 128):
            kids[j, pl.ds(k, KIDS, stride=CL)] = raw[k, :, j * 128 : j * 128 + 128].astype(F32)
    for y in range(NY):
        for core in range(NC):
            to, at = core * PART + y * 64, (y * NC + core) * 64
            for j in range(D // 128):
                w[to : to + 64, j * 128 : j * 128 + 128] = kids[j, at : at + 64].astype(BF16)
    w[TOP : TOP + CL] = top[...]
    part[...] = w[pl.ds(pl.multiple_of(place[1] * TOP, 16), PART)]
    cap = inst.shape[1]
    rows[...] = jnp.zeros(rows.shape, F32)
    lane = lax.broadcasted_iota(jnp.int32, (1, cap), 1)
    for o in range(NZ * NX):
        alpha = jnp.where(lane < n[o], a[o : o + 1].astype(F32), 0.0)
        rows[o * 8 : o * 8 + 1, :cap] = alpha
        rows[o * 8 + 1 : o * 8 + 2, :cap] = i[o : o + 1].astype(F32)
        rows[o * 8 + 2 : o * 8 + 3, :cap] = c[o : o + 1].astype(F32)
    for z in range(NZ):
        side[z] = rows[z * 32 : z * 32 + 32].astype(BF16)

    def put(ref, lo, d, first=0, count=32):
        to = lax.rem(place[2] + d + NZ, NZ)
        ref[lo : lo + count] = jnp.zeros((count, D), BF16)
        for x in range(NX):
            ref[lo : lo + count, x * 128 : x * 128 + cap] = wv[to * NX + x, first : first + count]
        ref[lo : lo + count, 512:640] = side[to, first : first + count]

    put(s0, 0, 0)
    for ref1, ref2, by, half in ((up1, up2, 1, 0), (dn1, dn2, -1, 1)):
        ref1[0:64] = ev[...]
        put(ref1, 64, by)
        put(ref2, 0, 4, 16 * half, 16)
        ref2[16:48] = ev[half * 32 : half * 32 + 32]
        ref2[48:80] = ev[32 - half * 32 : 64 - half * 32]
        put(ref2, 80, 3 * by)
        put(ref2, 112, 2 * by)


def kid_row(k):
    core, y = k // 4 % NC, k // 8
    return core * (TOP + CL) + (y * 4 + k % 4) * CL


def slot_kernel(place, *refs, spots):
    blocks, (ay, wide, wants, sides) = refs[:-4], refs[-4:]
    x = place[0]
    lane_row = lax.broadcasted_iota(jnp.int32, (256, 128), 0)
    cluster_row = lax.broadcasted_iota(jnp.int32, (CL, 128), 0)
    for q in range(4):
        to = 0
        for ref, lo, n in spots[q]:
            sides[q, to : to + n] = blocks[ref][lo : lo + n, 512:640].astype(F32)
            wants[q, to : to + n] = blocks[ref][lo : lo + n, :512].astype(F32)
            to += n

    def step(r, _):
        owner = lax.rem(x - r + NX, NX)
        left = []
        for q in range(4):
            want = wants[q, :, pl.ds(pl.multiple_of(owner * 128, 128), 128)]
            side = sides[q, pl.ds(pl.multiple_of(owner * 8, 8), 8)]
            alpha, inst, clus = side[0:1], side[1:2].astype(jnp.int32), side[2:3].astype(jnp.int32)
            left.append(jnp.where(lane_row == inst + q * INST, alpha, 0.0).astype(BF16))
            member = cluster_row == clus
            for k in range(KIDS + 1):
                at = TOP if k == KIDS else kid_row(k)
                row = alpha if k == KIDS else want[k : k + 1]
                wide[at : at + CL, q * 128 : q * 128 + 128] = jnp.where(member, row, 0.0).astype(BF16)
        ay[r] = dot(wide[...], jnp.concatenate(left, axis=1), NT)
        return 0

    lax.fori_loop(0, NX, step, 0)


def owner_terms(r, e, w, ay1, ay2, dzs, z):
    top = pl.ds(TOP, CL)
    halves = ((ay1, pl.ds(0, 256)), (ay2, pl.ds(256, 256)))
    for (ay, lanes), zh in zip(halves, z):
        zh[...] = dot(w[...], e[lanes], NT)
    for (ay, lanes), zh in zip(halves, z):
        s1 = jax.nn.sigmoid(zh[top])
        s1a = s1 * ay[r, top]
        total = jnp.zeros((CL, 256), F32)
        for k in range(KIDS + 1):
            if k * CL == TOP:
                continue
            at = pl.ds(k * CL, CL)
            s2 = jax.nn.sigmoid(zh[at])
            t = s2 * (s1a * s2 - ay[r, at])
            total = total + t
            dzs[at, lanes] = (s1 * (1.0 - s2) * t).astype(BF16)
        dzs[top, lanes] = (total * s1 * (1.0 - s1)).astype(BF16)


def weight_terms(core, e, dzs, a, b):
    mine = pl.ds(pl.multiple_of(core * TOP, 16), PART)
    other = pl.ds(pl.multiple_of((1 - core) * TOP, 16), PART)
    b[...] = dot(dzs[other], e[...], NN).astype(BF16)
    a[...] = dot(dzs[mine], e[...], NN).astype(a.dtype)


def across_kernel(place, *refs):
    blocks, (n1, n2, f1, f2, ay1, ay2, a, b, dzs, e, w), z = refs[:9], refs[9:20], refs[20:]
    for d in range(NZ):
        to = d * INST
        for ref, lo, n in ROW_AT[d]:
            e[to : to + n] = blocks[ref][lo : lo + n]
            to += n
    core = place[1]
    for at, p1, p2 in ((core, n1, n2), (1 - core, f1, f2)):
        w[pl.ds(pl.multiple_of(at * TOP, 16), CUT)] = p1[...]
        w[pl.ds(pl.multiple_of(at * TOP + CUT, 16), PART - CUT)] = p2[...]
    owner_terms(2, e, w, ay1, ay2, dzs, z)
    weight_terms(core, e, dzs, a, b)


def beside_kernel(place, e, n1, f1, n3, f3, ay1, ay2, a1, a3, b, dz1, dz3, w1, w3, *z):
    core = place[1]
    for r, near, far, a, lo, dzs, w in ((1, n1, f1, a1, 0, dz1, w1), (3, n3, f3, a3, PART, dz3, w3)):
        w[pl.ds(pl.multiple_of(core * TOP, 16), PART)] = near[...]
        w[pl.ds(pl.multiple_of((1 - core) * TOP, 16), PART)] = far[...]
        owner_terms(r, e, w, ay1, ay2, dzs, z)
        weight_terms(core, e, dzs, a, b.at[pl.ds(lo, PART)])


def own_kernel(place, e, w, ay1, ay2, dz1, dz2, dz3, w1, w2, w3, a, b, near, last, far, own, *refs):
    z, dz0, ge = refs[:2], refs[2], refs[3]
    owner_terms(0, e, w, ay1, ay2, dz0, z)
    weight_terms(place[1], e, dz0, a, b)
    rows_kernel(place, dz0, dz1, dz2, dz3, w, w1, w2, w3, near, last, far, own, ge)


def rows_kernel(place, *refs):
    dzs, ws, (near, last, far, own, ge) = refs[:NX], refs[NX : 2 * NX], refs[2 * NX :]
    kids = (pl.ds(0, TOP), pl.ds(TOP + CL, TOP))
    tops = [jnp.concatenate([v[TOP : TOP + CL] for v in vs], axis=0) for vs in (dzs, ws)]
    ge[...] = dot(*tops, TN) + sum(dot(dzs[r][k], ws[r][k], TN) for r in range(NX) for k in kids)

    def block(d):
        at = jnp.where(place[1] == 0, ORDER.index(d), ORDER.index(-d % NZ))
        return ge[pl.ds(pl.multiple_of(at * INST, INST), INST)]

    own[...] = block(0)
    last[...] = block(4).astype(BF16)
    for i, d in enumerate((1, 2, 3)):
        near[i * INST : i * INST + INST] = block(d).astype(BF16)
        far[i * INST : i * INST + INST] = block(NZ - d).astype(BF16)


def pack_kernel(place, near, far, h1, h3):
    for h, at in ((h1, 0), (h3, 2 * INST)):
        h[:INST] = near[at : at + INST]
        h[INST:] = far[at : at + INST]


def pass_kernel(place, near, far, got3, got4, out):
    at = pl.ds(INST, INST)
    out[:INST] = (near[at].astype(F32) + got3[:INST].astype(F32) + got4[...].astype(F32)).astype(BF16)
    out[INST:] = (far[at].astype(F32) + got3[INST:].astype(F32)).astype(BF16)


def cut_kernel(place, a, b, low, high):
    low[...] = (a[:CUT] + b[:CUT].astype(F32)).astype(BF16)
    high[...] = (a[CUT:] + b[CUT:].astype(F32)).astype(BF16)


def merge_kernel(place, a1, a3, b, low, high, t1, t3):
    b1, b3 = b.at[pl.ds(0, PART)], b.at[pl.ds(PART, PART)]
    t1[:CUT] = (a1[:CUT] + b1[:CUT].astype(F32) + low[...].astype(F32)).astype(BF16)
    t1[CUT:] = (a1[CUT:] + b1[CUT:].astype(F32)).astype(BF16)
    t3[:CUT] = (a3[:CUT] + b3[:CUT].astype(F32)).astype(BF16)
    t3[CUT:] = (a3[CUT:] + b3[CUT:].astype(F32) + high[...].astype(F32)).astype(BF16)


def split_kernel(place, a, b, t1, t3, own, top, p1, p2, p3, total):
    core, y = place[1], place[3]
    total[...] = (a[...].astype(F32) + b[...].astype(F32)) + (
        t1[...].astype(F32) + t3[...].astype(F32)
    )

    def piece(d):
        return total[pl.ds(pl.multiple_of(core * CL + lax.rem(y + d, NY) * 64, 16), 64)]

    own[...] = piece(0)
    cluster = total[pl.ds(pl.multiple_of((1 - core) * TOP, 16), CL)].astype(BF16)
    top[...] = cluster
    for d, p in ((1, p1), (2, p2), (3, p3)):
        p[:64] = piece(d).astype(BF16)
        p[64:] = cluster


def finish_kernel(place, own, top, g1, g2, g3, leaf, cluster):
    out = own[...] + g1[:64].astype(F32) + g2[:64].astype(F32) + g3[:64].astype(F32)
    for k in range(4):
        leaf[:, k, :] = out[k * CL : k * CL + CL]
    even = lax.rem(place[3], 2) == 0
    one, two, three = (g[64:].astype(F32) for g in (g1, g2, g3))
    near = jnp.where(even, three, one)
    far = jnp.where(even, one, three)
    cluster[...] = (top[...].astype(F32) + near) + (two + far)


def shards(e, cw, lw, inst, clus, counts, prefix, targets):
    iy, ic, iz, ix = (lax.axis_index(n) for n in ("y", "core", "z", "x"))
    place = jnp.stack([ix, ic, iz, iy]).astype(jnp.int32)

    cap = prefix.shape[-1]
    owners = NZ * NX
    want = jnp.swapaxes(targets.reshape(owners, cap, KIDS), 1, 2)
    flat = tuple(v.reshape(owners, cap) for v in (inst, clus, prefix))
    w, part, up1, dn1, up2, dn2, s0 = call(
        prepare_kernel,
        [((n, D), BF16) for n in (WIDE, PART, 96, 96, 144, 144, 32)],
        (place, counts.reshape(owners)) + flat + (e, want, lw, cw),
        [
            (pltpu.SMEM((owners,), jnp.int32), None),
            ((owners, cap), jnp.int32),
            ((owners, cap), jnp.int32),
            ((owners, cap), BF16),
            ((INST, D), BF16),
            ((owners, KIDS, cap), BF16),
            ((CL, KIDS, D), BF16),
            ((CL, D), BF16),
            ((D // 128, KIDS * CL, 128), F32),
            ((owners * 8, 128), F32),
            ((NZ, 32, 128), BF16),
            (pltpu.SemaphoreType.DMA((8,)), None),
        ],
        own=8,
    )
    with jax.named_scope("weights"):
        low, high = shift(part, "x", 1), shift(part, "x", -1)
        low2, high2 = shift(low[:CUT], "x", 1), shift(high[CUT:], "x", -1)

    with jax.named_scope("rows"):
        up2, dn2 = shift(up2, "z", 2), shift(dn2, "z", -2)
        up1, dn1 = shift(up1, "z", 1), shift(dn1, "z", -1)
        low2, high2, up2, dn2 = lax.optimization_barrier((low2, high2, up2, dn2))
        up3, dn3 = shift(up2[16:112], "z", 1), shift(dn2[16:112], "z", -1)
        up4, dn4 = shift(up2[:48], "z", 2), shift(dn2[:48], "z", -2)

    def sum_slots(blocks, spots):
        return call(
            slot_kernel,
            [((NX, WIDE, 256), F32)],
            (place,) + blocks,
            [((WIDE, 512), BF16), ((4, 32, 512), F32), ((4, 32, 128), F32)],
            spots=spots,
        )[0]

    ay1 = sum_slots((s0, up1, dn1, up2), SLOT_AT[0])
    with jax.named_scope("weights"):
        low2, high2, up4, dn4, ay1 = lax.optimization_barrier((low2, high2, up4, dn4, ay1))
        low_o, high_o, low2_o, high2_o = (swap(p) for p in (low, high, low2, high2))
    ay2 = sum_slots((dn2, up3, dn3, up4, dn4), SLOT_AT[1])
    wide, dzs = ((WIDE, D), BF16), ((WIDE, ROWS), BF16)
    half, half32 = ((PART, D), BF16), ((PART, D), F32)
    z = [((WIDE, 256), F32)] * 2

    a2, b2, dz2, rows, w2 = call(
        across_kernel,
        [half32, half, dzs, ((ROWS, D), BF16), wide],
        (place, e, up1, dn1, up2, dn2, up3, dn3, up4, dn4, low2, high2, low2_o, high2_o, ay1, ay2),
        z,
    )
    with jax.named_scope("weights_x"):
        down, up = call(
            cut_kernel, [((CUT, D), BF16), ((PART - CUT, D), BF16)], (place, a2, swap(b2))
        )
    a1, a3, b13, dz1, dz3, w1, w3 = call(
        beside_kernel,
        [half32, half32, ((2 * PART, D), BF16), dzs, dzs, wide, wide],
        (place, rows, low, low_o, high, high_o, ay1, ay2),
        z,
    )
    b13 = swap(b13)
    rows, down, up = lax.optimization_barrier((rows, down, up))
    down, up = shift(down, "x", -1), shift(up, "x", 1)
    block = ((INST, D), BF16)
    three = ((3 * INST, D), BF16)
    a0, b0, near, last, far, own = call(
        own_kernel,
        [half, half, three, block, three, ((INST, D), F32)],
        (place, rows, w, ay1, ay2, dz1, dz2, dz3, w1, w2, w3),
        z + [dzs, ((ROWS, D), F32)],
    )
    b0 = swap(b0)

    with jax.named_scope("rows_back"):
        last = turn(last, "z", -2)
        far = swap(far)
        pair = ((2 * INST, D), BF16)
        h1, h3 = call(pack_kernel, [pair, pair], (place, near, far))
        h3, h1 = turn(h3, "z", -1), turn(h1, "z", -1)

    with jax.named_scope("weights_x"):
        down, a0 = lax.optimization_barrier((down, a0))
        t1, t3 = call(merge_kernel, [half, half], (place, a1, a3, b13, down, up))
        t1, t3 = shift(t1, "x", -1), shift(t3, "x", 1)

    with jax.named_scope("rows_back"):
        (h2,) = call(pass_kernel, [pair], (place, near, far, h3, last))
        h2 = turn(h2, "z", -2)

    with jax.named_scope("weights_y"):
        send = ((80, D), BF16)
        mine, top, s1, s2, s3 = call(
            split_kernel,
            [((64, D), F32), ((CL, D), BF16), send, send, send],
            (place, a0, b0, t1, t3),
            [((PART, D), F32)],
        )
        g2, g1, g3 = shift(s2, "y", 2), shift(s1, "y", 1), shift(s3, "y", 3)

    with jax.named_scope("rows_back"):
        h2, g2 = lax.optimization_barrier((h2, g2))
        both = h1.astype(F32) + h2.astype(F32)
        grad_embed = (own + both[:INST]) + swap(both[INST:])

    with jax.named_scope("weights_y"):
        grad_leaf, grad_cluster = call(
            finish_kernel, [((CL, 4, D), F32), ((CL, D), F32)], (place, mine, top, g1, g2, g3)
        )
    return grad_embed, grad_cluster, grad_leaf


def solution(mesh):
    fine = Mesh(mesh.devices.reshape(NY, NC, NZ, NX), ("y", "core", "z", "x"))
    dp, label = ("y", "core"), ("z", "x")
    every = dp + label
    in_specs = (
        P(every, None),
        P(label, None),
        P(label, None, None),
        P(dp, label, None, None),
        P(dp, label, None, None),
        P(dp, label, None),
        P(dp, label, None, None),
        P(dp, label, None, None, None),
    )
    out_specs = (P(every, None), P(label, None), P(label, dp, None))
    return jax.shard_map(shards, mesh=fine, in_specs=in_specs, out_specs=out_specs, check_vma=False)
```

```python
import functools

import jax
import jax.numpy as jnp
from jax import lax
from jax.experimental import pallas as pl
from jax.experimental.pallas import tpu as pltpu
from jax.sharding import Mesh, PartitionSpec as P

BF16 = jnp.bfloat16
F32 = jnp.float32
NY, NC, NZ, NX = 4, 2, 8, 4
SIZE = {"y": NY, "core": NC, "z": NZ, "x": NX}
INST, D, KIDS, CL = 64, 768, 32, 16
ROWS = INST * NZ
WIDE = (KIDS + 1) * CL
TOP = 256
PART = 272
CUT = 144
ORDER = (0, 1, 7, 2, 6, 3, 5, 4)
ROW_AT = (
    ((0, 0, 64),),
    ((1, 0, 64),),
    ((2, 0, 64),),
    ((3, 16, 64),),
    ((4, 48, 32), (4, 16, 32)),
    ((5, 0, 64),),
    ((6, 32, 32), (6, 0, 32)),
    ((7, 16, 32), (8, 16, 32)),
)
SLOT_AT = (
    (((0, 0, 32),), ((1, 64, 32),), ((2, 64, 32),), ((3, 112, 32),)),
    (((0, 112, 32),), ((1, 64, 32),), ((2, 64, 32),), ((3, 0, 16), (4, 0, 16))),
)
NT = (((1,), (1,)), ((), ()))
NN = (((1,), (0,)), ((), ()))
TN = (((0,), (0,)), ((), ()))
VMEM = pl.BlockSpec(memory_space=pltpu.VMEM)
SMEM = pl.BlockSpec(memory_space=pltpu.SMEM)


def dot(a, b, dims):
    return lax.dot_general(a, b, dims, preferred_element_type=F32)


def call(kernel, out, args, scratch=(), own=0, **static):
    specs = [SMEM] + [VMEM] * (len(args) - 1 - own)
    specs += [pl.BlockSpec(memory_space=pltpu.HBM)] * own
    return pl.pallas_call(
        functools.partial(kernel, **static),
        out_shape=tuple(jax.ShapeDtypeStruct(s, t) for s, t in out),
        in_specs=specs,
        out_specs=(VMEM,) * len(out),
        scratch_shapes=[s if t is None else pltpu.VMEM(s, t) for s, t in scratch],
        compiler_params=pltpu.CompilerParams(vmem_limit_bytes=18 * 1024 * 1024),
        cost_estimate=pl.CostEstimate(flops=2 * 10**9, bytes_accessed=1 << 20, transcendentals=0),
    )(*args)


def shift(x, axis, by):
    n = SIZE[axis]
    return lax.ppermute(x, axis, [(i, (i + by) % n) for i in range(n)])


def swap(x):
    return shift(x, "core", 1)


def turn(x, axis, by):
    n = SIZE[axis]
    pairs = [(i, (i + by) % n) for i in range(n)] + [(n + i, n + (i - by) % n) for i in range(n)]
    return lax.ppermute(x, ("core", axis), pairs)


def prepare_kernel(place, lw, cw, w, part, raw, top, kids, sems):
    copies = [
        pltpu.make_async_copy(lw, raw, sems.at[0]),
        pltpu.make_async_copy(cw, top, sems.at[1]),
    ]
    for c in copies:
        c.start()
    for c in copies:
        c.wait()
    for c in range(CL):
        for j in range(D // 128):
            kids[j, pl.ds(c, KIDS, stride=CL)] = raw[c, :, j * 128 : j * 128 + 128].astype(F32)
    for y in range(NY):
        for core in range(NC):
            to, at = core * PART + y * 64, (y * NC + core) * 64
            for j in range(D // 128):
                w[to : to + 64, j * 128 : j * 128 + 128] = kids[j, at : at + 64].astype(BF16)
    w[TOP : TOP + CL] = top[...]
    part[...] = w[pl.ds(pl.multiple_of(place[1] * TOP, 16), PART)]


def load_kernel(place, counts, inst, clus, prefix, e, want, *refs):
    (up1, dn1, up2, dn2, s0), (n, i, c, a, ev, wv, rows, side, sems) = refs[:5], refs[5:]
    pairs = ((counts, n), (inst, i), (clus, c), (prefix, a), (e, ev), (want, wv))
    copies = [pltpu.make_async_copy(x, v, sems.at[k]) for k, (x, v) in enumerate(pairs)]
    for copy in copies:
        copy.start()
    for copy in copies:
        copy.wait()
    cap = inst.shape[1]
    rows[...] = jnp.zeros(rows.shape, F32)
    lane = lax.broadcasted_iota(jnp.int32, (1, cap), 1)
    for o in range(NZ * NX):
        alpha = jnp.where(lane < n[o], a[o : o + 1].astype(F32), 0.0)
        rows[o * 8 : o * 8 + 1, :cap] = alpha
        rows[o * 8 + 1 : o * 8 + 2, :cap] = i[o : o + 1].astype(F32)
        rows[o * 8 + 2 : o * 8 + 3, :cap] = c[o : o + 1].astype(F32)
    for z in range(NZ):
        side[z] = rows[z * 32 : z * 32 + 32].astype(BF16)

    def put(ref, lo, d, first=0, count=32):
        to = lax.rem(place[2] + d + NZ, NZ)
        ref[lo : lo + count] = jnp.zeros((count, D), BF16)
        for x in range(NX):
            ref[lo : lo + count, x * 128 : x * 128 + cap] = wv[to * NX + x, first : first + count]
        ref[lo : lo + count, 512:640] = side[to, first : first + count]

    put(s0, 0, 0)
    for ref1, ref2, by, half in ((up1, up2, 1, 0), (dn1, dn2, -1, 1)):
        ref1[0:64] = ev[...]
        put(ref1, 64, by)
        put(ref2, 0, 4, 16 * half, 16)
        ref2[16:48] = ev[half * 32 : half * 32 + 32]
        ref2[48:80] = ev[32 - half * 32 : 64 - half * 32]
        put(ref2, 80, 3 * by)
        put(ref2, 112, 2 * by)


def kid_row(k):
    core, y = k // 4 % NC, k // 8
    return core * (TOP + CL) + (y * 4 + k % 4) * CL


def slot_kernel(place, *refs, spots):
    blocks, (ay, wide, wants, sides) = refs[:-4], refs[-4:]
    x = place[0]
    lane_row = lax.broadcasted_iota(jnp.int32, (256, 128), 0)
    cluster_row = lax.broadcasted_iota(jnp.int32, (CL, 128), 0)
    for q in range(4):
        to = 0
        for ref, lo, n in spots[q]:
            sides[q, to : to + n] = blocks[ref][lo : lo + n, 512:640].astype(F32)
            wants[q, to : to + n] = blocks[ref][lo : lo + n, :512].astype(F32)
            to += n

    def step(r, _):
        owner = lax.rem(x - r + NX, NX)
        left = []
        for q in range(4):
            want = wants[q, :, pl.ds(pl.multiple_of(owner * 128, 128), 128)]
            side = sides[q, pl.ds(pl.multiple_of(owner * 8, 8), 8)]
            alpha, inst, clus = side[0:1], side[1:2].astype(jnp.int32), side[2:3].astype(jnp.int32)
            left.append(jnp.where(lane_row == inst + q * INST, alpha, 0.0).astype(BF16))
            member = cluster_row == clus
            for k in range(KIDS + 1):
                at = TOP if k == KIDS else kid_row(k)
                row = alpha if k == KIDS else want[k : k + 1]
                wide[at : at + CL, q * 128 : q * 128 + 128] = jnp.where(member, row, 0.0).astype(BF16)
        ay[r] = dot(wide[...], jnp.concatenate(left, axis=1), NT)
        return 0

    lax.fori_loop(0, NX, step, 0)


def owner_terms(r, e, w, ay1, ay2, dzs, z):
    top = pl.ds(TOP, CL)
    halves = ((ay1, pl.ds(0, 256)), (ay2, pl.ds(256, 256)))
    for (ay, lanes), zh in zip(halves, z):
        zh[...] = dot(w[...], e[lanes], NT)
    for (ay, lanes), zh in zip(halves, z):
        s1 = jax.nn.sigmoid(zh[top])
        s1a = s1 * ay[r, top]
        total = jnp.zeros((CL, 256), F32)
        for k in range(KIDS + 1):
            if k * CL == TOP:
                continue
            at = pl.ds(k * CL, CL)
            s2 = jax.nn.sigmoid(zh[at])
            t = s2 * (s1a * s2 - ay[r, at])
            total = total + t
            dzs[at, lanes] = (s1 * (1.0 - s2) * t).astype(BF16)
        dzs[top, lanes] = (total * s1 * (1.0 - s1)).astype(BF16)


def weight_terms(core, e, dzs, a, b):
    mine = pl.ds(pl.multiple_of(core * TOP, 16), PART)
    other = pl.ds(pl.multiple_of((1 - core) * TOP, 16), PART)
    b[...] = dot(dzs[other], e[...], NN).astype(BF16)
    a[...] = dot(dzs[mine], e[...], NN).astype(a.dtype)


def across_kernel(place, *refs):
    blocks, (n1, n2, f1, f2, ay1, ay2, a, b, dzs, e, w), z = refs[:9], refs[9:20], refs[20:]
    for d in range(NZ):
        to = d * INST
        for ref, lo, n in ROW_AT[d]:
            e[to : to + n] = blocks[ref][lo : lo + n]
            to += n
    core = place[1]
    for at, p1, p2 in ((core, n1, n2), (1 - core, f1, f2)):
        w[pl.ds(pl.multiple_of(at * TOP, 16), CUT)] = p1[...]
        w[pl.ds(pl.multiple_of(at * TOP + CUT, 16), PART - CUT)] = p2[...]
    owner_terms(2, e, w, ay1, ay2, dzs, z)
    weight_terms(core, e, dzs, a, b)


def beside_kernel(place, e, n1, f1, n3, f3, ay1, ay2, a1, a3, b, dz1, dz3, w1, w3, *z):
    core = place[1]
    for r, near, far, a, lo, dzs, w in ((1, n1, f1, a1, 0, dz1, w1), (3, n3, f3, a3, PART, dz3, w3)):
        w[pl.ds(pl.multiple_of(core * TOP, 16), PART)] = near[...]
        w[pl.ds(pl.multiple_of((1 - core) * TOP, 16), PART)] = far[...]
        owner_terms(r, e, w, ay1, ay2, dzs, z)
        weight_terms(core, e, dzs, a, b.at[pl.ds(lo, PART)])


def own_kernel(place, e, w, ay1, ay2, dz1, dz2, dz3, w1, w2, w3, a, b, near, last, far, own, *refs):
    z, dz0, ge = refs[:2], refs[2], refs[3]
    owner_terms(0, e, w, ay1, ay2, dz0, z)
    weight_terms(place[1], e, dz0, a, b)
    rows_kernel(place, dz0, dz1, dz2, dz3, w, w1, w2, w3, near, last, far, own, ge)


def rows_kernel(place, *refs):
    dzs, ws, (near, last, far, own, ge) = refs[:NX], refs[NX : 2 * NX], refs[2 * NX :]
    kids = (pl.ds(0, TOP), pl.ds(TOP + CL, TOP))
    tops = [jnp.concatenate([v[TOP : TOP + CL] for v in vs], axis=0) for vs in (dzs, ws)]
    ge[...] = dot(*tops, TN) + sum(dot(dzs[r][k], ws[r][k], TN) for r in range(NX) for k in kids)

    def block(d):
        at = jnp.where(place[1] == 0, ORDER.index(d), ORDER.index(-d % NZ))
        return ge[pl.ds(pl.multiple_of(at * INST, INST), INST)]

    own[...] = block(0)
    last[...] = block(4).astype(BF16)
    for i, d in enumerate((1, 2, 3)):
        near[i * INST : i * INST + INST] = block(d).astype(BF16)
        far[i * INST : i * INST + INST] = block(NZ - d).astype(BF16)


def pack_kernel(place, near, far, h1, h3):
    for h, at in ((h1, 0), (h3, 2 * INST)):
        h[:INST] = near[at : at + INST]
        h[INST:] = far[at : at + INST]


def pass_kernel(place, near, far, got3, got4, out):
    at = pl.ds(INST, INST)
    out[:INST] = (near[at].astype(F32) + got3[:INST].astype(F32) + got4[...].astype(F32)).astype(BF16)
    out[INST:] = (far[at].astype(F32) + got3[INST:].astype(F32)).astype(BF16)


def cut_kernel(place, a, b, low, high):
    low[...] = (a[:CUT] + b[:CUT].astype(F32)).astype(BF16)
    high[...] = (a[CUT:] + b[CUT:].astype(F32)).astype(BF16)


def merge_kernel(place, a1, a3, b, low, high, t1, t3):
    b1, b3 = b.at[pl.ds(0, PART)], b.at[pl.ds(PART, PART)]
    t1[:CUT] = (a1[:CUT] + b1[:CUT].astype(F32) + low[...].astype(F32)).astype(BF16)
    t1[CUT:] = (a1[CUT:] + b1[CUT:].astype(F32)).astype(BF16)
    t3[:CUT] = (a3[:CUT] + b3[:CUT].astype(F32)).astype(BF16)
    t3[CUT:] = (a3[CUT:] + b3[CUT:].astype(F32) + high[...].astype(F32)).astype(BF16)


def split_kernel(place, a, b, t1, t3, own, top, p1, p2, p3, total):
    core, y = place[1], place[3]
    total[...] = (a[...].astype(F32) + b[...].astype(F32)) + (
        t1[...].astype(F32) + t3[...].astype(F32)
    )

    def piece(d):
        return total[pl.ds(pl.multiple_of(core * CL + lax.rem(y + d, NY) * 64, 16), 64)]

    own[...] = piece(0)
    cluster = total[pl.ds(pl.multiple_of((1 - core) * TOP, 16), CL)].astype(BF16)
    top[...] = cluster
    for d, p in ((1, p1), (2, p2), (3, p3)):
        p[:64] = piece(d).astype(BF16)
        p[64:] = cluster


def finish_kernel(place, own, top, g1, g2, g3, leaf, cluster):
    out = own[...] + g1[:64].astype(F32) + g2[:64].astype(F32) + g3[:64].astype(F32)
    for k in range(4):
        leaf[:, k, :] = out[k * CL : k * CL + CL]
    even = lax.rem(place[3], 2) == 0
    one, two, three = (g[64:].astype(F32) for g in (g1, g2, g3))
    near = jnp.where(even, three, one)
    far = jnp.where(even, one, three)
    cluster[...] = (top[...].astype(F32) + near) + (two + far)


def shards(e, cw, lw, inst, clus, counts, prefix, targets):
    iy, ic, iz, ix = (lax.axis_index(n) for n in ("y", "core", "z", "x"))
    place = jnp.stack([ix, ic, iz, iy]).astype(jnp.int32)

    with jax.named_scope("weights"):
        w, part = call(
            prepare_kernel,
            [((WIDE, D), BF16), ((PART, D), BF16)],
            (place, lw, cw),
            [
                ((CL, KIDS, D), BF16),
                ((CL, D), BF16),
                ((D // 128, KIDS * CL, 128), F32),
                (pltpu.SemaphoreType.DMA((2,)), None),
            ],
            own=2,
        )
        low, high = shift(part, "x", 1), shift(part, "x", -1)
        low2, high2 = shift(low[:CUT], "x", 1), shift(high[CUT:], "x", -1)

    with jax.named_scope("rows"):
        cap = prefix.shape[-1]
        owners = NZ * NX
        want = jnp.swapaxes(targets.reshape(owners, cap, KIDS), 1, 2)
        flat = tuple(v.reshape(owners, cap) for v in (inst, clus, prefix))
        up1, dn1, up2, dn2, s0 = call(
            load_kernel,
            [((n, D), BF16) for n in (96, 96, 144, 144, 32)],
            (place, counts.reshape(owners)) + flat + (e, want),
            [
                (pltpu.SMEM((owners,), jnp.int32), None),
                ((owners, cap), jnp.int32),
                ((owners, cap), jnp.int32),
                ((owners, cap), BF16),
                ((INST, D), BF16),
                ((owners, KIDS, cap), BF16),
                ((owners * 8, 128), F32),
                ((NZ, 32, 128), BF16),
                (pltpu.SemaphoreType.DMA((6,)), None),
            ],
            own=6,
        )
        up2, dn2 = shift(up2, "z", 2), shift(dn2, "z", -2)
        up1, dn1 = shift(up1, "z", 1), shift(dn1, "z", -1)
        low2, high2, up2, dn2 = lax.optimization_barrier((low2, high2, up2, dn2))
        up3, dn3 = shift(up2[16:112], "z", 1), shift(dn2[16:112], "z", -1)
        up4, dn4 = shift(up2[:48], "z", 2), shift(dn2[:48], "z", -2)

    def sum_slots(blocks, spots):
        return call(
            slot_kernel,
            [((NX, WIDE, 256), F32)],
            (place,) + blocks,
            [((WIDE, 512), BF16), ((4, 32, 512), F32), ((4, 32, 128), F32)],
            spots=spots,
        )[0]

    ay1 = sum_slots((s0, up1, dn1, up2), SLOT_AT[0])
    with jax.named_scope("weights"):
        low2, high2, up4, dn4, ay1 = lax.optimization_barrier((low2, high2, up4, dn4, ay1))
        low_o, high_o, low2_o, high2_o = (swap(p) for p in (low, high, low2, high2))
    ay2 = sum_slots((dn2, up3, dn3, up4, dn4), SLOT_AT[1])
    wide, dzs = ((WIDE, D), BF16), ((WIDE, ROWS), BF16)
    half, half32 = ((PART, D), BF16), ((PART, D), F32)
    z = [((WIDE, 256), F32)] * 2

    a2, b2, dz2, rows, w2 = call(
        across_kernel,
        [half32, half, dzs, ((ROWS, D), BF16), wide],
        (place, e, up1, dn1, up2, dn2, up3, dn3, up4, dn4, low2, high2, low2_o, high2_o, ay1, ay2),
        z,
    )
    with jax.named_scope("weights_x"):
        down, up = call(
            cut_kernel, [((CUT, D), BF16), ((PART - CUT, D), BF16)], (place, a2, swap(b2))
        )
    a1, a3, b13, dz1, dz3, w1, w3 = call(
        beside_kernel,
        [half32, half32, ((2 * PART, D), BF16), dzs, dzs, wide, wide],
        (place, rows, low, low_o, high, high_o, ay1, ay2),
        z,
    )
    b13 = swap(b13)
    rows, down, up = lax.optimization_barrier((rows, down, up))
    down, up = shift(down, "x", -1), shift(up, "x", 1)
    block = ((INST, D), BF16)
    three = ((3 * INST, D), BF16)
    a0, b0, near, last, far, own = call(
        own_kernel,
        [half, half, three, block, three, ((INST, D), F32)],
        (place, rows, w, ay1, ay2, dz1, dz2, dz3, w1, w2, w3),
        z + [dzs, ((ROWS, D), F32)],
    )
    b0 = swap(b0)

    with jax.named_scope("rows_back"):
        last = turn(last, "z", -2)
        far = swap(far)
        pair = ((2 * INST, D), BF16)
        h1, h3 = call(pack_kernel, [pair, pair], (place, near, far))
        h3, h1 = turn(h3, "z", -1), turn(h1, "z", -1)

    with jax.named_scope("weights_x"):
        down, a0 = lax.optimization_barrier((down, a0))
        t1, t3 = call(merge_kernel, [half, half], (place, a1, a3, b13, down, up))
        t1, t3 = shift(t1, "x", -1), shift(t3, "x", 1)

    with jax.named_scope("rows_back"):
        h3, last, h1 = lax.optimization_barrier((h3, last, h1))
        (h2,) = call(pass_kernel, [pair], (place, near, far, h3, last))
        h2 = turn(h2, "z", -2)

    with jax.named_scope("weights_y"):
        send = ((80, D), BF16)
        mine, top, s1, s2, s3 = call(
            split_kernel,
            [((64, D), F32), ((CL, D), BF16), send, send, send],
            (place, a0, b0, t1, t3),
            [((PART, D), F32)],
        )
        g2, g1, g3 = shift(s2, "y", 2), shift(s1, "y", 1), shift(s3, "y", 3)

    with jax.named_scope("rows_back"):
        h2, g2 = lax.optimization_barrier((h2, g2))
        both = h1.astype(F32) + h2.astype(F32)
        grad_embed = (own + both[:INST]) + swap(both[INST:])

    with jax.named_scope("weights_y"):
        grad_leaf, grad_cluster = call(
            finish_kernel, [((CL, 4, D), F32), ((CL, D), F32)], (place, mine, top, g1, g2, g3)
        )
    return grad_embed, grad_cluster, grad_leaf


def solution(mesh):
    fine = Mesh(mesh.devices.reshape(NY, NC, NZ, NX), ("y", "core", "z", "x"))
    dp, label = ("y", "core"), ("z", "x")
    every = dp + label
    in_specs = (
        P(every, None),
        P(label, None),
        P(label, None, None),
        P(dp, label, None, None),
        P(dp, label, None, None),
        P(dp, label, None),
        P(dp, label, None, None),
        P(dp, label, None, None, None),
    )
    out_specs = (P(every, None), P(label, None), P(label, dp, None))
    return jax.shard_map(shards, mesh=fine, in_specs=in_specs, out_specs=out_specs, check_vma=False)
```

```python
import functools

import jax
import jax.numpy as jnp
from jax import lax
from jax.experimental import pallas as pl
from jax.experimental.pallas import tpu as pltpu
from jax.sharding import Mesh, PartitionSpec as P

BF16 = jnp.bfloat16
F32 = jnp.float32
NY, NC, NZ, NX = 4, 2, 8, 4
SIZE = {"y": NY, "core": NC, "z": NZ, "x": NX}
INST, D, KIDS, CL = 64, 768, 32, 16
ROWS = INST * NZ
WIDE = (KIDS + 1) * CL
TOP = 256
PART = 272
CUT = 144
ORDER = (0, 2, 6, 4, 1, 7, 3, 5)
ROW_AT = (
    ((0, 0, 64),),
    ((1, 16, 64),),
    ((2, 48, 32), (2, 16, 32)),
    ((3, 16, 32), (4, 16, 32)),
    ((5, 0, 64),),
    ((6, 0, 64),),
    ((7, 0, 64),),
    ((8, 32, 32), (8, 0, 32)),
)
SLOT_AT = (
    (((0, 0, 32),), ((1, 112, 32),), ((2, 112, 32),), ((3, 0, 16), (4, 0, 16))),
    (((0, 64, 32),), ((1, 64, 32),), ((2, 64, 32),), ((3, 64, 32),)),
)
NT = (((1,), (1,)), ((), ()))
NN = (((1,), (0,)), ((), ()))
TN = (((0,), (0,)), ((), ()))
VMEM = pl.BlockSpec(memory_space=pltpu.VMEM)
SMEM = pl.BlockSpec(memory_space=pltpu.SMEM)


def dot(a, b, dims):
    return lax.dot_general(a, b, dims, preferred_element_type=F32)


def call(kernel, out, args, scratch=(), own=0, flops=2 * 10**9, **static):
    specs = [SMEM] + [VMEM] * (len(args) - 1 - own)
    specs += [pl.BlockSpec(memory_space=pltpu.HBM)] * own
    return pl.pallas_call(
        functools.partial(kernel, **static),
        out_shape=tuple(jax.ShapeDtypeStruct(s, t) for s, t in out),
        in_specs=specs,
        out_specs=(VMEM,) * len(out),
        scratch_shapes=[s if t is None else pltpu.VMEM(s, t) for s, t in scratch],
        compiler_params=pltpu.CompilerParams(vmem_limit_bytes=18 * 1024 * 1024),
        cost_estimate=pl.CostEstimate(flops=flops, bytes_accessed=1 << 20, transcendentals=0),
    )(*args)


def shift(x, axis, by):
    n = SIZE[axis]
    return lax.ppermute(x, axis, [(i, (i + by) % n) for i in range(n)])


def swap(x):
    return shift(x, "core", 1)


def turn(x, axis, by):
    n = SIZE[axis]
    pairs = [(i, (i + by) % n) for i in range(n)] + [(n + i, n + (i - by) % n) for i in range(n)]
    return lax.ppermute(x, ("core", axis), pairs)


def prepare_kernel(place, lw, cw, w, part, raw, top, kids, sems):
    copies = [
        pltpu.make_async_copy(lw, raw, sems.at[0]),
        pltpu.make_async_copy(cw, top, sems.at[1]),
    ]
    for c in copies:
        c.start()
    for c in copies:
        c.wait()
    for c in range(CL):
        for j in range(D // 128):
            kids[j, pl.ds(c, KIDS, stride=CL)] = raw[c, :, j * 128 : j * 128 + 128].astype(F32)
    for y in range(NY):
        for core in range(NC):
            to, at = core * PART + y * 64, (y * NC + core) * 64
            for j in range(D // 128):
                w[to : to + 64, j * 128 : j * 128 + 128] = kids[j, at : at + 64].astype(BF16)
    w[TOP : TOP + CL] = top[...]
    part[...] = w[pl.ds(pl.multiple_of(place[1] * TOP, 16), PART)]


def load_kernel(place, counts, inst, clus, prefix, e, want, *refs):
    (up1, dn1, up2, dn2, s0), (n, i, c, a, ev, wv, rows, side, sems) = refs[:5], refs[5:]
    pairs = ((counts, n), (inst, i), (clus, c), (prefix, a), (e, ev), (want, wv))
    copies = [pltpu.make_async_copy(x, v, sems.at[k]) for k, (x, v) in enumerate(pairs)]
    for copy in copies:
        copy.start()
    for copy in copies:
        copy.wait()
    cap = inst.shape[1]
    rows[...] = jnp.zeros(rows.shape, F32)
    lane = lax.broadcasted_iota(jnp.int32, (1, cap), 1)
    for o in range(NZ * NX):
        alpha = jnp.where(lane < n[o], a[o : o + 1].astype(F32), 0.0)
        rows[o * 8 : o * 8 + 1, :cap] = alpha
        rows[o * 8 + 1 : o * 8 + 2, :cap] = i[o : o + 1].astype(F32)
        rows[o * 8 + 2 : o * 8 + 3, :cap] = c[o : o + 1].astype(F32)
    for z in range(NZ):
        side[z] = rows[z * 32 : z * 32 + 32].astype(BF16)

    def put(ref, lo, d, first=0, count=32):
        to = lax.rem(place[2] + d + NZ, NZ)
        ref[lo : lo + count] = jnp.zeros((count, D), BF16)
        for x in range(NX):
            ref[lo : lo + count, x * 128 : x * 128 + cap] = wv[to * NX + x, first : first + count]
        ref[lo : lo + count, 512:640] = side[to, first : first + count]

    put(s0, 0, 0)
    for ref1, ref2, by, half in ((up1, up2, 1, 0), (dn1, dn2, -1, 1)):
        ref1[0:64] = ev[...]
        put(ref1, 64, by)
        put(ref2, 0, 4, 16 * half, 16)
        ref2[16:48] = ev[half * 32 : half * 32 + 32]
        ref2[48:80] = ev[32 - half * 32 : 64 - half * 32]
        put(ref2, 80, 3 * by)
        put(ref2, 112, 2 * by)


def kid_row(k):
    core, y = k // 4 % NC, k // 8
    return core * (TOP + CL) + (y * 4 + k % 4) * CL


def slot_kernel(place, *refs, spots):
    blocks, (ay, wide, wants, sides) = refs[:-4], refs[-4:]
    x = place[0]
    lane_row = lax.broadcasted_iota(jnp.int32, (256, 128), 0)
    cluster_row = lax.broadcasted_iota(jnp.int32, (CL, 128), 0)
    for q in range(4):
        to = 0
        for ref, lo, n in spots[q]:
            sides[q, to : to + n] = blocks[ref][lo : lo + n, 512:640].astype(F32)
            wants[q, to : to + n] = blocks[ref][lo : lo + n, :512].astype(F32)
            to += n

    def step(r, _):
        owner = lax.rem(x - r + NX, NX)
        left = []
        for q in range(4):
            want = wants[q, :, pl.ds(pl.multiple_of(owner * 128, 128), 128)]
            side = sides[q, pl.ds(pl.multiple_of(owner * 8, 8), 8)]
            alpha, inst, clus = side[0:1], side[1:2].astype(jnp.int32), side[2:3].astype(jnp.int32)
            left.append(jnp.where(lane_row == inst + q * INST, alpha, 0.0).astype(BF16))
            member = cluster_row == clus
            for k in range(KIDS + 1):
                at = TOP if k == KIDS else kid_row(k)
                row = alpha if k == KIDS else want[k : k + 1]
                wide[at : at + CL, q * 128 : q * 128 + 128] = jnp.where(member, row, 0.0).astype(BF16)
        ay[r] = dot(wide[...], jnp.concatenate(left, axis=1), NT)
        return 0

    lax.fori_loop(0, NX, step, 0)


def owner_terms(r, e, w, ay1, ay2, dzs, z):
    top = pl.ds(TOP, CL)
    halves = ((ay1, pl.ds(0, 256)), (ay2, pl.ds(256, 256)))
    for (ay, lanes), zh in zip(halves, z):
        zh[...] = dot(w[...], e[lanes], NT)
    for (ay, lanes), zh in zip(halves, z):
        s1 = jax.nn.sigmoid(zh[top])
        s1a = s1 * ay[r, top]
        total = jnp.zeros((CL, 256), F32)
        for k in range(KIDS + 1):
            if k * CL == TOP:
                continue
            at = pl.ds(k * CL, CL)
            s2 = jax.nn.sigmoid(zh[at])
            t = s2 * (s1a * s2 - ay[r, at])
            total = total + t
            dzs[at, lanes] = (s1 * (1.0 - s2) * t).astype(BF16)
        dzs[top, lanes] = (total * s1 * (1.0 - s1)).astype(BF16)


def weight_terms(core, e, dzs, a, b):
    mine = pl.ds(pl.multiple_of(core * TOP, 16), PART)
    other = pl.ds(pl.multiple_of((1 - core) * TOP, 16), PART)
    b[...] = dot(dzs[other], e[...], NN).astype(BF16)
    a[...] = dot(dzs[mine], e[...], NN).astype(a.dtype)


def across_kernel(place, *refs):
    blocks, (n1, n2, f1, f2, ay1, ay2, a, b, dzs, e, w), z = refs[:9], refs[9:20], refs[20:]
    for d in range(NZ):
        to = d * INST
        for ref, lo, n in ROW_AT[d]:
            e[to : to + n] = blocks[ref][lo : lo + n]
            to += n
    core = place[1]
    for at, p1, p2 in ((core, n1, n2), (1 - core, f1, f2)):
        w[pl.ds(pl.multiple_of(at * TOP, 16), CUT)] = p1[...]
        w[pl.ds(pl.multiple_of(at * TOP + CUT, 16), PART - CUT)] = p2[...]
    owner_terms(2, e, w, ay1, ay2, dzs, z)
    weight_terms(core, e, dzs, a, b)


def beside_kernel(place, e, near, far, ay1, ay2, a, b, dzs, w, *z, r):
    core = place[1]
    w[pl.ds(pl.multiple_of(core * TOP, 16), PART)] = near[...]
    w[pl.ds(pl.multiple_of((1 - core) * TOP, 16), PART)] = far[...]
    owner_terms(r, e, w, ay1, ay2, dzs, z)
    weight_terms(core, e, dzs, a, b)


def own_kernel(place, e, w, ay1, ay2, dz1, dz2, dz3, w1, w2, w3, a, b, near, last, far, own, *refs):
    z, dz0, ge = refs[:2], refs[2], refs[3]
    owner_terms(0, e, w, ay1, ay2, dz0, z)
    weight_terms(place[1], e, dz0, a, b)
    rows_kernel(place, dz0, dz1, dz2, dz3, w, w1, w2, w3, near, last, far, own, ge)


def rows_kernel(place, *refs):
    dzs, ws, (near, last, far, own, ge) = refs[:NX], refs[NX : 2 * NX], refs[2 * NX :]
    kids = (pl.ds(0, TOP), pl.ds(TOP + CL, TOP))
    tops = [jnp.concatenate([v[TOP : TOP + CL] for v in vs], axis=0) for vs in (dzs, ws)]
    ge[...] = dot(*tops, TN) + sum(dot(dzs[r][k], ws[r][k], TN) for r in range(NX) for k in kids)

    def block(d):
        at = jnp.where(place[1] == 0, ORDER.index(d), ORDER.index(-d % NZ))
        return ge[pl.ds(pl.multiple_of(at * INST, INST), INST)]

    own[...] = block(0)
    last[...] = block(4).astype(BF16)
    for i, d in enumerate((1, 2, 3)):
        near[i * INST : i * INST + INST] = block(d).astype(BF16)
        far[i * INST : i * INST + INST] = block(NZ - d).astype(BF16)


def pack_kernel(place, near, far, h1, h3):
    for h, at in ((h1, 0), (h3, 2 * INST)):
        h[:INST] = near[at : at + INST]
        h[INST:] = far[at : at + INST]


def pass_kernel(place, near, far, got3, got4, out):
    at = pl.ds(INST, INST)
    out[:INST] = (near[at].astype(F32) + got3[:INST].astype(F32) + got4[...].astype(F32)).astype(BF16)
    out[INST:] = (far[at].astype(F32) + got3[INST:].astype(F32)).astype(BF16)


def cut_kernel(place, a, b, low, high):
    low[...] = (a[:CUT] + b[:CUT].astype(F32)).astype(BF16)
    high[...] = (a[CUT:] + b[CUT:].astype(F32)).astype(BF16)


def merge_kernel(place, a1, b1, a3, b3, low, high, t1, t3):
    t1[:CUT] = (a1[:CUT] + b1[:CUT].astype(F32) + low[...].astype(F32)).astype(BF16)
    t1[CUT:] = (a1[CUT:] + b1[CUT:].astype(F32)).astype(BF16)
    t3[:CUT] = (a3[:CUT] + b3[:CUT].astype(F32)).astype(BF16)
    t3[CUT:] = (a3[CUT:] + b3[CUT:].astype(F32) + high[...].astype(F32)).astype(BF16)


def split_kernel(place, a, b, t1, t3, own, top, p1, p2, p3, total):
    core, y = place[1], place[3]
    total[...] = (a[...].astype(F32) + b[...].astype(F32)) + (
        t1[...].astype(F32) + t3[...].astype(F32)
    )

    def piece(d):
        return total[pl.ds(pl.multiple_of(core * CL + lax.rem(y + d, NY) * 64, 16), 64)]

    own[...] = piece(0)
    cluster = total[pl.ds(pl.multiple_of((1 - core) * TOP, 16), CL)].astype(BF16)
    top[...] = cluster
    for d, p in ((1, p1), (2, p2), (3, p3)):
        p[:64] = piece(d).astype(BF16)
        p[64:] = cluster


def finish_kernel(place, own, top, g1, g2, g3, leaf, cluster):
    out = own[...] + g1[:64].astype(F32) + g2[:64].astype(F32) + g3[:64].astype(F32)
    for k in range(4):
        leaf[:, k, :] = out[k * CL : k * CL + CL]
    even = lax.rem(place[3], 2) == 0
    one, two, three = (g[64:].astype(F32) for g in (g1, g2, g3))
    near = jnp.where(even, three, one)
    far = jnp.where(even, one, three)
    cluster[...] = (top[...].astype(F32) + near) + (two + far)


def shards(e, cw, lw, inst, clus, counts, prefix, targets):
    iy, ic, iz, ix = (lax.axis_index(n) for n in ("y", "core", "z", "x"))
    place = jnp.stack([ix, ic, iz, iy]).astype(jnp.int32)

    with jax.named_scope("weights"):
        w, part = call(
            prepare_kernel,
            [((WIDE, D), BF16), ((PART, D), BF16)],
            (place, lw, cw),
            [
                ((CL, KIDS, D), BF16),
                ((CL, D), BF16),
                ((D // 128, KIDS * CL, 128), F32),
                (pltpu.SemaphoreType.DMA((2,)), None),
            ],
            own=2,
        )
        low, high = shift(part, "x", 1), shift(part, "x", -1)
        low2, high2 = shift(low[:CUT], "x", 1), shift(high[CUT:], "x", -1)

    with jax.named_scope("rows"):
        cap = prefix.shape[-1]
        owners = NZ * NX
        want = jnp.swapaxes(targets.reshape(owners, cap, KIDS), 1, 2)
        flat = tuple(v.reshape(owners, cap) for v in (inst, clus, prefix))
        up1, dn1, up2, dn2, s0 = call(
            load_kernel,
            [((n, D), BF16) for n in (96, 96, 144, 144, 32)],
            (place, counts.reshape(owners)) + flat + (e, want),
            [
                (pltpu.SMEM((owners,), jnp.int32), None),
                ((owners, cap), jnp.int32),
                ((owners, cap), jnp.int32),
                ((owners, cap), BF16),
                ((INST, D), BF16),
                ((owners, KIDS, cap), BF16),
                ((owners * 8, 128), F32),
                ((NZ, 32, 128), BF16),
                (pltpu.SemaphoreType.DMA((6,)), None),
            ],
            own=6,
        )
        up2, dn2 = shift(up2, "z", 2), shift(dn2, "z", -2)
        low2, high2, up2, dn2 = lax.optimization_barrier((low2, high2, up2, dn2))
        up3, dn3 = shift(up2[16:112], "z", 1), shift(dn2[16:112], "z", -1)
        up4, dn4 = shift(up2[:48], "z", 2), shift(dn2[:48], "z", -2)
        up1, dn1, _, _ = lax.optimization_barrier((up1, dn1, up2, dn2))
        up1, dn1 = shift(up1, "z", 1), shift(dn1, "z", -1)

    def sum_slots(blocks, spots):
        return call(
            slot_kernel,
            [((NX, WIDE, 256), F32)],
            (place,) + blocks,
            [((WIDE, 512), BF16), ((4, 32, 512), F32), ((4, 32, 128), F32)],
            spots=spots,
        )[0]

    ay1 = sum_slots((s0, up2, dn2, up4, dn4), SLOT_AT[0])
    with jax.named_scope("weights"):
        low2, high2, ay1 = lax.optimization_barrier((low2, high2, ay1))
        low_o, high_o, low2_o, high2_o = (swap(p) for p in (low, high, low2, high2))
    ay2 = sum_slots((up1, dn1, up3, dn3), SLOT_AT[1])
    wide, dzs = ((WIDE, D), BF16), ((WIDE, ROWS), BF16)
    half, half32 = ((PART, D), BF16), ((PART, D), F32)
    z = [((WIDE, 256), F32)] * 2

    a2, b2, dz2, rows, w2 = call(
        across_kernel,
        [half32, half, dzs, ((ROWS, D), BF16), wide],
        (place, e, up2, dn2, up4, dn4, up1, dn1, up3, dn3, low2, high2, low2_o, high2_o, ay1, ay2),
        z,
    )
    with jax.named_scope("weights_x"):
        down, up = call(
            cut_kernel, [((CUT, D), BF16), ((PART - CUT, D), BF16)], (place, a2, swap(b2))
        )
    outs = [half32, half, dzs, wide]
    a1, b1, dz1, w1 = call(beside_kernel, outs, (place, rows, low, low_o, ay1, ay2), z, r=1)
    b1 = swap(b1)
    rows, down, up = lax.optimization_barrier((rows, down, up))
    down, up = shift(down, "x", -1), shift(up, "x", 1)
    a3, b3, dz3, w3 = call(beside_kernel, outs, (place, rows, high, high_o, ay1, ay2), z, r=3)
    b3 = swap(b3)
    block = ((INST, D), BF16)
    three = ((3 * INST, D), BF16)
    a0, b0, near, last, far, own = call(
        own_kernel,
        [half, half, three, block, three, ((INST, D), F32)],
        (place, rows, w, ay1, ay2, dz1, dz2, dz3, w1, w2, w3),
        z + [dzs, ((ROWS, D), F32)],
        flops=4 * 10**9,
    )
    b0 = swap(b0)

    with jax.named_scope("rows_back"):
        last = turn(last, "z", -2)
        far = swap(far)
        pair = ((2 * INST, D), BF16)
        h1, h3 = call(pack_kernel, [pair, pair], (place, near, far))
        h3, h1 = turn(h3, "z", -1), turn(h1, "z", -1)

    with jax.named_scope("weights_x"):
        down, a0 = lax.optimization_barrier((down, a0))
        t1, t3 = call(merge_kernel, [half, half], (place, a1, b1, a3, b3, down, up))
        t1, t3 = shift(t1, "x", -1), shift(t3, "x", 1)

    with jax.named_scope("rows_back"):
        h3, last, h1 = lax.optimization_barrier((h3, last, h1))
        (h2,) = call(pass_kernel, [pair], (place, near, far, h3, last))
        h2 = turn(h2, "z", -2)

    with jax.named_scope("weights_y"):
        send = ((80, D), BF16)
        mine, top, s1, s2, s3 = call(
            split_kernel,
            [((64, D), F32), ((CL, D), BF16), send, send, send],
            (place, a0, b0, t1, t3),
            [((PART, D), F32)],
        )
        g2, g1, g3 = shift(s2, "y", 2), shift(s1, "y", 1), shift(s3, "y", 3)

    with jax.named_scope("rows_back"):
        h2, g2 = lax.optimization_barrier((h2, g2))
        both = h1.astype(F32) + h2.astype(F32)
        grad_embed = (own + both[:INST]) + swap(both[INST:])

    with jax.named_scope("weights_y"):
        grad_leaf, grad_cluster = call(
            finish_kernel, [((CL, 4, D), F32), ((CL, D), F32)], (place, mine, top, g1, g2, g3)
        )
    return grad_embed, grad_cluster, grad_leaf


def solution(mesh):
    fine = Mesh(mesh.devices.reshape(NY, NC, NZ, NX), ("y", "core", "z", "x"))
    dp, label = ("y", "core"), ("z", "x")
    every = dp + label
    in_specs = (
        P(every, None),
        P(label, None),
        P(label, None, None),
        P(dp, label, None, None),
        P(dp, label, None, None),
        P(dp, label, None),
        P(dp, label, None, None),
        P(dp, label, None, None, None),
    )
    out_specs = (P(every, None), P(label, None), P(label, dp, None))
    return jax.shard_map(shards, mesh=fine, in_specs=in_specs, out_specs=out_specs, check_vma=False)
```

```python
import functools

import jax
import jax.numpy as jnp
from jax import lax
from jax.experimental import pallas as pl
from jax.experimental.pallas import tpu as pltpu
from jax.sharding import Mesh, PartitionSpec as P

BF16 = jnp.bfloat16
F32 = jnp.float32
NY, NC, NZ, NX = 4, 2, 8, 4
SIZE = {"y": NY, "core": NC, "z": NZ, "x": NX}
INST, D, KIDS, CL = 64, 768, 32, 16
ROWS = INST * NZ
WIDE = (KIDS + 1) * CL
TOP = 256
PART = 272
CUT = 144
ORDER = (0, 1, 7, 2, 6, 3, 5, 4)
ROW_AT = (
    ((0, 0, 64),),
    ((1, 0, 64),),
    ((2, 0, 64),),
    ((3, 16, 64),),
    ((4, 48, 32), (4, 16, 32)),
    ((5, 0, 64),),
    ((6, 32, 32), (6, 0, 32)),
    ((7, 16, 32), (8, 16, 32)),
)
SLOT_AT = (
    (((0, 0, 32),), ((1, 64, 32),), ((2, 64, 32),), ((3, 112, 32),)),
    (((0, 112, 32),), ((1, 64, 32),), ((2, 64, 32),), ((3, 0, 16), (4, 0, 16))),
)
NT = (((1,), (1,)), ((), ()))
NN = (((1,), (0,)), ((), ()))
TN = (((0,), (0,)), ((), ()))
VMEM = pl.BlockSpec(memory_space=pltpu.VMEM)
SMEM = pl.BlockSpec(memory_space=pltpu.SMEM)


def dot(a, b, dims):
    return lax.dot_general(a, b, dims, preferred_element_type=F32)


def call(kernel, out, args, scratch=(), own=0, **static):
    specs = [SMEM] + [VMEM] * (len(args) - 1 - own)
    specs += [pl.BlockSpec(memory_space=pltpu.HBM)] * own
    return pl.pallas_call(
        functools.partial(kernel, **static),
        out_shape=tuple(jax.ShapeDtypeStruct(s, t) for s, t in out),
        in_specs=specs,
        out_specs=(VMEM,) * len(out),
        scratch_shapes=[s if t is None else pltpu.VMEM(s, t) for s, t in scratch],
        compiler_params=pltpu.CompilerParams(vmem_limit_bytes=16 * 1024 * 1024),
        cost_estimate=pl.CostEstimate(flops=2 * 10**9, bytes_accessed=1 << 20, transcendentals=0),
    )(*args)


def shift(x, axis, by):
    n = SIZE[axis]
    return lax.ppermute(x, axis, [(i, (i + by) % n) for i in range(n)])


def swap(x):
    return shift(x, "core", 1)


def turn(x, axis, by):
    n = SIZE[axis]
    pairs = [(i, (i + by) % n) for i in range(n)] + [(n + i, n + (i - by) % n) for i in range(n)]
    return lax.ppermute(x, ("core", axis), pairs)


def prepare_kernel(place, lw, cw, w, part, kids):
    for c in range(CL):
        for j in range(D // 128):
            kids[j, pl.ds(c, KIDS, stride=CL)] = lw[c, :, j * 128 : j * 128 + 128].astype(F32)
    for y in range(NY):
        for core in range(NC):
            to, at = core * PART + y * 64, (y * NC + core) * 64
            for j in range(D // 128):
                w[to : to + 64, j * 128 : j * 128 + 128] = kids[j, at : at + 64].astype(BF16)
    w[TOP : TOP + CL] = cw[...]
    part[...] = w[pl.ds(pl.multiple_of(place[1] * TOP, 16), PART)]


def load_kernel(place, counts, inst, clus, prefix, e, want, *refs):
    (up1, dn1, up2, dn2, s0), (n, i, c, a, ev, wv, rows, side, sems) = refs[:5], refs[5:]
    pairs = ((counts, n), (inst, i), (clus, c), (prefix, a), (e, ev), (want, wv))
    copies = [pltpu.make_async_copy(x, v, sems.at[k]) for k, (x, v) in enumerate(pairs)]
    for copy in copies:
        copy.start()
    for copy in copies:
        copy.wait()
    cap = inst.shape[1]
    rows[...] = jnp.zeros(rows.shape, F32)
    lane = lax.broadcasted_iota(jnp.int32, (1, cap), 1)
    for o in range(NZ * NX):
        alpha = jnp.where(lane < n[o], a[o : o + 1].astype(F32), 0.0)
        rows[o * 8 : o * 8 + 1, :cap] = alpha
        rows[o * 8 + 1 : o * 8 + 2, :cap] = i[o : o + 1].astype(F32)
        rows[o * 8 + 2 : o * 8 + 3, :cap] = c[o : o + 1].astype(F32)
    for z in range(NZ):
        side[z] = rows[z * 32 : z * 32 + 32].astype(BF16)

    def put(ref, lo, d, first=0, count=32):
        to = lax.rem(place[2] + d + NZ, NZ)
        ref[lo : lo + count] = jnp.zeros((count, D), BF16)
        for x in range(NX):
            ref[lo : lo + count, x * 128 : x * 128 + cap] = wv[to * NX + x, first : first + count]
        ref[lo : lo + count, 512:640] = side[to, first : first + count]

    put(s0, 0, 0)
    for ref1, ref2, by, half in ((up1, up2, 1, 0), (dn1, dn2, -1, 1)):
        ref1[0:64] = ev[...]
        put(ref1, 64, by)
        put(ref2, 0, 4, 16 * half, 16)
        ref2[16:48] = ev[half * 32 : half * 32 + 32]
        ref2[48:80] = ev[32 - half * 32 : 64 - half * 32]
        put(ref2, 80, 3 * by)
        put(ref2, 112, 2 * by)


def kid_row(k):
    core, y = k // 4 % NC, k // 8
    return core * (TOP + CL) + (y * 4 + k % 4) * CL


def slot_kernel(place, *refs, spots):
    blocks, (ay, wide, wants, sides) = refs[:-4], refs[-4:]
    x = place[0]
    lane_row = lax.broadcasted_iota(jnp.int32, (256, 128), 0)
    cluster_row = lax.broadcasted_iota(jnp.int32, (CL, 128), 0)
    for q in range(4):
        to = 0
        for ref, lo, n in spots[q]:
            sides[q, to : to + n] = blocks[ref][lo : lo + n, 512:640].astype(F32)
            wants[q, to : to + n] = blocks[ref][lo : lo + n, :512].astype(F32)
            to += n

    def step(r, _):
        owner = lax.rem(x - r + NX, NX)
        left = []
        for q in range(4):
            want = wants[q, :, pl.ds(pl.multiple_of(owner * 128, 128), 128)]
            side = sides[q, pl.ds(pl.multiple_of(owner * 8, 8), 8)]
            alpha, inst, clus = side[0:1], side[1:2].astype(jnp.int32), side[2:3].astype(jnp.int32)
            left.append(jnp.where(lane_row == inst + q * INST, alpha, 0.0).astype(BF16))
            member = cluster_row == clus
            for k in range(KIDS + 1):
                at = TOP if k == KIDS else kid_row(k)
                row = alpha if k == KIDS else want[k : k + 1]
                wide[at : at + CL, q * 128 : q * 128 + 128] = jnp.where(member, row, 0.0).astype(BF16)
        ay[r] = dot(wide[...], jnp.concatenate(left, axis=1), NT)
        return 0

    lax.fori_loop(0, NX, step, 0)


def owner_kernel(place, *refs, r):
    core = place[1]
    mine = pl.ds(pl.multiple_of(core * TOP, 16), PART)
    other = pl.ds(pl.multiple_of((1 - core) * TOP, 16), PART)
    if r == 2:
        blocks, (n1, n2, f1, f2, ay1, ay2, a, b, dzs, e, w, z) = refs[:9], refs[9:]
        for d in range(NZ):
            to = d * INST
            for ref, lo, n in ROW_AT[d]:
                e[to : to + n] = blocks[ref][lo : lo + n]
                to += n
        for at, p1, p2 in ((core, n1, n2), (1 - core, f1, f2)):
            w[pl.ds(pl.multiple_of(at * TOP, 16), CUT)] = p1[...]
            w[pl.ds(pl.multiple_of(at * TOP + CUT, 16), PART - CUT)] = p2[...]
    elif r == 0:
        e, w, ay1, ay2, a, b, dzs, z = refs
    else:
        e, near, far, ay1, ay2, a, b, dzs, w, z = refs
        w[mine] = near[...]
        w[other] = far[...]
    z[...] = dot(w[...], e[...], NT)
    top = pl.ds(TOP, CL)
    for ay, lanes in ((ay1, pl.ds(0, 256)), (ay2, pl.ds(256, 256))):
        s1 = jax.nn.sigmoid(z[top, lanes])
        s1a = s1 * ay[r, top]
        total = jnp.zeros((CL, 256), F32)
        for k in range(KIDS + 1):
            if k * CL == TOP:
                continue
            at = pl.ds(k * CL, CL)
            s2 = jax.nn.sigmoid(z[at, lanes])
            t = s2 * (s1a * s2 - ay[r, at])
            total = total + t
            dzs[at, lanes] = (s1 * (1.0 - s2) * t).astype(BF16)
        dzs[top, lanes] = (total * s1 * (1.0 - s1)).astype(BF16)
    b[...] = dot(dzs[other], e[...], NN).astype(BF16)
    a[...] = dot(dzs[mine], e[...], NN).astype(a.dtype)


def rows_kernel(place, *refs):
    dzs, ws, (near, last, far, own, ge) = refs[:NX], refs[NX : 2 * NX], refs[2 * NX :]
    kids = (pl.ds(0, TOP), pl.ds(TOP + CL, TOP))
    tops = [jnp.concatenate([v[TOP : TOP + CL] for v in vs], axis=0) for vs in (dzs, ws)]
    ge[...] = dot(*tops, TN) + sum(dot(dzs[r][k], ws[r][k], TN) for r in range(NX) for k in kids)

    def block(d):
        at = jnp.where(place[1] == 0, ORDER.index(d), ORDER.index(-d % NZ))
        return ge[pl.ds(pl.multiple_of(at * INST, INST), INST)]

    own[...] = block(0)
    last[...] = block(4).astype(BF16)
    for i, d in enumerate((1, 2, 3)):
        near[i * INST : i * INST + INST] = block(d).astype(BF16)
        far[i * INST : i * INST + INST] = block(NZ - d).astype(BF16)


def pack_kernel(place, near, far, h1, h3):
    for h, at in ((h1, 0), (h3, 2 * INST)):
        h[:INST] = near[at : at + INST]
        h[INST:] = far[at : at + INST]


def pass_kernel(place, near, far, got3, got4, out):
    at = pl.ds(INST, INST)
    out[:INST] = (near[at].astype(F32) + got3[:INST].astype(F32) + got4[...].astype(F32)).astype(BF16)
    out[INST:] = (far[at].astype(F32) + got3[INST:].astype(F32)).astype(BF16)


def cut_kernel(place, a, b, low, high):
    low[...] = (a[:CUT] + b[:CUT].astype(F32)).astype(BF16)
    high[...] = (a[CUT:] + b[CUT:].astype(F32)).astype(BF16)


def merge_kernel(place, a1, b1, a3, b3, low, high, t1, t3):
    t1[:CUT] = (a1[:CUT] + b1[:CUT].astype(F32) + low[...].astype(F32)).astype(BF16)
    t1[CUT:] = (a1[CUT:] + b1[CUT:].astype(F32)).astype(BF16)
    t3[:CUT] = (a3[:CUT] + b3[:CUT].astype(F32)).astype(BF16)
    t3[CUT:] = (a3[CUT:] + b3[CUT:].astype(F32) + high[...].astype(F32)).astype(BF16)


def split_kernel(place, a, b, t1, t3, own, top, p1, p2, p3, total):
    core, y = place[1], place[3]
    total[...] = (a[...].astype(F32) + b[...].astype(F32)) + (
        t1[...].astype(F32) + t3[...].astype(F32)
    )

    def piece(d):
        return total[pl.ds(pl.multiple_of(core * CL + lax.rem(y + d, NY) * 64, 16), 64)]

    own[...] = piece(0)
    cluster = total[pl.ds(pl.multiple_of((1 - core) * TOP, 16), CL)].astype(BF16)
    top[...] = cluster
    for d, p in ((1, p1), (2, p2), (3, p3)):
        p[:64] = piece(d).astype(BF16)
        p[64:] = cluster


def finish_kernel(place, own, top, g1, g2, g3, leaf, cluster):
    out = own[...] + g1[:64].astype(F32) + g2[:64].astype(F32) + g3[:64].astype(F32)
    for k in range(4):
        leaf[:, k, :] = out[k * CL : k * CL + CL]
    even = lax.rem(place[3], 2) == 0
    one, two, three = (g[64:].astype(F32) for g in (g1, g2, g3))
    near = jnp.where(even, three, one)
    far = jnp.where(even, one, three)
    cluster[...] = (top[...].astype(F32) + near) + (two + far)


def shards(e, cw, lw, inst, clus, counts, prefix, targets):
    iy, ic, iz, ix = (lax.axis_index(n) for n in ("y", "core", "z", "x"))
    place = jnp.stack([ix, ic, iz, iy]).astype(jnp.int32)

    with jax.named_scope("weights"):
        w, part = call(
            prepare_kernel,
            [((WIDE, D), BF16), ((PART, D), BF16)],
            (place, lw, cw),
            [((D // 128, KIDS * CL, 128), F32)],
        )
        low, high = shift(part, "x", 1), shift(part, "x", -1)
        low2, high2 = shift(low[:CUT], "x", 1), shift(high[CUT:], "x", -1)

    with jax.named_scope("rows"):
        cap = prefix.shape[-1]
        owners = NZ * NX
        want = jnp.swapaxes(targets.reshape(owners, cap, KIDS), 1, 2)
        flat = tuple(v.reshape(owners, cap) for v in (inst, clus, prefix))
        up1, dn1, up2, dn2, s0 = call(
            load_kernel,
            [((n, D), BF16) for n in (96, 96, 144, 144, 32)],
            (place, counts.reshape(owners)) + flat + (e, want),
            [
                (pltpu.SMEM((owners,), jnp.int32), None),
                ((owners, cap), jnp.int32),
                ((owners, cap), jnp.int32),
                ((owners, cap), BF16),
                ((INST, D), BF16),
                ((owners, KIDS, cap), BF16),
                ((owners * 8, 128), F32),
                ((NZ, 32, 128), BF16),
                (pltpu.SemaphoreType.DMA((6,)), None),
            ],
            own=6,
        )
        up2, dn2 = shift(up2, "z", 2), shift(dn2, "z", -2)
        up1, dn1 = shift(up1, "z", 1), shift(dn1, "z", -1)
        low2, high2, up2, dn2 = lax.optimization_barrier((low2, high2, up2, dn2))
        up3, dn3 = shift(up2[16:112], "z", 1), shift(dn2[16:112], "z", -1)
        up4, dn4 = shift(up2[:48], "z", 2), shift(dn2[:48], "z", -2)

    def sum_slots(blocks, spots):
        return call(
            slot_kernel,
            [((NX, WIDE, 256), F32)],
            (place,) + blocks,
            [((WIDE, 512), BF16), ((4, 32, 512), F32), ((4, 32, 128), F32)],
            spots=spots,
        )[0]

    ay1 = sum_slots((s0, up1, dn1, up2), SLOT_AT[0])
    with jax.named_scope("weights"):
        low2, high2, up4, dn4, ay1 = lax.optimization_barrier((low2, high2, up4, dn4, ay1))
        low_o, high_o, low2_o, high2_o = (swap(p) for p in (low, high, low2, high2))
    ay2 = sum_slots((dn2, up3, dn3, up4, dn4), SLOT_AT[1])
    blocks, ay = (e, up1, dn1, up2, dn2, up3, dn3, up4, dn4), (ay1, ay2)

    wide, dzs = ((WIDE, D), BF16), ((WIDE, ROWS), BF16)
    half, half32 = ((PART, D), BF16), ((PART, D), F32)
    z = [((WIDE, ROWS), F32)]

    a2, b2, dz2, rows, w2 = call(
        owner_kernel,
        [half32, half, dzs, ((ROWS, D), BF16), wide],
        (place,) + blocks + (low2, high2, low2_o, high2_o) + ay,
        z,
        r=2,
    )
    with jax.named_scope("weights_x"):
        down, up = call(
            cut_kernel, [((CUT, D), BF16), ((PART - CUT, D), BF16)], (place, a2, swap(b2))
        )
    outs = [half32, half, dzs, wide]
    a1, b1, dz1, w1 = call(owner_kernel, outs, (place, rows, low, low_o) + ay, z, r=1)
    b1 = swap(b1)
    rows, down, up = lax.optimization_barrier((rows, down, up))
    down, up = shift(down, "x", -1), shift(up, "x", 1)
    a3, b3, dz3, w3 = call(owner_kernel, outs, (place, rows, high, high_o) + ay, z, r=3)
    b3 = swap(b3)
    a0, b0, dz0 = call(owner_kernel, [half, half, dzs], (place, rows, w) + ay, z, r=0)
    b0 = swap(b0)
    near, last, far, own = call(
        rows_kernel,
        [((3 * INST, D), BF16), ((INST, D), BF16), ((3 * INST, D), BF16), ((INST, D), F32)],
        (place, dz0, dz1, dz2, dz3, w, w1, w2, w3),
        [((ROWS, D), F32)],
    )

    with jax.named_scope("rows_back"):
        last = turn(last, "z", -2)
        far = swap(far)
        pair = ((2 * INST, D), BF16)
        h1, h3 = call(pack_kernel, [pair, pair], (place, near, far))
        h3, h1 = turn(h3, "z", -1), turn(h1, "z", -1)

    with jax.named_scope("weights_x"):
        down, a0 = lax.optimization_barrier((down, a0))
        t1, t3 = call(merge_kernel, [half, half], (place, a1, b1, a3, b3, down, up))
        t1, t3 = shift(t1, "x", -1), shift(t3, "x", 1)

    with jax.named_scope("rows_back"):
        (h2,) = call(pass_kernel, [pair], (place, near, far, h3, last))
        h2 = turn(h2, "z", -2)

    with jax.named_scope("weights_y"):
        send = ((80, D), BF16)
        mine, top, s1, s2, s3 = call(
            split_kernel,
            [((64, D), F32), ((CL, D), BF16), send, send, send],
            (place, a0, b0, t1, t3),
            [((PART, D), F32)],
        )
        g2, g1, g3 = shift(s2, "y", 2), shift(s1, "y", 1), shift(s3, "y", 3)

    with jax.named_scope("rows_back"):
        h2, g2 = lax.optimization_barrier((h2, g2))
        both = h1.astype(F32) + h2.astype(F32)
        grad_embed = (own + both[:INST]) + swap(both[INST:])

    with jax.named_scope("weights_y"):
        grad_leaf, grad_cluster = call(
            finish_kernel, [((CL, 4, D), F32), ((CL, D), F32)], (place, mine, top, g1, g2, g3)
        )
    return grad_embed, grad_cluster, grad_leaf


def solution(mesh):
    fine = Mesh(mesh.devices.reshape(NY, NC, NZ, NX), ("y", "core", "z", "x"))
    dp, label = ("y", "core"), ("z", "x")
    every = dp + label
    in_specs = (
        P(every, None),
        P(label, None),
        P(label, None, None),
        P(dp, label, None, None),
        P(dp, label, None, None),
        P(dp, label, None),
        P(dp, label, None, None),
        P(dp, label, None, None, None),
    )
    out_specs = (P(every, None), P(label, None), P(label, dp, None))
    return jax.shard_map(shards, mesh=fine, in_specs=in_specs, out_specs=out_specs, check_vma=False)
```

```python
import functools

import jax
import jax.numpy as jnp
from jax import lax
from jax.experimental import pallas as pl
from jax.experimental.pallas import tpu as pltpu
from jax.sharding import Mesh, PartitionSpec as P

BF16 = jnp.bfloat16
F32 = jnp.float32
NY, NC, NZ, NX = 4, 2, 8, 4
SIZE = {"y": NY, "core": NC, "z": NZ, "x": NX}
INST, D, KIDS, CL = 64, 768, 32, 16
ROWS = INST * NZ
WIDE = (KIDS + 1) * CL
TOP = 256
PART = 272
CUT = 144
ORDER = (0, 1, 7, 2, 6, 3, 5, 4)
ROW_AT = (
    ((0, 0, 64),),
    ((1, 0, 64),),
    ((2, 0, 64),),
    ((3, 16, 64),),
    ((4, 48, 32), (4, 16, 32)),
    ((5, 0, 64),),
    ((6, 32, 32), (6, 0, 32)),
    ((7, 16, 32), (8, 16, 32)),
)
SLOT_AT = (
    (((0, 0, 32),), ((1, 64, 32),), ((2, 64, 32),), ((3, 112, 32),)),
    (((0, 112, 32),), ((1, 64, 32),), ((2, 64, 32),), ((3, 0, 16), (4, 0, 16))),
)
NT = (((1,), (1,)), ((), ()))
NN = (((1,), (0,)), ((), ()))
TN = (((0,), (0,)), ((), ()))
VMEM = pl.BlockSpec(memory_space=pltpu.VMEM)
SMEM = pl.BlockSpec(memory_space=pltpu.SMEM)


def dot(a, b, dims):
    return lax.dot_general(a, b, dims, preferred_element_type=F32)


def call(kernel, out, args, scratch=(), own=0, **static):
    specs = [SMEM] + [VMEM] * (len(args) - 1 - own)
    specs += [pl.BlockSpec(memory_space=pltpu.HBM)] * own
    return pl.pallas_call(
        functools.partial(kernel, **static),
        out_shape=tuple(jax.ShapeDtypeStruct(s, t) for s, t in out),
        in_specs=specs,
        out_specs=(VMEM,) * len(out),
        scratch_shapes=[s if t is None else pltpu.VMEM(s, t) for s, t in scratch],
        compiler_params=pltpu.CompilerParams(vmem_limit_bytes=16 * 1024 * 1024),
        cost_estimate=pl.CostEstimate(flops=2 * 10**9, bytes_accessed=1 << 20, transcendentals=0),
    )(*args)


def shift(x, axis, by):
    n = SIZE[axis]
    return lax.ppermute(x, axis, [(i, (i + by) % n) for i in range(n)])


def swap(x):
    return shift(x, "core", 1)


def turn(x, axis, by):
    n = SIZE[axis]
    pairs = [(i, (i + by) % n) for i in range(n)] + [(n + i, n + (i - by) % n) for i in range(n)]
    return lax.ppermute(x, ("core", axis), pairs)


def prepare_kernel(place, lw, cw, w, part, kids):
    for c in range(CL):
        for j in range(D // 128):
            kids[j, pl.ds(c, KIDS, stride=CL)] = lw[c, :, j * 128 : j * 128 + 128].astype(F32)
    for y in range(NY):
        for core in range(NC):
            to, at = core * PART + y * 64, (y * NC + core) * 64
            for j in range(D // 128):
                w[to : to + 64, j * 128 : j * 128 + 128] = kids[j, at : at + 64].astype(BF16)
    w[TOP : TOP + CL] = cw[...]
    part[...] = w[pl.ds(pl.multiple_of(place[1] * TOP, 16), PART)]


def load_kernel(place, counts, inst, clus, prefix, e, want, *refs):
    (up1, dn1, up2, dn2, s0), (n, i, c, a, ev, wv, rows, side, sems) = refs[:5], refs[5:]
    pairs = ((counts, n), (inst, i), (clus, c), (prefix, a), (e, ev), (want, wv))
    copies = [pltpu.make_async_copy(x, v, sems.at[k]) for k, (x, v) in enumerate(pairs)]
    for copy in copies:
        copy.start()
    for copy in copies:
        copy.wait()
    cap = inst.shape[1]
    rows[...] = jnp.zeros(rows.shape, F32)
    lane = lax.broadcasted_iota(jnp.int32, (1, cap), 1)
    for o in range(NZ * NX):
        alpha = jnp.where(lane < n[o], a[o : o + 1].astype(F32), 0.0)
        rows[o * 8 : o * 8 + 1, :cap] = alpha
        rows[o * 8 + 1 : o * 8 + 2, :cap] = i[o : o + 1].astype(F32)
        rows[o * 8 + 2 : o * 8 + 3, :cap] = c[o : o + 1].astype(F32)
    for z in range(NZ):
        side[z] = rows[z * 32 : z * 32 + 32].astype(BF16)

    def put(ref, lo, d, first=0, count=32):
        to = lax.rem(place[2] + d + NZ, NZ)
        ref[lo : lo + count] = jnp.zeros((count, D), BF16)
        for x in range(NX):
            ref[lo : lo + count, x * 128 : x * 128 + cap] = wv[to * NX + x, first : first + count]
        ref[lo : lo + count, 512:640] = side[to, first : first + count]

    put(s0, 0, 0)
    for ref1, ref2, by, half in ((up1, up2, 1, 0), (dn1, dn2, -1, 1)):
        ref1[0:64] = ev[...]
        put(ref1, 64, by)
        put(ref2, 0, 4, 16 * half, 16)
        ref2[16:48] = ev[half * 32 : half * 32 + 32]
        ref2[48:80] = ev[32 - half * 32 : 64 - half * 32]
        put(ref2, 80, 3 * by)
        put(ref2, 112, 2 * by)


def kid_row(k):
    core, y = k // 4 % NC, k // 8
    return core * (TOP + CL) + (y * 4 + k % 4) * CL


def slot_kernel(place, *refs, spots):
    blocks, (ay, wide, wants, sides) = refs[:-4], refs[-4:]
    x = place[0]
    lane_row = lax.broadcasted_iota(jnp.int32, (256, 128), 0)
    cluster_row = lax.broadcasted_iota(jnp.int32, (CL, 128), 0)
    for q in range(4):
        to = 0
        for ref, lo, n in spots[q]:
            sides[q, to : to + n] = blocks[ref][lo : lo + n, 512:640].astype(F32)
            wants[q, to : to + n] = blocks[ref][lo : lo + n, :512].astype(F32)
            to += n

    def step(r, _):
        owner = lax.rem(x - r + NX, NX)
        left = []
        for q in range(4):
            want = wants[q, :, pl.ds(pl.multiple_of(owner * 128, 128), 128)]
            side = sides[q, pl.ds(pl.multiple_of(owner * 8, 8), 8)]
            alpha, inst, clus = side[0:1], side[1:2].astype(jnp.int32), side[2:3].astype(jnp.int32)
            left.append(jnp.where(lane_row == inst + q * INST, alpha, 0.0).astype(BF16))
            member = cluster_row == clus
            for k in range(KIDS + 1):
                at = TOP if k == KIDS else kid_row(k)
                row = alpha if k == KIDS else want[k : k + 1]
                wide[at : at + CL, q * 128 : q * 128 + 128] = jnp.where(member, row, 0.0).astype(BF16)
        ay[r] = dot(wide[...], jnp.concatenate(left, axis=1), NT)
        return 0

    lax.fori_loop(0, NX, step, 0)


def owner_kernel(place, *refs, r):
    core = place[1]
    mine = pl.ds(pl.multiple_of(core * TOP, 16), PART)
    other = pl.ds(pl.multiple_of((1 - core) * TOP, 16), PART)
    if r == 2:
        blocks, (n1, n2, f1, f2, ay1, ay2, a, b, dzs, e, w, z) = refs[:9], refs[9:]
        for d in range(NZ):
            to = d * INST
            for ref, lo, n in ROW_AT[d]:
                e[to : to + n] = blocks[ref][lo : lo + n]
                to += n
        for at, p1, p2 in ((core, n1, n2), (1 - core, f1, f2)):
            w[pl.ds(pl.multiple_of(at * TOP, 16), CUT)] = p1[...]
            w[pl.ds(pl.multiple_of(at * TOP + CUT, 16), PART - CUT)] = p2[...]
    elif r == 0:
        e, w, ay1, ay2, a, b, dzs, z = refs
    else:
        e, near, far, ay1, ay2, a, b, dzs, w, z = refs
        w[mine] = near[...]
        w[other] = far[...]
    z[...] = dot(w[...], e[...], NT)
    top = pl.ds(TOP, CL)
    for ay, lanes in ((ay1, pl.ds(0, 256)), (ay2, pl.ds(256, 256))):
        s1 = jax.nn.sigmoid(z[top, lanes])
        s1a = s1 * ay[r, top]
        total = jnp.zeros((CL, 256), F32)
        for k in range(KIDS + 1):
            if k * CL == TOP:
                continue
            at = pl.ds(k * CL, CL)
            s2 = jax.nn.sigmoid(z[at, lanes])
            t = s2 * (s1a * s2 - ay[r, at])
            total = total + t
            dzs[at, lanes] = (s1 * (1.0 - s2) * t).astype(BF16)
        dzs[top, lanes] = (total * s1 * (1.0 - s1)).astype(BF16)
    b[...] = dot(dzs[other], e[...], NN).astype(BF16)
    a[...] = dot(dzs[mine], e[...], NN).astype(a.dtype)


def rows_kernel(place, *refs):
    dzs, ws, (near, last, far, own, ge) = refs[:NX], refs[NX : 2 * NX], refs[2 * NX :]
    kids = (pl.ds(0, TOP), pl.ds(TOP + CL, TOP))
    tops = [jnp.concatenate([v[TOP : TOP + CL] for v in vs], axis=0) for vs in (dzs, ws)]
    ge[...] = dot(*tops, TN) + sum(dot(dzs[r][k], ws[r][k], TN) for r in range(NX) for k in kids)

    def block(d):
        at = jnp.where(place[1] == 0, ORDER.index(d), ORDER.index(-d % NZ))
        return ge[pl.ds(pl.multiple_of(at * INST, INST), INST)]

    own[...] = block(0)
    last[...] = block(4).astype(BF16)
    for i, d in enumerate((1, 2, 3)):
        near[i * INST : i * INST + INST] = block(d).astype(BF16)
        far[i * INST : i * INST + INST] = block(NZ - d).astype(BF16)


def pack_kernel(place, near, far, h1, h3):
    for h, at in ((h1, 0), (h3, 2 * INST)):
        h[:INST] = near[at : at + INST]
        h[INST:] = far[at : at + INST]


def pass_kernel(place, near, far, got3, got4, out):
    at = pl.ds(INST, INST)
    out[:INST] = (near[at].astype(F32) + got3[:INST].astype(F32) + got4[...].astype(F32)).astype(BF16)
    out[INST:] = (far[at].astype(F32) + got3[INST:].astype(F32)).astype(BF16)


def cut_kernel(place, a, b, low, high):
    low[...] = (a[:CUT] + b[:CUT].astype(F32)).astype(BF16)
    high[...] = (a[CUT:] + b[CUT:].astype(F32)).astype(BF16)


def merge_kernel(place, a1, b1, a3, b3, low, high, t1, t3):
    t1[:CUT] = (a1[:CUT] + b1[:CUT].astype(F32) + low[...].astype(F32)).astype(BF16)
    t1[CUT:] = (a1[CUT:] + b1[CUT:].astype(F32)).astype(BF16)
    t3[:CUT] = (a3[:CUT] + b3[:CUT].astype(F32)).astype(BF16)
    t3[CUT:] = (a3[CUT:] + b3[CUT:].astype(F32) + high[...].astype(F32)).astype(BF16)


def split_kernel(place, a, b, t1, t3, own, top, p1, p2, p3, total):
    core, y = place[1], place[3]
    total[...] = (a[...].astype(F32) + b[...].astype(F32)) + (
        t1[...].astype(F32) + t3[...].astype(F32)
    )

    def piece(d):
        return total[pl.ds(pl.multiple_of(core * CL + lax.rem(y + d, NY) * 64, 16), 64)]

    own[...] = piece(0)
    cluster = total[pl.ds(pl.multiple_of((1 - core) * TOP, 16), CL)].astype(BF16)
    top[...] = cluster
    for d, p in ((1, p1), (2, p2), (3, p3)):
        p[:64] = piece(d).astype(BF16)
        p[64:] = cluster


def finish_kernel(place, own, top, g1, g2, g3, leaf, cluster):
    out = own[...] + g1[:64].astype(F32) + g2[:64].astype(F32) + g3[:64].astype(F32)
    for k in range(4):
        leaf[:, k, :] = out[k * CL : k * CL + CL]
    even = lax.rem(place[3], 2) == 0
    one, two, three = (g[64:].astype(F32) for g in (g1, g2, g3))
    near = jnp.where(even, three, one)
    far = jnp.where(even, one, three)
    cluster[...] = (top[...].astype(F32) + near) + (two + far)


def shards(e, cw, lw, inst, clus, counts, prefix, targets):
    iy, ic, iz, ix = (lax.axis_index(n) for n in ("y", "core", "z", "x"))
    place = jnp.stack([ix, ic, iz, iy]).astype(jnp.int32)

    with jax.named_scope("weights"):
        w, part = call(
            prepare_kernel,
            [((WIDE, D), BF16), ((PART, D), BF16)],
            (place, lw, cw),
            [((D // 128, KIDS * CL, 128), F32)],
        )
        low, high = shift(part, "x", 1), shift(part, "x", -1)
        low2, high2 = shift(low[:CUT], "x", 1), shift(high[CUT:], "x", -1)

    with jax.named_scope("rows"):
        cap = prefix.shape[-1]
        owners = NZ * NX
        want = jnp.swapaxes(targets.reshape(owners, cap, KIDS), 1, 2)
        flat = tuple(v.reshape(owners, cap) for v in (inst, clus, prefix))
        up1, dn1, up2, dn2, s0 = call(
            load_kernel,
            [((n, D), BF16) for n in (96, 96, 144, 144, 32)],
            (place, counts.reshape(owners)) + flat + (e, want),
            [
                (pltpu.SMEM((owners,), jnp.int32), None),
                ((owners, cap), jnp.int32),
                ((owners, cap), jnp.int32),
                ((owners, cap), BF16),
                ((INST, D), BF16),
                ((owners, KIDS, cap), BF16),
                ((owners * 8, 128), F32),
                ((NZ, 32, 128), BF16),
                (pltpu.SemaphoreType.DMA((6,)), None),
            ],
            own=6,
        )
        up2, dn2 = shift(up2, "z", 2), shift(dn2, "z", -2)
        up1, dn1 = shift(up1, "z", 1), shift(dn1, "z", -1)
        low2, high2, up2, dn2 = lax.optimization_barrier((low2, high2, up2, dn2))
        up3, dn3 = shift(up2[16:112], "z", 1), shift(dn2[16:112], "z", -1)
        up4, dn4 = shift(up2[:48], "z", 2), shift(dn2[:48], "z", -2)

    def sum_slots(blocks, spots):
        return call(
            slot_kernel,
            [((NX, WIDE, 256), F32)],
            (place,) + blocks,
            [((WIDE, 512), BF16), ((4, 32, 512), F32), ((4, 32, 128), F32)],
            spots=spots,
        )[0]

    ay1 = sum_slots((s0, up1, dn1, up2), SLOT_AT[0])
    with jax.named_scope("weights"):
        low2, high2, up4, dn4, ay1 = lax.optimization_barrier((low2, high2, up4, dn4, ay1))
        low_o, high_o, low2_o, high2_o = (swap(p) for p in (low, high, low2, high2))
    ay2 = sum_slots((dn2, up3, dn3, up4, dn4), SLOT_AT[1])
    blocks, ay = (e, up1, dn1, up2, dn2, up3, dn3, up4, dn4), (ay1, ay2)

    wide, dzs = ((WIDE, D), BF16), ((WIDE, ROWS), BF16)
    half, half32 = ((PART, D), BF16), ((PART, D), F32)
    z = [((WIDE, ROWS), F32)]

    a2, b2, dz2, rows, w2 = call(
        owner_kernel,
        [half32, half, dzs, ((ROWS, D), BF16), wide],
        (place,) + blocks + (low2, high2, low2_o, high2_o) + ay,
        z,
        r=2,
    )
    with jax.named_scope("weights_x"):
        down, up = call(
            cut_kernel, [((CUT, D), BF16), ((PART - CUT, D), BF16)], (place, a2, swap(b2))
        )
    outs = [half32, half, dzs, wide]
    a1, b1, dz1, w1 = call(owner_kernel, outs, (place, rows, low, low_o) + ay, z, r=1)
    b1 = swap(b1)
    rows, down, up = lax.optimization_barrier((rows, down, up))
    down, up = shift(down, "x", -1), shift(up, "x", 1)
    a3, b3, dz3, w3 = call(owner_kernel, outs, (place, rows, high, high_o) + ay, z, r=3)
    b3 = swap(b3)
    a0, b0, dz0 = call(owner_kernel, [half, half, dzs], (place, rows, w) + ay, z, r=0)
    b0 = swap(b0)
    near, last, far, own = call(
        rows_kernel,
        [((3 * INST, D), BF16), ((INST, D), BF16), ((3 * INST, D), BF16), ((INST, D), F32)],
        (place, dz0, dz1, dz2, dz3, w, w1, w2, w3),
        [((ROWS, D), F32)],
    )

    with jax.named_scope("rows_back"):
        last = turn(last, "z", -2)
        far = swap(far)
        pair = ((2 * INST, D), BF16)
        h1, h3 = call(pack_kernel, [pair, pair], (place, near, far))
        h3, h1 = turn(h3, "z", -1), turn(h1, "z", -1)

    with jax.named_scope("weights_x"):
        down, a0 = lax.optimization_barrier((down, a0))
        t1, t3 = call(merge_kernel, [half, half], (place, a1, b1, a3, b3, down, up))
        t1, t3 = shift(t1, "x", -1), shift(t3, "x", 1)

    with jax.named_scope("rows_back"):
        h3, last, h1 = lax.optimization_barrier((h3, last, h1))
        (h2,) = call(pass_kernel, [pair], (place, near, far, h3, last))
        h2 = turn(h2, "z", -2)

    with jax.named_scope("weights_y"):
        send = ((80, D), BF16)
        mine, top, s1, s2, s3 = call(
            split_kernel,
            [((64, D), F32), ((CL, D), BF16), send, send, send],
            (place, a0, b0, t1, t3),
            [((PART, D), F32)],
        )
        g2, g1, g3 = shift(s2, "y", 2), shift(s1, "y", 1), shift(s3, "y", 3)

    with jax.named_scope("rows_back"):
        h2, g2 = lax.optimization_barrier((h2, g2))
        both = h1.astype(F32) + h2.astype(F32)
        grad_embed = (own + both[:INST]) + swap(both[INST:])

    with jax.named_scope("weights_y"):
        grad_leaf, grad_cluster = call(
            finish_kernel, [((CL, 4, D), F32), ((CL, D), F32)], (place, mine, top, g1, g2, g3)
        )
    return grad_embed, grad_cluster, grad_leaf


def solution(mesh):
    fine = Mesh(mesh.devices.reshape(NY, NC, NZ, NX), ("y", "core", "z", "x"))
    dp, label = ("y", "core"), ("z", "x")
    every = dp + label
    in_specs = (
        P(every, None),
        P(label, None),
        P(label, None, None),
        P(dp, label, None, None),
        P(dp, label, None, None),
        P(dp, label, None),
        P(dp, label, None, None),
        P(dp, label, None, None, None),
    )
    out_specs = (P(every, None), P(label, None), P(label, dp, None))
    return jax.shard_map(shards, mesh=fine, in_specs=in_specs, out_specs=out_specs, check_vma=False)
```
